128 devices in a mesh: section: 2 (over core), replica: 4 (over y), shard: 16 (over x, z).
Axes of the slice: x: 4, y: 4, z: 4, core: 2. Of those that a mesh axis runs over, the one named last changes fastest.
Arguments:
- inputs: bfloat16 [2, 49152, 512], P(None, ('replica', 'shard')), may hold values from -6 to 6
- cotangent: bfloat16 [2, 49152, 512], P(None, ('replica', 'shard')), may hold values from -6 to 6
- lengths: int32 [2, 64, 4], P(None, ('replica', 'shard')), may hold values from 0 to 768, as said below
- norm1_gain: bfloat16 [2, 512], P('section', 'shard'), may hold values from 0.5 to 1.5
- norm1_bias: bfloat16 [2, 512], P('section', 'shard'), may hold values from -1.5 to 1.5
- qkv_weight: bfloat16 [2, 512, 1536], P('section', 'shard'), may hold values from -0.375 to 0.375
- qkv_bias: bfloat16 [2, 1536], P('section', 'shard'), may hold values from -2.5 to 2.5
- dense_weight: bfloat16 [2, 512, 512], P('section', 'shard'), may hold values from -1 to 1
- norm2_gain: bfloat16 [2, 512], P('section', 'shard'), may hold values from 0.5 to 1.5
- norm2_bias: bfloat16 [2, 512], P('section', 'shard'), may hold values from -1.5 to 1.5
- fc_in_weight: bfloat16 [2, 512, 2048], P('section', 'shard'), may hold values from -0.25 to 0.25
- fc_in_bias: bfloat16 [2, 2048], P('section', 'shard'), may hold values from -2.5 to 2.5
- fc_out_weight: bfloat16 [2, 2048, 512], P('section', 'shard'), may hold values from -0.1875 to 0.1875
- out_bias: bfloat16 [2, 512], P('section', 'shard'), may hold values from -2.5 to 2.5
Outputs:
- activations: bfloat16 [2, 2, 49152, 512], P('section', None, ('replica', 'shard'))
- input_grads: bfloat16 [2, 2, 49152, 512], P('section', None, ('replica', 'shard'))
- grad_norm1_gain: float32 [2, 512], P('section', 'shard')
- grad_norm1_bias: float32 [2, 512], P('section', 'shard')
- grad_qkv_weight: float32 [2, 512, 1536], P('section', 'shard')
- grad_qkv_bias: float32 [2, 1536], P('section', 'shard')
- grad_dense_weight: float32 [2, 512, 512], P('section', 'shard')
- grad_norm2_gain: float32 [2, 512], P('section', 'shard')
- grad_norm2_bias: float32 [2, 512], P('section', 'shard')
- grad_fc_in_weight: float32 [2, 512, 2048], P('section', 'shard')
- grad_fc_in_bias: float32 [2, 2048], P('section', 'shard')
- grad_fc_out_weight: float32 [2, 2048, 512], P('section', 'shard')
- grad_out_bias: float32 [2, 512], P('section', 'shard')
The draws below stay inside these ranges and needn't reach their ends.
Inputs may be any that keep to these rules, and one draw needn't show every extreme that they name: `lengths`: in each slab the sequences, each padded up to a multiple of 128 rows, fill at most 768 rows; a length of 0 is an empty sequence. In every micro-batch some slab holds a single sequence of 768 rows.
All inputs are finite; a program needn't handle non-finite values.
Results may differ from the reference program's by a relative error of at most 0.025.
Values may be sent and summed in bfloat16 or wider, within the bound.
A program may use at most 256 MiB of HBM per device.

```python
import math
import jax
import jax.numpy as jnp
from jax import lax

D = 512
HEADS = 8
FF = 2048
ROT = 16
HEAD = 64
BLOCK = 128
SEQS = 4
MICRO = 2
TOK_DEV = 768
SHARDS = 64
TOKENS = 49152
N_SECTION = 2


def draw_lengths(key, part):
    key = jax.random.fold_in(key, 7)
    fill_key, cut_key, trim_key, choose_key = jax.random.split(key, 4)
    block_total = TOK_DEV // BLOCK
    filled_blocks = jax.random.randint(fill_key, (MICRO, SHARDS, 1), (block_total + 1) // 2, block_total + 1)
    cut_points = jax.random.randint(cut_key, (MICRO, SHARDS, SEQS - 1), 0, filled_blocks + 1)
    boundaries = jnp.concatenate([jnp.zeros((MICRO, SHARDS, 1), jnp.int32), jnp.sort(cut_points, axis=-1), filled_blocks], axis=-1)
    block_counts = boundaries[..., 1:] - boundaries[..., :-1]
    trimmed = jax.random.randint(trim_key, (MICRO, SHARDS, SEQS), 0, BLOCK // 2)
    drawn = jnp.where(block_counts > 0, block_counts * BLOCK - trimmed, 0)
    chosen = jax.random.randint(choose_key, (MICRO, 1, 1), 0, SHARDS)
    full_row = jnp.where(jnp.arange(SEQS, dtype=jnp.int32) == 0, TOK_DEV, 0)
    picked = jnp.arange(SHARDS, dtype=jnp.int32)[None, :, None] == chosen
    drawn = jnp.where(picked, full_row[None, None, :], drawn)
    return drawn.astype(jnp.int32)


def shard_levels(key, extent, cuts, low, high):
    level, own = 1.0, jax.random.fold_in(key, 6)
    for dim, shards_of in cuts:
        draws = jnp.exp(jax.random.uniform(jax.random.fold_in(own, dim), (shards_of,), jnp.float32, low / len(cuts), high / len(cuts)))
        level = level * jnp.repeat(draws, extent[dim] // shards_of).reshape([-1 if axis == dim else 1 for axis in range(len(extent))])
    return level


def gaussian(stream_key, extent, deviation, reach, pieces=(), kind=jnp.bfloat16):
    array = jax.random.normal(stream_key, extent, jnp.float32) * deviation
    if len(pieces) > 0:
        array = shard_levels(stream_key, extent, pieces, -0.22, 0.18) * array
    return jnp.clip(array, min=-reach, max=reach).astype(kind)


def setup_inputs(seed: int = 0) -> dict:
    key_list = jax.random.split(jax.random.key(seed), 15)
    return {
        "inputs": gaussian(key_list[0], (MICRO, TOKENS, D), 1.0, 6.0, ((1, 64),)),
        "cotangent": gaussian(key_list[1], (MICRO, TOKENS, D), 1.0, 6.0, ((1, 64),)),
        "lengths": draw_lengths(jax.random.fold_in(key_list[14], 71), 0),
        "norm1_gain": jnp.clip(1.0 + 0.1 * jax.random.normal(key_list[3], (N_SECTION, D), jnp.float32), 0.5, 1.5).astype(jnp.bfloat16),
        "norm1_bias": gaussian(key_list[4], (N_SECTION, D), 0.3, 1.5, ((0, 2), (1, 16))),
        "qkv_weight": gaussian(key_list[5], (N_SECTION, D, 3 * D), (D // 2) ** -0.5, 0.375, ((0, 2), (1, 16))),
        "qkv_bias": gaussian(key_list[6], (N_SECTION, 3 * D), 0.5, 2.5, ((0, 2), (1, 16))),
        "dense_weight": gaussian(key_list[7], (N_SECTION, D, D), (D // 16) ** -0.5, 1.0, ((0, 2), (1, 16))),
        "norm2_gain": jnp.clip(1.0 + 0.1 * jax.random.normal(key_list[8], (N_SECTION, D), jnp.float32), 0.5, 1.5).astype(jnp.bfloat16),
        "norm2_bias": gaussian(key_list[9], (N_SECTION, D), 0.3, 1.5, ((0, 2), (1, 16))),
        "fc_in_weight": gaussian(key_list[10], (N_SECTION, D, FF), D ** -0.5, 0.25, ((0, 2), (1, 16))),
        "fc_in_bias": gaussian(key_list[11], (N_SECTION, FF), 0.5, 2.5, ((0, 2), (1, 16))),
        "fc_out_weight": gaussian(key_list[12], (N_SECTION, FF, D), (FF // 2) ** -0.5, 0.1875, ((0, 2), (1, 16))),
        "out_bias": gaussian(key_list[13], (N_SECTION, D), 0.5, 2.5, ((0, 2), (1, 16))),
    }


@jax.custom_vjp
def low(v):
    return lax.optimization_barrier(v.astype(jnp.bfloat16)).astype(jnp.float32)

@jax.custom_vjp
def low_back(v):
    return v

def low_keep(v):
    return (low(v), None)

def low_pass(kept, grad):
    return (grad,)

def back_keep(v):
    return (v, None)

def back_low(kept, grad):
    return (low(grad),)
low.defvjp(low_keep, low_pass)
low_back.defvjp(back_keep, back_low)
epsilon = 1e-05
masked_value = -1000000000.0
highest = lax.Precision.HIGHEST

def layout(slab_lengths):
    places = jnp.arange(TOK_DEV, dtype=jnp.int32)
    padded = (slab_lengths + BLOCK - 1) // BLOCK * BLOCK
    starts = jnp.cumsum(padded, dtype=jnp.int32) - padded
    inside = (places[:, None] >= starts[None, :]) & (places[:, None] < (starts + slab_lengths)[None, :])
    labels = jnp.arange(1, SEQS + 1, dtype=jnp.int32)
    sequence_ids = lax.optimization_barrier(jnp.sum(jnp.where(inside, labels[None, :], 0), axis=1, dtype=jnp.int32)) - 1
    offsets = lax.optimization_barrier(jnp.sum(jnp.where(inside, places[:, None] - starts[None, :], 0), axis=1, dtype=jnp.int32))
    alive = sequence_ids >= 0
    allowed = (sequence_ids[:, None] == sequence_ids[None, :]) & (places[None, :] <= places[:, None]) & alive[:, None] | (places[:, None] == places[None, :])
    return (alive, offsets, allowed)

def rotary_tables(offsets):
    indices = jnp.arange(ROT // 2, dtype=jnp.float32)
    frequencies = jnp.exp(indices * (-2.0 * math.log(10000.0) / ROT))
    angles = offsets.astype(jnp.float32)[:, None] * frequencies[None, :]
    return (jnp.cos(angles), jnp.sin(angles))

def rotate(by_heads, cosine_table, sine_table):
    half_rot = ROT // 2
    lower_half = by_heads[..., :half_rot]
    upper_half = by_heads[..., half_rot:ROT]
    cosine_part = cosine_table[:, None, :]
    sine_part = sine_table[:, None, :]
    return jnp.concatenate([lower_half * cosine_part - upper_half * sine_part, upper_half * cosine_part + lower_half * sine_part, by_heads[..., ROT:]], axis=-1)

def norm_rows(rows_in, gain_row, shift_row):
    average = lax.optimization_barrier(jnp.mean(rows_in, axis=-1, keepdims=True))
    centred = rows_in - average
    spread = lax.optimization_barrier(jnp.mean(centred * centred, axis=-1, keepdims=True))
    return centred * lax.rsqrt(spread + epsilon) * gain_row + shift_row

def slab_layer(hidden, slab_lengths, weights):
    gain_one, shift_one, attend_matrix, attend_offset, dense_matrix, gain_two, shift_two, widen_matrix, widen_offset, narrow_matrix, output_offset = weights
    alive, offsets, allowed = layout(slab_lengths)
    cosine_table, sine_table = rotary_tables(offsets)
    row_count = hidden.shape[0]
    normed_one = low(norm_rows(hidden, gain_one, shift_one))
    projected = low_back(jnp.dot(normed_one, attend_matrix, precision=highest) + attend_offset)
    queries = low(rotate(projected[:, :D].reshape(row_count, HEADS, HEAD), cosine_table, sine_table))
    keys_all = low(rotate(projected[:, D:2 * D].reshape(row_count, HEADS, HEAD), cosine_table, sine_table))
    values_all = low(projected[:, 2 * D:].reshape(row_count, HEADS, HEAD))
    head_scale = 1.0 / math.sqrt(HEAD)
    scores = low_back(jnp.einsum('qhd,khd->hqk', queries, keys_all, precision=highest) * head_scale)
    scores = jnp.where(allowed[None, :, :], scores, masked_value)
    attention = low(jax.nn.softmax(scores, axis=-1))
    blended = jnp.einsum('hqk,khd->qhd', attention, values_all, precision=highest).reshape(row_count, D)
    blended = low_back(low(blended))
    attended = jnp.dot(blended, dense_matrix, precision=highest)
    normed_two = low(norm_rows(hidden, gain_two, shift_two))
    widened = low_back(jnp.dot(normed_two, widen_matrix, precision=highest) + widen_offset)
    activated = low(jax.nn.gelu(widened, approximate=False))
    narrowed = jnp.dot(activated, narrow_matrix, precision=highest)
    return jnp.where(alive[:, None], hidden + attended + narrowed + output_offset, 0.0)

def section_pass(stream, flat_lengths, weights):

    def one_slab(pair):
        return slab_layer(pair[0], pair[1], weights)
    return lax.map(jax.checkpoint(one_slab), (stream, flat_lengths))

def reference(inputs, cotangent, lengths, norm1_gain, norm1_bias, qkv_weight, qkv_bias, dense_weight, norm2_gain, norm2_bias, fc_in_weight, fc_in_bias, fc_out_weight, out_bias):
    params = tuple((member.astype(jnp.float32) for member in (norm1_gain, norm1_bias, qkv_weight, qkv_bias, dense_weight, norm2_gain, norm2_bias, fc_in_weight, fc_in_bias, fc_out_weight, out_bias)))
    stream = inputs.astype(jnp.float32).reshape(MICRO * SHARDS, TOK_DEV, D)
    flat_lengths = lengths.reshape(MICRO * SHARDS, SEQS)
    probe_rows = jnp.zeros_like(stream)

    def forward(stream_in, probe_in, layer_params):
        lower_weights = tuple((member[0] for member in layer_params))
        upper_weights = tuple((member[1] for member in layer_params))
        middle = low(section_pass(low_back(stream_in), flat_lengths, lower_weights))
        handed = low_back(middle + probe_in)
        final_rows = section_pass(handed, flat_lengths, upper_weights)
        return (final_rows, middle)
    outputs, pullback = jax.vjp(forward, stream, probe_rows, params)
    final_rows, middle = outputs
    upstream = cotangent.astype(jnp.float32).reshape(MICRO * SHARDS, TOK_DEV, D)
    grad_stream, grad_probe, grad_params = pullback((upstream, jnp.zeros_like(middle)))
    activations = jnp.stack([middle, final_rows]).reshape(2, MICRO, TOKENS, D).astype(jnp.bfloat16)
    input_grads = jnp.stack([grad_stream, grad_probe]).reshape(2, MICRO, TOKENS, D).astype(jnp.bfloat16)
    grad_gain_one, grad_shift_one, grad_attend_matrix, grad_attend_offset, grad_dense_matrix, grad_gain_two, grad_shift_two, grad_widen_matrix, grad_widen_offset, grad_narrow_matrix, grad_output_offset = grad_params
    return (activations, input_grads, grad_gain_one, grad_shift_one, grad_attend_matrix, grad_attend_offset, grad_dense_matrix, grad_gain_two, grad_shift_two, grad_widen_matrix, grad_widen_offset, grad_narrow_matrix, grad_output_offset)
```

```python
import math

import jax
import jax.numpy as jnp
from jax import lax
from jax.experimental import pallas as pl
from jax.experimental.pallas import tpu as pltpu
from jax.sharding import PartitionSpec as P

T = 768
D = 512
FF = 2048
HEADS = 8
HEAD = 64
ROT = 16
BLOCK = 128
SEQS = 4
TILE = 256
EPS = 1e-5
MASKED = -1e9
LOG2E = 1.0 / math.log(2.0)
LN2 = math.log(2.0)
MESH = pl.DeviceIdType.MESH
BF = jnp.bfloat16
F32 = jnp.float32

QKV, DENSE, FIN, FOUT, VEC = range(5)
HALF_ROWS = (16, 16, 16, 64, 8)
WIDTH = (1536, 512, 2048, 512, 128)
KIND = (BF, BF, BF, BF, F32)


def dg(a, b, ca, cb):
    return lax.dot_general(a, b, (((ca,), (cb,)), ((), ())), preferred_element_type=F32)


class Place:
    def __init__(self):
        self.s = lax.axis_index("section")
        self.y = lax.axis_index("replica")
        shard = lax.axis_index("shard")
        x, z = shard // 4, shard % 4
        self.shard = shard
        self.p = x + self.s * (z - x)
        self.q = z + self.s * (x - z)

    def at(self, p, q):
        return (1 - self.s) * (4 * p + q) + self.s * (4 * q + p)

    def sibling(self):
        return (1 - self.s, self.y, self.shard)

    def along_p(self, d):
        return (self.s, self.y, self.at((self.p + d) % 4, self.q))

    def along_q(self, d):
        return (self.s, self.y, self.at(self.p, (self.q + d) % 4))

    def along_y(self, d):
        return (self.s, (self.y + d) % 4, self.shard)


def remote(src, dst, send, recv, device):
    return pltpu.make_async_remote_copy(
        src_ref=src, dst_ref=dst, send_sem=send, recv_sem=recv, device_id=device, device_id_type=MESH
    )


class Gather:
    def __init__(self, me, layer, part, shard_ref, whole, send, recv, local):
        self.me, self.layer, self.part = me, layer, part
        self.shard_ref, self.w = shard_ref, whole
        self.send = lambda k: send.at[layer, part, k]
        self.recv = lambda k: recv.at[layer, part, k]
        self.local = local.at[part]
        self.rows = HALF_ROWS[part]

    def half(self, h):
        if self.part == VEC:
            return self.shard_ref.at[h]
        return self.shard_ref.at[0, pl.ds(pl.multiple_of(h * self.rows, self.rows), self.rows), :]

    def own_copy(self):
        me = self.me
        return pltpu.make_async_copy(self.half(me.s), self.w.at[me.s, me.p, me.q], self.local)

    def hand_over(self):
        me = self.me
        return remote(
            self.half(1 - me.s), self.w.at[1 - me.s, me.q, me.p], self.send(0), self.recv(0), me.sibling()
        )

    def first(self, d):
        me = self.me
        own = self.w.at[me.s, me.p, me.q]
        return remote(own, own, self.send(d), self.recv(d), me.along_q(d))

    def first_landing(self, d):
        me = self.me
        there = self.w.at[me.s, me.p, (me.q + 4 - d) % 4]
        return remote(there, there, self.send(d), self.recv(d), me.along_q(d))

    def second(self, d):
        me = self.me
        row = self.w.at[me.s, me.p]
        return remote(row, row, self.send(3 + d), self.recv(3 + d), me.along_p(d))

    def second_landing(self, d):
        me = self.me
        row = self.w.at[me.s, (me.p + 4 - d) % 4]
        return remote(row, row, self.send(3 + d), self.recv(3 + d), me.along_p(d))

    def across(self, d):
        me = self.me
        row = self.w.at[me.s, (me.p + 4 - d) % 4]
        return remote(row, row, self.send(7 + d), self.recv(7 + d), me.sibling())

    def across_landing(self, d):
        me = self.me
        row = self.w.at[1 - me.s, (me.q + 4 - d) % 4]
        return remote(row, row, self.send(7 + d), self.recv(7 + d), me.sibling())

    def step0(self):
        @pl.when(self.me.s == self.layer)
        def _():
            self.own_copy().start()
            self.hand_over().start()

    def step1(self):
        @pl.when(self.me.s == self.layer)
        def _():
            self.own_copy().wait()

        @pl.when(self.me.s != self.layer)
        def _():
            me = self.me
            own = self.w.at[me.s, me.p, me.q]
            remote(own, own, self.send(0), self.recv(0), me.sibling()).wait_recv()

        for d in (1, 3, 2):
            self.first(d).start()

    def step2(self):
        for d in (1, 3, 2):
            self.first_landing(d).wait_recv()
        for d in (1, 3, 2):
            self.second(d).start()
        self.across(0).start()

    def step3(self):
        for d in (1, 3, 2):
            self.second_landing(d).wait_recv()
            self.across(d).start()

    def step4(self):
        for d in range(4):
            self.across_landing(d).wait_recv()

    def finish(self):
        @pl.when(self.me.s == self.layer)
        def _():
            self.hand_over().wait_send()

        for d in (1, 2, 3):
            self.first(d).wait_send()
            self.second(d).wait_send()
        for d in range(4):
            self.across(d).wait_send()


class Reduce:
    def __init__(self, me, layer, part, terms, buffers, send, recv):
        self.me, self.layer, self.part = me, layer, part
        self.g = terms
        self.r, self.one, self.two, self.ys, self.f, self.out = buffers
        self.send = lambda k: send.at[layer, part, k]
        self.recv = lambda k: recv.at[layer, part, k]
        self.kind = KIND[part]

    def swap(self):
        me = self.me
        return remote(self.g.at[1 - me.s], self.r, self.send(0), self.recv(0), me.sibling())

    def first(self, d):
        me = self.me
        return remote(
            self.r.at[(me.p + d) % 4], self.one.at[d - 1], self.send(d), self.recv(d), me.along_p(d)
        )

    def second(self, d):
        me = self.me
        return remote(
            self.r.at[me.p, (me.q + d) % 4],
            self.two.at[d - 1],
            self.send(3 + d),
            self.recv(3 + d),
            me.along_q(d),
        )

    def third(self, d):
        me = self.me
        return remote(
            self.ys.at[me.y], self.ys.at[me.y], self.send(6 + d), self.recv(6 + d), me.along_y(d)
        )

    def third_landing(self, d):
        me = self.me
        there = self.ys.at[(me.y + 4 - d) % 4]
        return remote(there, there, self.send(6 + d), self.recv(6 + d), me.along_y(d))

    def back(self):
        me = self.me
        return remote(self.f, self.out.at[me.s], self.send(10), self.recv(10), me.sibling())

    def step0(self):
        self.swap().start()

    def step1(self):
        me = self.me
        self.swap().wait_recv()

        def one(k, c):
            a, b = k // 4, k % 4
            self.r[a, b] = (self.r[a, b].astype(F32) + self.g[me.s, a, b].astype(F32)).astype(self.kind)
            return c

        lax.fori_loop(0, 16, one, 0)
        for d in (1, 3, 2):
            self.first(d).start()
        self.swap().wait_send()

    def step2(self):
        me = self.me
        for d in (1, 2, 3):
            self.first(d).wait_recv()

        def one(b, c):
            total = self.r[me.p, b].astype(F32) + self.one[0, b].astype(F32)
            total = total + (self.one[1, b].astype(F32) + self.one[2, b].astype(F32))
            self.r[me.p, b] = total.astype(self.kind)
            return c

        lax.fori_loop(0, 4, one, 0)
        for d in (1, 3, 2):
            self.second(d).start()

    def step3(self):
        me = self.me
        for d in (1, 2, 3):
            self.second(d).wait_recv()
        total = self.r[me.p, me.q].astype(F32) + self.two[0].astype(F32)
        total = total + (self.two[1].astype(F32) + self.two[2].astype(F32))
        self.ys[me.y] = total.astype(self.kind)
        for d in (1, 3, 2):
            self.third(d).start()

    def step4(self):
        me = self.me
        for d in (1, 2, 3):
            self.third_landing(d).wait_recv()
        total = (self.ys[0].astype(F32) + self.ys[1].astype(F32)) + (
            self.ys[2].astype(F32) + self.ys[3].astype(F32)
        )

        @pl.when(me.s == self.layer)
        def _():
            self.out[me.s] = total

        @pl.when(me.s != self.layer)
        def _():
            self.f[...] = total
            self.back().start()

    def step5(self):
        me = self.me

        @pl.when(me.s == self.layer)
        def _():
            there = self.out.at[1 - me.s]
            remote(there, there, self.send(10), self.recv(10), me.sibling()).wait_recv()

    def finish(self):
        for d in (1, 2, 3):
            self.first(d).wait_send()
            self.second(d).wait_send()
            self.third(d).wait_send()

        @pl.when(self.me.s != self.layer)
        def _():
            self.back().wait_send()


def natural_rows(ref, columns):
    pieces = []
    for x in range(4):
        for z in range(4):
            pieces.append(ref[0, x, z, :, columns])
            pieces.append(ref[1, z, x, :, columns])
    return jnp.concatenate(pieces, axis=0)


def group_rows(ref, x):
    pieces = []
    for z in range(4):
        pieces.append(ref[0, x, z])
        pieces.append(ref[1, z, x])
    return jnp.concatenate(pieces, axis=0)


def put_natural(ref, columns, value):
    for x in range(4):
        for z in range(4):
            row = 32 * (4 * x + z)
            ref[0, x, z, :, columns] = value[row : row + 16]
            ref[1, z, x, :, columns] = value[row + 16 : row + 32]


def put_group(ref, x, value, rows):
    for z in range(4):
        row = 2 * rows * z
        ref[0, x, z] = value[row : row + rows]
        ref[1, z, x] = value[row + rows : row + 2 * rows]


def to_column(row):
    here = lax.broadcasted_iota(jnp.int32, (128, 128), 0) == lax.broadcasted_iota(
        jnp.int32, (128, 128), 1
    )
    return jnp.sum(jnp.where(here, row, 0.0), axis=1, keepdims=True)


def turn(rows, cosine, sine):
    pieces = []
    for e in (0, 64):
        low, high = rows[e : e + 8], rows[e + 8 : e + 16]
        pieces += [low * cosine - high * sine, high * cosine + low * sine, rows[e + 16 : e + 64]]
    return jnp.concatenate(pieces, axis=0)


def columns(start, size):
    return pl.ds(pl.multiple_of(start, size), size)


def loop(count, step):
    def one(k, c):
        step(k)
        return c

    lax.fori_loop(0, count, one, 0)


def kernel(
    lengths,
    x_ref,
    cot_ref,
    wq_ref,
    wd_ref,
    wi_ref,
    wo_ref,
    vec_ref,
    act_out,
    ig_out,
    gq_out,
    gd_out,
    gi_out,
    go_out,
    gv_out,
    st_qkv,
    st_p0,
    st_p1,
    st_p2,
    st_bt,
    st_rinv,
    st_act,
    st_slo,
    *scratch,
):
    scratch = list(scratch)

    def take(count):
        taken, scratch[:count] = scratch[:count], []
        return taken

    w = [take(5), take(5)]
    g = take(5)
    r = [take(5), take(5)]
    one = [take(5), take(5)]
    two = [take(5), take(5)]
    ys = [take(5), take(5)]
    f = take(5)
    hid, grad, n1t, n2, acc, carried = take(6)
    qkvt, p0, p1, p2, bt, rinv, act, slo = take(8)
    d0, d1, d2, dn1 = take(4)
    vd, vq, vf, dvec, fvec, live, bias, cos_ref, sin_ref = take(9)
    ag_send, ag_recv, rs_send, rs_recv, ag_local, sems, ex_send, ex_recv = take(8)
    probs = (p0, p1, p2)
    dscores = (d0, d1, d2)
    outs = (gq_out, gd_out, gi_out, go_out, gv_out)
    shards = (wq_ref, wd_ref, wi_ref, wo_ref, vec_ref)

    me = Place()
    s = me.s
    barrier = pltpu.get_barrier_semaphore()
    partners = [me.sibling()]
    for d in (1, 2, 3):
        partners += [me.along_q(d), me.along_p(d), me.along_y(d)]
    for device in partners:
        pl.semaphore_signal(barrier, inc=1, device_id=device, device_id_type=MESH)
    pl.semaphore_wait(barrier, len(partners))

    gather = [
        [Gather(me, l, c, shards[c], w[l][c], ag_send, ag_recv, ag_local) for c in range(5)]
        for l in (0, 1)
    ]
    reduce = [
        [
            Reduce(
                me, l, c, g[c], (r[l][c], one[l][c], two[l][c], ys[l][c], f[c], outs[c]), rs_send, rs_recv
            )
            for c in range(5)
        ]
        for l in (0, 1)
    ]
    order = (VEC, QKV, DENSE, FIN, FOUT)

    x_in = pltpu.make_async_copy(x_ref.at[s], hid.at[0], sems.at[0])
    cot_in = pltpu.make_async_copy(cot_ref.at[s], grad.at[2], sems.at[1])
    x_in.start()
    for l in (0, 1):
        for c in order:
            gather[l][c].step0()
    for c in order:
        gather[0][c].step1()
    cot_in.start()

    starts, ends, at = [], [], jnp.int32(0)
    for k in range(SEQS):
        size = lengths[s, 0, k]
        starts.append(at)
        ends.append(at + size)
        at = at + (size + BLOCK - 1) // BLOCK * BLOCK

    def inside(places):
        return [(places >= a) & (places < b) for a, b in zip(starts, ends)]

    def live_tile(k):
        places = lax.broadcasted_iota(jnp.int32, (TILE, 1), 0) + k * TILE
        total = jnp.zeros((TILE, 1), F32)
        for found in inside(places):
            total = total + jnp.where(found, 1.0, 0.0)
        live[columns(k * TILE, TILE), :] = total

    loop(3, live_tile)
    places = lax.broadcasted_iota(jnp.int32, (8, T), 1)
    begin = jnp.zeros((8, T), jnp.int32)
    offset = jnp.zeros((8, T), jnp.int32)
    for found, a in zip(inside(places), starts):
        begin = begin + jnp.where(found, a, 0)
        offset = offset + jnp.where(found, places - a, 0)
    rates = jnp.exp(
        lax.broadcasted_iota(jnp.int32, (8, T), 0).astype(F32) * (-2.0 * math.log(10000.0) / ROT)
    )
    angles = offset.astype(F32) * rates
    cos_ref[...] = jnp.cos(angles)
    sin_ref[...] = jnp.sin(angles)
    for j in range(3):
        for i in range(j + 1):
            keys = lax.broadcasted_iota(jnp.int32, (TILE, TILE), 0) + i * TILE
            queries = lax.broadcasted_iota(jnp.int32, (TILE, TILE), 1) + j * TILE
            fits = (keys >= begin[0:1, j * TILE : (j + 1) * TILE]) & (keys <= queries)
            bias[j * (j + 1) // 2 + i] = jnp.where(fits, 0.0, MASKED)

    def unpack(l):
        ref = w[l][VEC]
        for x in range(4):
            vd[:, 128 * x : 128 * x + 128] = (ref[0, x, 0] + ref[0, x, 1]) + (ref[0, x, 2] + ref[0, x, 3])
            group = (ref[1, 0, x] + ref[1, 1, x]) + (ref[1, 2, x] + ref[1, 3, x])
            for k in range(3):
                vq[3 * x + k : 3 * x + k + 1, :] = group[k : k + 1]
            for z in range(4):
                vf[x : x + 1, 128 * z : 128 * z + 128] = ref[1, z, x][3:4]

    def normed(l, rows):
        v = hid[l, rows, :].astype(F32)
        centred = v - jnp.mean(v, axis=1, keepdims=True)
        scale = lax.rsqrt(jnp.mean(centred * centred, axis=1, keepdims=True) + EPS)
        return centred * scale, scale

    def norms(l):
        def tile(k):
            rows = columns(k * TILE, TILE)
            u, _ = normed(l, rows)
            n1t[:, rows] = (u * vd[0:1, :] + vd[1:2, :]).astype(BF).T
            n2[rows, :] = (u * vd[2:3, :] + vd[3:4, :]).astype(BF)

        loop(3, tile)

    def attend(l, hp):
        pair = []
        for which in range(3):
            rows = columns(which * D + hp * 128, 128)
            weight = natural_rows(w[l][QKV], rows)
            value = dg(weight, n1t[...], 0, 0) + to_column(vq[pl.ds(which * 4 + hp, 1), :])
            if which < 2:
                value = turn(value, cos_ref[...], sin_ref[...])
            if which == 0:
                value = value * (LOG2E / 8.0)
            pair.append(value.astype(BF))
            qkvt[rows, :] = pair[which]
        keys = pair[1].T
        blank = jnp.zeros((HEAD, TILE), BF)
        for e in (0, 1):
            h = 2 * hp + e
            query = pair[0][e * HEAD : (e + 1) * HEAD]
            value = pair[2][e * HEAD : (e + 1) * HEAD]
            for j in range(3):
                at_j = slice(j * TILE, (j + 1) * TILE)
                mine = query[:, at_j]
                mine = jnp.concatenate([mine, blank] if e == 0 else [blank, mine], axis=0)
                scores = [
                    dg(keys[i * TILE : (i + 1) * TILE], mine, 1, 0) + bias[j * (j + 1) // 2 + i]
                    for i in range(j + 1)
                ]
                peak = jnp.max(scores[0], axis=0, keepdims=True)
                for i in range(1, j + 1):
                    peak = jnp.maximum(peak, jnp.max(scores[i], axis=0, keepdims=True))
                total = jnp.zeros((1, TILE), F32)
                blended = jnp.zeros((HEAD, TILE), F32)
                for i in range(j + 1):
                    raised = jnp.exp2(scores[i] - peak)
                    total = total + jnp.sum(raised, axis=0, keepdims=True)
                    raised = raised.astype(BF)
                    probs[i][h, :, (j - i) * TILE : (j - i + 1) * TILE] = raised
                    blended = blended + dg(value[:, i * TILE : (i + 1) * TILE], raised, 1, 0)
                inverse = 1.0 / total
                rinv[pl.ds(h, 1), at_j] = inverse
                bt[columns(hp * 128 + e * HEAD, HEAD), at_j] = (blended * inverse).astype(BF)

    def widen(l, c):
        cols = columns(c * 512, 512)
        weight = natural_rows(w[l][FIN], cols)
        shift = vf[pl.ds(c, 1), :]

        def tile(k):
            rows = columns(k * TILE, TILE)
            v = dg(n2[rows, :], weight, 1, 0) + shift
            below = 0.5 + 0.5 * lax.erf(v * (1.0 / math.sqrt(2.0)))
            act[rows, cols] = (v * below).astype(BF)
            slope = below + v * (jnp.exp(-0.5 * v * v) * (1.0 / math.sqrt(2.0 * math.pi)))
            slo[rows, cols] = slope.astype(BF)

        for k in range(3):
            tile(k)

    def join(l):
        def part(t):
            cols = columns(t * TILE, TILE)
            weight = jnp.concatenate(
                [
                    piece
                    for x in range(4)
                    for z in range(4)
                    for piece in (w[l][FOUT][0, x, z, :, cols], w[l][FOUT][1, z, x, :, cols])
                ],
                axis=0,
            )
            total = dg(act[...], weight, 1, 0)
            total = total + dg(bt[...], natural_rows(w[l][DENSE], cols), 0, 0)
            total = total + hid[l, :, cols].astype(F32) + vd[4:5, cols]
            hid[l + 1, :, cols] = (total * live[...]).astype(BF)

        loop(2, part)

    def local(src, dst, k):
        return pltpu.make_async_copy(src, dst, sems.at[k])

    attention_kept = [
        (qkvt, st_qkv, 2),
        (p0, st_p0, 3),
        (p1, st_p1, 4),
        (p2, st_p2, 5),
        (bt, st_bt, 6),
        (rinv, st_rinv, 7),
    ]
    wide_kept = [(act, st_act, 8), (slo, st_slo, 9)]

    for c in order:
        gather[0][c].step2()
    for c in order:
        gather[1][c].step1()
    x_in.wait()
    gather[0][VEC].step3()
    gather[0][VEC].step4()
    unpack(0)
    norms(0)
    gather[0][QKV].step3()
    gather[0][QKV].step4()
    loop(2, lambda hp: attend(0, hp))
    for c in (DENSE, FIN, FOUT):
        gather[0][c].step3()
    for c in order:
        gather[1][c].step2()
    loop(2, lambda hp: attend(0, hp + 2))
    for a, b, k in attention_kept:
        local(a, b, k).start()
    for c in (DENSE, FIN, FOUT):
        gather[0][c].step4()
    loop(4, lambda c: widen(0, c))
    for c in order:
        gather[1][c].step3()
    join(0)
    for a, b, k in wide_kept:
        local(a, b, k).start()
    for c in (VEC, QKV, DENSE):
        gather[1][c].step4()

    unpack(1)
    norms(1)
    for a, b, k in attention_kept:
        local(a, b, k).wait()
    loop(4, lambda hp: attend(1, hp))
    for c in (FIN, FOUT):
        gather[1][c].step4()
    for a, b, k in wide_kept:
        local(a, b, k).wait()
    loop(4, lambda c: widen(1, c))
    join(1)
    for l in (0, 1):
        for c in order:
            gather[l][c].finish()
    act_mine = local(hid.at[1 + s], act_out.at[s], 10)
    act_theirs = remote(hid.at[2 - s], act_out.at[s], ex_send.at[0], ex_recv.at[0], me.sibling())
    act_mine.start()
    act_theirs.start()
    cot_in.wait()

    def start_back(l):
        def tile(k):
            rows = columns(k * TILE, TILE)
            v = grad[l + 1, rows, :].astype(F32) * live[rows, :]
            carried[rows, :] = v.astype(BF)
            here = jnp.sum(v, axis=0, keepdims=True)
            dvec[4:5, :] = here + jnp.where(k == 0, 0.0, dvec[4:5, :])

        dvec[...] = jnp.zeros((8, D), F32)
        loop(3, tile)

    def back_out(l, c):
        cols = columns(c * 512, 512)
        put_group(g[FOUT], c, dg(act[:, cols], carried[...], 0, 0).astype(BF), 64)
        weight = group_rows(w[l][FOUT], c)
        total = jnp.zeros((1, 512), F32)
        for k in range(3):
            rows = slice(k * TILE, (k + 1) * TILE)
            v = dg(carried[rows, :], weight, 1, 1) * slo[rows, cols].astype(F32)
            v = v.astype(BF)
            slo[rows, cols] = v
            total = total + jnp.sum(v.astype(F32), axis=0, keepdims=True)
        fvec[pl.ds(c, 1), :] = total

    def back_in(l, c):
        cols = columns(c * 512, 512)
        put_natural(g[FIN], cols, dg(n2[...], slo[:, cols], 0, 0).astype(BF))

    def back_norm_two(l, t):
        cols = columns(t * TILE, TILE)
        pieces = []
        for x in range(2):
            for z in range(4):
                pieces.append(w[l][FIN][0, 2 * t + x, z])
                pieces.append(w[l][FIN][1, z, 2 * t + x])
        acc[:, cols] = dg(slo[...], jnp.concatenate(pieces, axis=0), 1, 1)

    def back_dense(l):
        put_natural(g[DENSE], slice(0, 512), dg(bt[...], carried[...], 1, 0).astype(BF))

    def back_attend(l, hp):
        weight = group_rows(w[l][DENSE], hp)
        below = dg(weight, carried[...], 1, 1)
        queries = qkvt[columns(hp * 128, 128), :]
        keys = qkvt[columns(D + hp * 128, 128), :]
        values = qkvt[columns(2 * D + hp * 128, 128), :].T
        blended = bt[columns(hp * 128, 128), :].astype(F32)
        blank = jnp.zeros((HEAD, TILE), BF)
        done = []
        for e in (0, 1):
            h = 2 * hp + e
            query = queries[e * HEAD : (e + 1) * HEAD]
            key = keys[e * HEAD : (e + 1) * HEAD]
            down = below[e * HEAD : (e + 1) * HEAD] * rinv[pl.ds(h, 1), :]
            centre = jnp.sum(down * blended[e * HEAD : (e + 1) * HEAD], axis=0, keepdims=True)
            down = down.astype(BF)
            grad_query = []
            for j in range(3):
                at_j = slice(j * TILE, (j + 1) * TILE)
                mine = down[:, at_j]
                mine = jnp.concatenate([mine, blank] if e == 0 else [blank, mine], axis=0)
                total = jnp.zeros((HEAD, TILE), F32)
                for i in range(j + 1):
                    cols = slice((j - i) * TILE, (j - i + 1) * TILE)
                    slope = dg(values[i * TILE : (i + 1) * TILE], mine, 1, 0) - centre[:, at_j]
                    slope = (slope * probs[i][h, :, cols].astype(F32)).astype(BF)
                    dscores[i][:, cols] = slope
                    total = total + dg(key[:, i * TILE : (i + 1) * TILE], slope, 1, 0)
                grad_query.append(total * 0.125)
            grad_key, grad_value = [], []
            for i in range(3):
                grad_key.append(dg(query[:, i * TILE :], dscores[i][...], 1, 1) * LN2)
                grad_value.append(dg(down[:, i * TILE :], probs[i][h], 1, 1))
            done.append(
                [jnp.concatenate(pieces, axis=1) for pieces in (grad_query, grad_key, grad_value)]
            )
        for which in range(3):
            value = jnp.concatenate([done[0][which], done[1][which]], axis=0)
            if which < 2:
                value = turn(value, cos_ref[...], -sin_ref[...])
            qkvt[columns(which * D + hp * 128, 128), :] = value.astype(BF)

    def back_qkv(l, t):
        cols = columns(t * 512, 512)
        put_natural(g[QKV], cols, dg(n1t[...], qkvt[cols, :], 1, 1).astype(BF))

    def back_norm_one(l, t):
        weight = group_rows(w[l][QKV], t)
        dn1[:, columns(t * 128, 128)] = dg(weight, qkvt[...], 1, 0).astype(BF).T

    def end_back(l):
        def tile(k):
            rows = columns(k * TILE, TILE)
            u, scale = normed(l, rows)
            first = dn1[rows, :].astype(F32)
            second = acc[rows, :]
            dvec[0:1, :] += jnp.sum(first * u, axis=0, keepdims=True)
            dvec[1:2, :] += jnp.sum(first, axis=0, keepdims=True)
            dvec[2:3, :] += jnp.sum(second * u, axis=0, keepdims=True)
            dvec[3:4, :] += jnp.sum(second, axis=0, keepdims=True)
            total = first * vd[0:1, :] + second * vd[2:3, :]
            centre = jnp.mean(total, axis=1, keepdims=True)
            along = jnp.mean(total * u, axis=1, keepdims=True)
            total = carried[rows, :].astype(F32) + scale * (total - centre - u * along)
            grad[l, rows, :] = total.astype(BF)

        loop(3, tile)

    def put_vectors(l):
        sums = dg(jnp.ones((8, T), BF), qkvt[...], 1, 1)
        g[VEC][...] = jnp.zeros((2, 4, 4, 8, 128), F32)
        for x in range(4):
            for z in range(4):
                g[VEC][0, x, z] = dvec[:, 128 * x : 128 * x + 128]
                for k in range(3):
                    row = 128 * (3 * x + k)
                    g[VEC][1, z, x, k : k + 1, :] = sums[0:1, row : row + 128]
                g[VEC][1, z, x, 3:4, :] = fvec[x : x + 1, 128 * z : 128 * z + 128]

    start_back(1)
    loop(4, lambda c: back_out(1, c))
    reduce[1][FOUT].step0()
    loop(4, lambda c: back_in(1, c))
    reduce[1][FIN].step0()
    reduce[1][FOUT].step1()
    loop(2, lambda t: back_norm_two(1, t))
    local(st_act, act, 8).start()
    local(st_slo, slo, 9).start()
    back_dense(1)
    reduce[1][DENSE].step0()
    reduce[1][FIN].step1()
    loop(2, lambda hp: back_attend(1, hp))
    reduce[1][FOUT].step2()
    reduce[1][DENSE].step1()
    loop(2, lambda hp: back_attend(1, hp + 2))
    reduce[1][FIN].step2()
    reduce[1][FOUT].step3()
    loop(3, lambda t: back_qkv(1, t))
    reduce[1][QKV].step0()
    loop(4, lambda t: back_norm_one(1, t))
    end_back(1)
    put_vectors(1)
    reduce[1][VEC].step0()
    for k, (a, b) in zip((2, 3, 4, 5, 6, 7), ((st_qkv, qkvt), (st_p0, p0), (st_p1, p1), (st_p2, p2), (st_bt, bt), (st_rinv, rinv))):
        local(a, b, k).start()
    reduce[1][QKV].step1()
    reduce[1][VEC].step1()
    reduce[1][DENSE].step2()

    unpack(0)
    norms(0)
    start_back(0)
    local(st_act, act, 8).wait()
    local(st_slo, slo, 9).wait()
    loop(4, lambda c: back_out(0, c))
    reduce[0][FOUT].step0()
    reduce[1][FIN].step3()
    reduce[1][FOUT].step4()
    loop(4, lambda c: back_in(0, c))
    reduce[0][FIN].step0()
    reduce[0][FOUT].step1()
    reduce[1][DENSE].step3()
    reduce[1][QKV].step2()
    reduce[1][VEC].step2()
    reduce[1][FIN].step4()
    loop(2, lambda t: back_norm_two(0, t))
    for k, (a, b) in zip((2, 3, 4, 5, 6, 7), ((st_qkv, qkvt), (st_p0, p0), (st_p1, p1), (st_p2, p2), (st_bt, bt), (st_rinv, rinv))):
        local(a, b, k).wait()
    back_dense(0)
    reduce[0][DENSE].step0()
    reduce[0][FIN].step1()
    loop(2, lambda hp: back_attend(0, hp))
    reduce[0][FOUT].step2()
    reduce[0][DENSE].step1()
    reduce[1][QKV].step3()
    reduce[1][VEC].step3()
    reduce[1][DENSE].step4()
    loop(2, lambda hp: back_attend(0, hp + 2))
    reduce[0][FIN].step2()
    reduce[0][FOUT].step3()
    loop(3, lambda t: back_qkv(0, t))
    reduce[0][QKV].step0()
    reduce[0][DENSE].step2()
    reduce[1][QKV].step4()
    reduce[1][VEC].step4()
    loop(4, lambda t: back_norm_one(0, t))
    reduce[0][QKV].step1()
    end_back(0)
    put_vectors(0)
    reduce[0][VEC].step0()
    grad_mine = local(grad.at[s], ig_out.at[s], 11)
    grad_theirs = remote(grad.at[1 - s], ig_out.at[s], ex_send.at[1], ex_recv.at[1], me.sibling())
    grad_mine.start()
    grad_theirs.start()
    reduce[0][FIN].step3()
    reduce[0][FOUT].step4()
    reduce[0][VEC].step1()
    reduce[0][DENSE].step3()
    reduce[0][FIN].step4()
    reduce[0][QKV].step2()
    reduce[0][VEC].step2()
    reduce[0][DENSE].step4()
    reduce[0][QKV].step3()
    reduce[0][VEC].step3()
    reduce[0][QKV].step4()
    reduce[0][VEC].step4()
    for l in (1, 0):
        for c in order:
            reduce[l][c].step5()
            reduce[l][c].finish()
    act_mine.wait()
    act_theirs.wait_send()
    remote(hid.at[2 - s], act_out.at[1 - s], ex_send.at[0], ex_recv.at[0], me.sibling()).wait_recv()
    grad_mine.wait()
    grad_theirs.wait_send()
    remote(grad.at[1 - s], ig_out.at[1 - s], ex_send.at[1], ex_recv.at[1], me.sibling()).wait_recv()


def scratch_shapes():
    def parts(lead):
        return [
            pltpu.VMEM((*lead, HALF_ROWS[c], WIDTH[c]), KIND[c]) for c in range(5)
        ]

    shapes = []
    for _ in (0, 1):
        shapes += parts((2, 4, 4))
    shapes += parts((2, 4, 4))
    for _ in (0, 1):
        shapes += parts((4, 4))
    for _ in (0, 1):
        shapes += parts((3, 4))
    for _ in (0, 1):
        shapes += parts((3,))
    for _ in (0, 1):
        shapes += parts((4,))
    shapes += [pltpu.VMEM((HALF_ROWS[c], WIDTH[c]), F32) for c in range(5)]
    shapes += [
        pltpu.VMEM((3, T, D), BF),
        pltpu.VMEM((3, T, D), BF),
        pltpu.VMEM((D, T), BF),
        pltpu.VMEM((T, D), BF),
        pltpu.VMEM((T, D), F32),
        pltpu.VMEM((T, D), BF),
    ]
    shapes += [pltpu.VMEM(shape, kind) for shape, kind in KEPT]
    shapes += [
        pltpu.VMEM((TILE, 768), BF),
        pltpu.VMEM((TILE, 512), BF),
        pltpu.VMEM((TILE, 256), BF),
        pltpu.VMEM((T, D), BF),
    ]
    shapes += [
        pltpu.VMEM((8, D), F32),
        pltpu.VMEM((16, 128), F32),
        pltpu.VMEM((8, 512), F32),
        pltpu.VMEM((8, D), F32),
        pltpu.VMEM((8, 512), F32),
        pltpu.VMEM((T, 1), F32),
        pltpu.VMEM((6, TILE, TILE), F32),
        pltpu.VMEM((8, T), F32),
        pltpu.VMEM((8, T), F32),
    ]
    dma = pltpu.SemaphoreType.DMA
    shapes += [dma((2, 5, 11))] * 4 + [dma((5,)), dma((12,)), dma((2,)), dma((2,))]
    return shapes


KEPT = (
    ((3 * D, T), BF),
    ((HEADS, TILE, 768), BF),
    ((HEADS, TILE, 512), BF),
    ((HEADS, TILE, 256), BF),
    ((D, T), BF),
    ((HEADS, T), F32),
    ((T, FF), BF),
    ((T, FF), BF),
)


def body(
    inputs,
    cotangent,
    lengths,
    norm1_gain,
    norm1_bias,
    qkv_weight,
    qkv_bias,
    dense_weight,
    norm2_gain,
    norm2_bias,
    fc_in_weight,
    fc_in_bias,
    fc_out_weight,
    out_bias,
):
    z = lax.axis_index("shard") % 4
    here = (jnp.arange(4) == z).astype(F32)
    five = jnp.concatenate([norm1_gain, norm1_bias, norm2_gain, norm2_bias, out_bias], axis=0).astype(F32)
    five = (five[:, None, :] * here[None, :, None]).reshape(5, 128)
    three = (qkv_bias.astype(F32) * here[:, None]).reshape(3, 128)
    last = jnp.concatenate([three, fc_in_bias.astype(F32)], axis=0)
    vec = jnp.stack([jnp.pad(five, ((0, 3), (0, 0))), jnp.pad(last, ((0, 4), (0, 0)))])

    hbm = pl.BlockSpec(memory_space=pl.ANY)
    vmem = pl.BlockSpec(memory_space=pltpu.VMEM)
    shape = jax.ShapeDtypeStruct
    results = pl.pallas_call(
        kernel,
        out_shape=[shape((2, T, D), BF), shape((2, T, D), BF)]
        + [shape((2, HALF_ROWS[c], WIDTH[c]), F32) for c in range(5)]
        + [shape(s, k) for s, k in KEPT],
        in_specs=[pl.BlockSpec(memory_space=pltpu.SMEM)] + [hbm] * 7,
        out_specs=[hbm] * 2 + [vmem] * 5 + [hbm] * len(KEPT),
        scratch_shapes=scratch_shapes(),
        compiler_params=pltpu.CompilerParams(
            collective_id=0, has_side_effects=True, vmem_limit_bytes=64 * 1024 * 1024
        ),
        name="layers",
    )(lengths, inputs, cotangent, qkv_weight, dense_weight, fc_in_weight, fc_out_weight, vec)
    activations, input_grads, gq, gd, gi, go, gv = results[:7]
    five = jnp.sum(gv[0, :5].reshape(5, 4, 32) * here[None, :, None], axis=1)
    bias = jnp.sum(gv[1, :3].reshape(4, 96) * here[:, None], axis=0)[None]
    return (
        activations[None],
        input_grads[None],
        five[0:1],
        five[1:2],
        gq.reshape(1, 32, 1536),
        bias,
        gd.reshape(1, 32, 512),
        five[2:3],
        five[3:4],
        gi.reshape(1, 32, 2048),
        gv[1, 3:4],
        go.reshape(1, 128, 512),
        five[4:5],
    )


def solution(mesh):
    rows = P(None, ("replica", "shard"), None)
    vector, matrix = P("section", "shard"), P("section", "shard", None)
    slabs = P("section", None, ("replica", "shard"), None)
    return jax.shard_map(
        body,
        mesh=mesh,
        in_specs=(
            rows, rows, rows, vector, vector, matrix, vector, matrix, vector, vector, matrix, vector, matrix, vector,
        ),
        out_specs=(
            slabs, slabs, vector, vector, matrix, vector, matrix, vector, vector, matrix, vector, matrix, vector,
        ),
        check_vma=False,
    )
```

```python
import math

import jax
import jax.numpy as jnp
from jax import lax
from jax.experimental import pallas as pl
from jax.experimental.pallas import tpu as pltpu
from jax.sharding import PartitionSpec as P

T = 768
D = 512
FF = 2048
HEADS = 8
HEAD = 64
ROT = 16
BLOCK = 128
SEQS = 4
TILE = 256
EPS = 1e-5
MASKED = -1e9
LOG2E = 1.0 / math.log(2.0)
LN2 = math.log(2.0)
MESH = pl.DeviceIdType.MESH
BF = jnp.bfloat16
F32 = jnp.float32

PAIRS = 4
DENSE, FIN, FOUT, VEC = 4, 5, 6, 7
PARTS = 8
LETTERS = "abcdDIOV"
HALF_ROWS = (16, 16, 16, 16, 16, 16, 64, 8)
WIDTH = (384, 384, 384, 384, 512, 2048, 512, 128)
KIND = (BF, BF, BF, BF, BF, BF, BF, F32)


def dg(a, b, ca, cb):
    return lax.dot_general(a, b, (((ca,), (cb,)), ((), ())), preferred_element_type=F32)


class Place:
    def __init__(self):
        self.s = lax.axis_index("section")
        self.y = lax.axis_index("replica")
        shard = lax.axis_index("shard")
        x, z = shard // 4, shard % 4
        self.shard, self.x, self.z = shard, x, z
        self.p = x + self.s * (z - x)
        self.q = z + self.s * (x - z)

    def at(self, p, q):
        return (1 - self.s) * (4 * p + q) + self.s * (4 * q + p)

    def sibling(self):
        return (1 - self.s, self.y, self.shard)

    def along_p(self, d):
        return (self.s, self.y, self.at((self.p + d) % 4, self.q))

    def along_q(self, d):
        return (self.s, self.y, self.at(self.p, (self.q + d) % 4))

    def along_y(self, d):
        return (self.s, (self.y + d) % 4, self.shard)


def remote(src, dst, send, recv, device):
    return pltpu.make_async_remote_copy(
        src_ref=src, dst_ref=dst, send_sem=send, recv_sem=recv, device_id=device, device_id_type=MESH
    )


class Gather:
    def __init__(self, me, layer, part, shard_ref, whole, send, recv, local):
        self.me, self.layer, self.part = me, layer, part
        self.shard_ref, self.w = shard_ref, whole
        self.send = lambda k: send.at[layer, part, k]
        self.recv = lambda k: recv.at[layer, part, k]
        self.local = local.at[part]
        self.rows = HALF_ROWS[part]
        self.direct = layer == 0 and part in (0, 1, 2, 3, VEC)
        self.ways = (1, 3, 2) if self.direct else (1, 3)

    def halves(self, h, target):
        if self.part == VEC:
            return [(self.shard_ref.at[h], target)]
        rows = pl.ds(pl.multiple_of(h * self.rows, self.rows), self.rows)
        if self.part < PAIRS:
            return [
                (
                    self.shard_ref.at[0, rows, pl.ds(512 * which + 128 * self.part, 128)],
                    target.at[:, pl.ds(128 * which, 128)],
                )
                for which in range(3)
            ]
        return [(self.shard_ref.at[0, rows, :], target)]

    def move(self, ref, sent, came, device):
        return remote(ref, ref, self.send(sent), self.recv(came), device)

    def shards(self, count):
        return self.move(self.w.at[self.me.s, pl.ds(0, count)], 1, 1, self.me.sibling())

    def row(self, half, p):
        return self.w.at[half, pl.ds(4 * p, 4)]

    def own(self, half, p, q):
        return self.w.at[half, 4 * p + q]

    def step0(self):
        me = self.me

        @pl.when(me.s == self.layer)
        def _():
            for src, dst in self.halves(me.s, self.own(me.s, me.p, me.q)):
                pltpu.make_async_copy(src, dst, self.local).start()
            for src, dst in self.halves(1 - me.s, self.own(1 - me.s, me.q, me.p)):
                remote(src, dst, self.send(0), self.recv(0), me.sibling()).start()

    def step1(self):
        me = self.me
        own = self.own(me.s, me.p, me.q)

        @pl.when(me.s == self.layer)
        def _():
            pltpu.make_async_copy(own, own, self.local).wait()

        @pl.when(me.s != self.layer)
        def _():
            self.move(own, 0, 0, me.sibling()).wait_recv()

        for d in (1, 3, 2):
            self.move(own, 1, 1, me.along_q(d)).start()

    def across(self, p):
        self.move(self.row(self.me.s, p), 2, 4, self.me.sibling()).start()

    def step2(self):
        me = self.me
        self.shards(3).wait_recv()
        for d in self.ways:
            self.move(self.row(me.s, me.p), 1, 2, me.along_p(d)).start()
        self.across(me.p)

    def step3(self):
        me = self.me
        ref = self.w.at[me.s, pl.ds(0, 4 * len(self.ways))]
        self.move(ref, 1, 2, me.sibling()).wait_recv()
        if not self.direct:
            for d in (1, 3):
                half = self.w.at[me.s, pl.ds(4 * ((me.p + 4 - d) % 4) + d - 1, 2)]
                self.move(half, 1, 3, me.along_p(d)).start()
        for d in self.ways:
            self.across((me.p + 4 - d) % 4)

    def step4(self):
        me = self.me
        if not self.direct:
            self.move(self.row(me.s, me.p), 1, 3, me.sibling()).wait_recv()
            self.across((me.p + 2) % 4)

    def step5(self):
        self.move(self.w.at[1 - self.me.s], 2, 4, self.me.sibling()).wait_recv()

    def finish(self):
        me = self.me

        @pl.when(me.s == self.layer)
        def _():
            self.move(self.own(1 - me.s, me.q, me.p), 0, 0, me.sibling()).wait_send()

        self.shards(15).wait_send()
        self.move(self.w.at[me.s], 2, 4, me.sibling()).wait_send()


class Reduce:
    def __init__(self, me, layer, part, terms, buffers, send, recv):
        self.me, self.layer, self.part = me, layer, part
        self.g = terms
        self.r, self.one, self.two, self.ys, self.f, self.out = buffers
        self.send = lambda k: send.at[layer, part, k]
        self.recv = lambda k: recv.at[layer, part, k]
        self.kind = KIND[part]

    def swap(self):
        me = self.me
        return remote(self.g.at[1 - me.s], self.r, self.send(0), self.recv(0), me.sibling())

    def first(self, d):
        me = self.me
        row = self.r.at[pl.ds(4 * ((me.p + d) % 4), 4)]
        return remote(row, self.one.at[d - 1], self.send(1), self.recv(1), me.along_p(d))

    def second(self, d):
        me = self.me
        shard = self.r.at[4 * me.p + (me.q + d) % 4]
        return remote(shard, self.two.at[d - 1], self.send(2), self.recv(2), me.along_q(d))

    def third(self, d):
        me = self.me
        return remote(self.ys.at[me.y], self.ys.at[me.y], self.send(3), self.recv(3), me.along_y(d))

    def all_of(self, ref, k):
        return remote(ref, ref, self.send(k), self.recv(k), self.me.sibling())

    def back(self):
        me = self.me
        return remote(self.f, self.out.at[me.s], self.send(4), self.recv(4), me.sibling())

    def step0(self):
        self.swap().start()

    def step1(self):
        me = self.me
        self.swap().wait_recv()

        def one(k, c):
            self.r[k] = (self.r[k].astype(F32) + self.g[me.s, k].astype(F32)).astype(self.kind)
            return c

        lax.fori_loop(0, 16, one, 0)
        for d in (1, 3, 2):
            self.first(d).start()
        self.swap().wait_send()

    def step2(self):
        me = self.me
        self.all_of(self.one, 1).wait_recv()

        def one(b, c):
            total = self.r[4 * me.p + b].astype(F32) + self.one[0, b].astype(F32)
            total = total + (self.one[1, b].astype(F32) + self.one[2, b].astype(F32))
            self.r[4 * me.p + b] = total.astype(self.kind)
            return c

        lax.fori_loop(0, 4, one, 0)
        for d in (1, 3, 2):
            self.second(d).start()

    def step3(self):
        me = self.me
        self.all_of(self.two, 2).wait_recv()
        total = self.r[4 * me.p + me.q].astype(F32) + self.two[0].astype(F32)
        total = total + (self.two[1].astype(F32) + self.two[2].astype(F32))
        self.ys[me.y] = total.astype(self.kind)
        for d in (1, 3, 2):
            self.third(d).start()

    def step4(self):
        me = self.me
        self.all_of(self.ys.at[pl.ds(0, 3)], 3).wait_recv()
        total = (self.ys[0].astype(F32) + self.ys[1].astype(F32)) + (
            self.ys[2].astype(F32) + self.ys[3].astype(F32)
        )

        @pl.when(me.s == self.layer)
        def _():
            self.out[me.s] = total

        @pl.when(me.s != self.layer)
        def _():
            self.f[...] = total
            self.back().start()

    def step5(self):
        me = self.me

        @pl.when(me.s == self.layer)
        def _():
            self.all_of(self.out.at[1 - me.s], 4).wait_recv()

    def finish(self):
        self.all_of(self.one, 1).wait_send()
        self.all_of(self.two, 2).wait_send()
        self.all_of(self.ys.at[pl.ds(0, 3)], 3).wait_send()

        @pl.when(self.me.s != self.layer)
        def _():
            self.back().wait_send()


class ReduceVectors:
    def __init__(self, me, layer, terms, buffers, send, recv):
        self.me, self.layer, self.g = me, layer, terms
        self.r, self.one, self.ys, self.out = buffers
        self.send = lambda k: send.at[layer, VEC, k]
        self.recv = lambda k: recv.at[layer, VEC, k]

    def swap(self):
        return remote(self.g, self.r, self.send(0), self.recv(0), self.me.sibling())

    def first(self, k):
        x, z = (self.me.x + k // 4) % 4, (self.me.z + k % 4) % 4
        device = (self.me.s, self.me.y, 4 * x + z)
        return remote(self.r.at[x, z], self.one.at[k], self.send(1), self.recv(1), device)

    def all_first(self):
        ref = self.one.at[pl.ds(1, 15)]
        return remote(ref, ref, self.send(1), self.recv(1), self.me.sibling())

    def third(self, d):
        me = self.me
        return remote(self.ys.at[me.y], self.ys.at[me.y], self.send(3), self.recv(3), me.along_y(d))

    def all_third(self):
        ref = self.ys.at[pl.ds(0, 3)]
        return remote(ref, ref, self.send(3), self.recv(3), self.me.sibling())

    def owner(self, step):
        pl.when(self.me.s == self.layer)(step)

    def step0(self):
        @pl.when(self.me.s != self.layer)
        def _():
            self.swap().start()

    def step1(self):
        def step():
            self.swap().wait_recv()
            self.r[...] += self.g[...]
            for k in (1, 4, 3, 12, 5, 7, 13, 15, 2, 8, 6, 9, 11, 14, 10):
                self.first(k).start()

        self.owner(step)

        @pl.when(self.me.s != self.layer)
        def _():
            self.swap().wait_send()

    def step2(self):
        def step():
            self.all_first().wait_recv()
            total = self.r[self.me.x, self.me.z]
            for k in range(1, 16):
                total = total + self.one[k]
            self.ys[self.me.y] = total
            for d in (1, 3, 2):
                self.third(d).start()

        self.owner(step)

    def step3(self):
        def step():
            self.all_third().wait_recv()
            self.out[...] = (self.ys[0] + self.ys[1]) + (self.ys[2] + self.ys[3])

        self.owner(step)

    def step5(self):
        pass

    def finish(self):
        def step():
            self.all_first().wait_send()
            self.all_third().wait_send()

        self.owner(step)


def natural_rows(ref, columns):
    pieces = []
    for x in range(4):
        for z in range(4):
            pieces.append(ref[0, 4 * x + z, :, columns])
            pieces.append(ref[1, 4 * z + x, :, columns])
    return jnp.concatenate(pieces, axis=0)


def group_rows(ref, x):
    pieces = []
    for z in range(4):
        pieces.append(ref[0, 4 * x + z])
        pieces.append(ref[1, 4 * z + x])
    return jnp.concatenate(pieces, axis=0)


def put_natural(ref, columns, value):
    for x in range(4):
        for z in range(4):
            row = 32 * (4 * x + z)
            ref[0, 4 * x + z, :, columns] = value[row : row + 16]
            ref[1, 4 * z + x, :, columns] = value[row + 16 : row + 32]


def put_group(ref, x, value, rows):
    for z in range(4):
        row = 2 * rows * z
        ref[0, 4 * x + z] = value[row : row + rows]
        ref[1, 4 * z + x] = value[row + rows : row + 2 * rows]


def to_column(row):
    here = lax.broadcasted_iota(jnp.int32, (128, 128), 0) == lax.broadcasted_iota(
        jnp.int32, (128, 128), 1
    )
    return jnp.sum(jnp.where(here, row, 0.0), axis=1, keepdims=True)


def turn(rows, cosine, sine):
    pieces = []
    for e in (0, 64):
        low, high = rows[e : e + 8], rows[e + 8 : e + 16]
        pieces += [low * cosine - high * sine, high * cosine + low * sine, rows[e + 16 : e + 64]]
    return jnp.concatenate(pieces, axis=0)


def columns(start, size):
    return pl.ds(pl.multiple_of(start, size), size)


def loop(count, step):
    def one(k, c):
        step(k)
        return c

    lax.fori_loop(0, count, one, 0)


def kernel(
    lengths,
    x_ref,
    cot_ref,
    wq_ref,
    wd_ref,
    wi_ref,
    wo_ref,
    gain1_ref,
    shift1_ref,
    gain2_ref,
    shift2_ref,
    last_ref,
    qkvb_ref,
    finb_ref,
    act_out,
    ig_out,
    gq_out,
    gd_out,
    gi_out,
    go_out,
    gv_out,
    st_qkv,
    st_p0,
    st_p1,
    st_p2,
    st_bt,
    st_rinv,
    st_act,
    st_slo,
    *scratch,
):
    scratch = list(scratch)

    def take(count):
        taken, scratch[:count] = scratch[:count], []
        return taken

    def take_parts(count=4):
        pairs, *rest = take(count)
        return [pairs] + [pairs.at[k] for k in range(PAIRS)] + rest

    (wq0, *w0), (wq1, *w1) = take_parts(5), take_parts(5)
    w, wq = (w0, w1), (wq0, wq1)
    gq, *g = take_parts()
    r, one, two, ys = [(take_parts()[1:], take_parts()[1:]) for _ in range(4)]
    f = take_parts()[1:]
    gvec, *rvec = take(3)
    vecs, yvec, (vsrc, vrow) = take(2), take(2), take(2)
    hid, grad, n1t, n2, acc, carried = take(6)
    qkvt, p0, p1, p2, bt, rinv, act, slo = take(8)
    d0, d1, d2, dn1 = take(4)
    vd, vq, vf, dvec, fvec, live, bias, cos_ref, sin_ref = take(9)
    sends, ag_recv, rs_recv, ag_local, sems, ex_send, ex_recv = take(7)
    probs = (p0, p1, p2)
    dscores = (d0, d1, d2)
    outs = [gq_out.at[k] for k in range(PAIRS)] + [gd_out, gi_out, go_out]
    shards = [wq_ref] * PAIRS + [wd_ref, wi_ref, wo_ref, vsrc]

    me = Place()
    s = me.s
    barrier = pltpu.get_barrier_semaphore()
    partners = [me.sibling()]
    for d in (1, 2, 3):
        partners += [me.along_q(d), me.along_p(d), me.along_y(d)]
        for e in (1, 2, 3):
            partners.append((s, me.y, 4 * ((me.x + d) % 4) + (me.z + e) % 4))
    for device in partners:
        pl.semaphore_signal(barrier, inc=1, device_id=device, device_id_type=MESH)
    pl.semaphore_wait(barrier, len(partners))

    gather = [
        [Gather(me, l, c, shards[c], w[l][c], sends, ag_recv, ag_local) for c in range(PARTS)]
        for l in (0, 1)
    ]
    reduce = [
        [
            Reduce(
                me, l, c, g[c], (r[l][c], one[l][c], two[l][c], ys[l][c], f[c], outs[c]), sends, rs_recv
            )
            for c in range(VEC)
        ]
        + [ReduceVectors(me, l, gvec, (rvec[l], vecs[l], yvec[l], gv_out), sends, rs_recv)]
        for l in (0, 1)
    ]

    def fetch(*plan):
        for word in plan:
            item = gather[int(word[0])][LETTERS.index(word[1])]
            getattr(item, "step" + word[2])()

    def send(*plan):
        for word in plan:
            item = reduce[int(word[0])][LETTERS.index(word[1])]
            getattr(item, "step" + word[2])()

    vsrc[...] = jnp.zeros((2, 8, 128), F32)
    for k in range(4):
        here = me.z == k
        for row, ref in enumerate((gain1_ref, shift1_ref, gain2_ref, shift2_ref, last_ref)):
            vsrc[0, row : row + 1, 32 * k : 32 * k + 32] = jnp.where(here, ref[...].astype(F32), 0.0)
        vrow[0:1, 96 * k : 96 * k + 96] = jnp.where(here, qkvb_ref[...].astype(F32), 0.0)
    for k in range(3):
        vsrc[1, k : k + 1, :] = vrow[0:1, 128 * k : 128 * k + 128]
    vsrc[1, 3:4, :] = finb_ref[...].astype(F32)

    x_in = pltpu.make_async_copy(x_ref.at[s], hid.at[0], sems.at[0])
    cot_in = pltpu.make_async_copy(cot_ref.at[s], grad.at[0], sems.at[1])
    x_in.start()
    fetch("0V0", "0a0", "0b0", "0c0", "0d0", "0I0", "0D0", "0O0", "1V0", "1a0", "1b0", "1c0", "1d0", "1I0", "1D0", "1O0")
    fetch("0V1", "0a1", "0b1", "0c1", "0d1", "0D1", "0I1", "0O1")
    cot_in.start()

    starts, ends, at = [], [], jnp.int32(0)
    for k in range(SEQS):
        size = lengths[s, 0, k]
        starts.append(at)
        ends.append(at + size)
        at = at + (size + BLOCK - 1) // BLOCK * BLOCK

    def inside(places):
        return [(places >= a) & (places < b) for a, b in zip(starts, ends)]

    def live_tile(k):
        places = lax.broadcasted_iota(jnp.int32, (TILE, 1), 0) + k * TILE
        total = jnp.zeros((TILE, 1), F32)
        for found in inside(places):
            total = total + jnp.where(found, 1.0, 0.0)
        live[columns(k * TILE, TILE), :] = total

    loop(3, live_tile)
    places = lax.broadcasted_iota(jnp.int32, (8, T), 1)
    begin = jnp.zeros((8, T), jnp.int32)
    offset = jnp.zeros((8, T), jnp.int32)
    for found, a in zip(inside(places), starts):
        begin = begin + jnp.where(found, a, 0)
        offset = offset + jnp.where(found, places - a, 0)
    rates = jnp.exp(
        lax.broadcasted_iota(jnp.int32, (8, T), 0).astype(F32) * (-2.0 * math.log(10000.0) / ROT)
    )
    angles = offset.astype(F32) * rates
    cos_ref[...] = jnp.cos(angles)
    sin_ref[...] = jnp.sin(angles)
    for j in range(3):
        for i in range(j + 1):
            keys = lax.broadcasted_iota(jnp.int32, (TILE, TILE), 0) + i * TILE
            queries = lax.broadcasted_iota(jnp.int32, (TILE, TILE), 1) + j * TILE
            fits = (keys >= begin[0:1, j * TILE : (j + 1) * TILE]) & (keys <= queries)
            bias[j * (j + 1) // 2 + i] = jnp.where(fits, 0.0, MASKED)

    def unpack(l):
        ref = w[l][VEC]
        for x in range(4):
            vd[:, 128 * x : 128 * x + 128] = (ref[0, 4 * x] + ref[0, 4 * x + 1]) + (
                ref[0, 4 * x + 2] + ref[0, 4 * x + 3]
            )
            group = (ref[1, x] + ref[1, 4 + x]) + (ref[1, 8 + x] + ref[1, 12 + x])
            for k in range(3):
                vq[3 * x + k : 3 * x + k + 1, :] = group[k : k + 1]
            for z in range(4):
                vf[x : x + 1, 128 * z : 128 * z + 128] = ref[1, 4 * z + x][3:4]

    def normed(l, rows):
        v = hid[l, rows, :].astype(F32)
        centred = v - jnp.mean(v, axis=1, keepdims=True)
        scale = lax.rsqrt(jnp.mean(centred * centred, axis=1, keepdims=True) + EPS)
        return centred * scale, scale

    def norms(l):
        def tile(k):
            rows = columns(k * TILE, TILE)
            u, _ = normed(l, rows)
            n1t[:, rows] = (u * vd[0:1, :] + vd[1:2, :]).astype(BF).T
            n2[rows, :] = (u * vd[2:3, :] + vd[3:4, :]).astype(BF)

        loop(3, tile)

    def attend(l, hp):
        pair = []
        for which in range(3):
            rows = columns(hp * 384 + which * 128, 128)
            weight = natural_rows(wq[l].at[hp], slice(128 * which, 128 * which + 128))
            value = dg(weight, n1t[...], 0, 0) + to_column(vq[pl.ds(which * 4 + hp, 1), :])
            if which < 2:
                value = turn(value, cos_ref[...], sin_ref[...])
            if which == 0:
                value = value * (LOG2E / 8.0)
            pair.append(value.astype(BF))
            qkvt[rows, :] = pair[which]
        keys = pair[1].T
        blank = jnp.zeros((HEAD, TILE), BF)
        for e in (0, 1):
            h = 2 * hp + e
            query = pair[0][e * HEAD : (e + 1) * HEAD]
            value = pair[2][e * HEAD : (e + 1) * HEAD]
            for j in range(3):
                at_j = slice(j * TILE, (j + 1) * TILE)
                mine = query[:, at_j]
                mine = jnp.concatenate([mine, blank] if e == 0 else [blank, mine], axis=0)
                scores = [
                    dg(keys[i * TILE : (i + 1) * TILE], mine, 1, 0) + bias[j * (j + 1) // 2 + i]
                    for i in range(j + 1)
                ]
                peak = jnp.max(scores[0], axis=0, keepdims=True)
                for i in range(1, j + 1):
                    peak = jnp.maximum(peak, jnp.max(scores[i], axis=0, keepdims=True))
                total = jnp.zeros((1, TILE), F32)
                blended = jnp.zeros((HEAD, TILE), F32)
                for i in range(j + 1):
                    raised = jnp.exp2(scores[i] - peak)
                    total = total + jnp.sum(raised, axis=0, keepdims=True)
                    raised = raised.astype(BF)
                    probs[i][h, :, (j - i) * TILE : (j - i + 1) * TILE] = raised
                    blended = blended + dg(value[:, i * TILE : (i + 1) * TILE], raised, 1, 0)
                inverse = 1.0 / total
                rinv[pl.ds(h, 1), at_j] = inverse
                bt[columns(hp * 128 + e * HEAD, HEAD), at_j] = (blended * inverse).astype(BF)

    def widen(l, c):
        cols = columns(c * 512, 512)
        weight = natural_rows(w[l][FIN], cols)
        shift = vf[pl.ds(c, 1), :]

        def tile(k):
            rows = columns(k * TILE, TILE)
            v = dg(n2[rows, :], weight, 1, 0) + shift
            below = 0.5 + 0.5 * lax.erf(v * (1.0 / math.sqrt(2.0)))
            act[rows, cols] = (v * below).astype(BF)
            slope = below + v * (jnp.exp(-0.5 * v * v) * (1.0 / math.sqrt(2.0 * math.pi)))
            slo[rows, cols] = slope.astype(BF)

        for k in range(3):
            tile(k)

    def join(l):
        def part(t):
            cols = columns(t * TILE, TILE)
            weight = jnp.concatenate(
                [
                    piece
                    for x in range(4)
                    for z in range(4)
                    for piece in (w[l][FOUT][0, 4 * x + z, :, cols], w[l][FOUT][1, 4 * z + x, :, cols])
                ],
                axis=0,
            )
            total = dg(act[...], weight, 1, 0)
            total = total + dg(bt[...], natural_rows(w[l][DENSE], cols), 0, 0)
            total = total + hid[l, :, cols].astype(F32) + vd[4:5, cols]
            hid[l + 1, :, cols] = (total * live[...]).astype(BF)

        loop(2, part)

    def local(src, dst, k):
        return pltpu.make_async_copy(src, dst, sems.at[k])

    attention_kept = [
        (qkvt, st_qkv, 2),
        (p0, st_p0, 3),
        (p1, st_p1, 4),
        (p2, st_p2, 5),
        (bt, st_bt, 6),
        (rinv, st_rinv, 7),
    ]
    wide_kept = [(act, st_act, 8), (slo, st_slo, 9)]

    fetch("0V2", "0a2", "0b2", "0c2", "0d2")
    x_in.wait()
    fetch("0V3", "0a3")
    fetch("0D2", "0I2")
    fetch("0V5")
    unpack(0)
    norms(0)
    fetch("0b3", "0O2", "0a5")
    attend(0, 0)
    fetch("0c3", "0b5")
    attend(0, 1)
    fetch("0d3", "0D3", "0I3", "0c5")
    fetch("1V1", "1a1", "1b1", "1c1", "1d1")
    attend(0, 2)
    fetch("0O3", "0d5")
    fetch("1I1", "1D1", "1O1")
    attend(0, 3)
    for a, b, k in attention_kept:
        local(a, b, k).start()
    fetch("0D4", "0I4", "1V2", "1a2", "1b2")
    fetch("0I5")
    loop(2, lambda c: widen(0, c))
    fetch("0O4")
    fetch("1c2", "1d2", "1V3", "1a3")
    loop(2, lambda c: widen(0, c + 2))
    fetch("1b3", "1c3", "1d3", "1I2", "1D2", "1O2", "0D5", "0O5")
    join(0)
    for a, b, k in wide_kept:
        local(a, b, k).start()

    fetch("1V4", "1a4", "1b4")
    fetch("1V5")
    unpack(1)
    norms(1)
    fetch("1c4", "1d4", "1a5")
    for a, b, k in attention_kept:
        local(a, b, k).wait()
    attend(1, 0)
    fetch("1I3", "1D3", "1b5")
    attend(1, 1)
    fetch("1O3", "1c5")
    attend(1, 2)
    fetch("1I4", "1D4", "1d5")
    attend(1, 3)
    fetch("1O4", "1I5")
    for a, b, k in wide_kept:
        local(a, b, k).wait()
    loop(4, lambda c: widen(1, c))
    fetch("1D5", "1O5")
    join(1)
    for l in (0, 1):
        for c in range(PARTS):
            gather[l][c].finish()
    act_mine = local(hid.at[1 + s], act_out.at[s], 10)
    act_theirs = remote(hid.at[2 - s], act_out.at[s], ex_send.at[0], ex_recv.at[0], me.sibling())
    act_mine.start()
    act_theirs.start()
    cot_in.wait()

    def start_back(l):
        def tile(k):
            rows = columns(k * TILE, TILE)
            v = grad[1 - l, rows, :].astype(F32) * live[rows, :]
            carried[rows, :] = v.astype(BF)
            here = jnp.sum(v, axis=0, keepdims=True)
            dvec[4:5, :] = here + jnp.where(k == 0, 0.0, dvec[4:5, :])

        dvec[...] = jnp.zeros((8, D), F32)
        loop(3, tile)

    def back_out(c):
        cols = columns(c * 512, 512)
        put_group(g[FOUT], c, dg(act[:, cols], carried[...], 0, 0).astype(BF), 64)

    def back_wide(l, c):
        cols = columns(c * 512, 512)
        weight = group_rows(w[l][FOUT], c)
        total = jnp.zeros((1, 512), F32)
        for k in range(3):
            rows = slice(k * TILE, (k + 1) * TILE)
            v = dg(carried[rows, :], weight, 1, 1) * slo[rows, cols].astype(F32)
            v = v.astype(BF)
            slo[rows, cols] = v
            total = total + jnp.sum(v.astype(F32), axis=0, keepdims=True)
        fvec[pl.ds(c, 1), :] = total

    def back_in(l, c):
        cols = columns(c * 512, 512)
        put_natural(g[FIN], cols, dg(n2[...], slo[:, cols], 0, 0).astype(BF))

    def back_norm_two(l, t):
        low = w[l][FIN][0, pl.ds(8 * t, 8)]
        high = [w[l][FIN][1, pl.ds(4 * z + 2 * t, 2)] for z in range(4)]
        pieces = []
        for x in range(2):
            for z in range(4):
                pieces += [low[4 * x + z], high[z][x]]
        acc[:, columns(t * TILE, TILE)] = dg(slo[...], jnp.concatenate(pieces, axis=0), 1, 1)

    def back_dense(l):
        put_natural(g[DENSE], slice(0, 512), dg(bt[...], carried[...], 1, 0).astype(BF))

    def back_attend(l, hp):
        weight = group_rows(w[l][DENSE], hp)
        below = dg(weight, carried[...], 1, 1)
        queries = qkvt[columns(hp * 384, 128), :]
        keys = qkvt[columns(hp * 384 + 128, 128), :]
        values = qkvt[columns(hp * 384 + 256, 128), :].T
        blended = bt[columns(hp * 128, 128), :].astype(F32)
        blank = jnp.zeros((HEAD, TILE), BF)
        done = []
        for e in (0, 1):
            h = 2 * hp + e
            query = queries[e * HEAD : (e + 1) * HEAD]
            key = keys[e * HEAD : (e + 1) * HEAD]
            down = below[e * HEAD : (e + 1) * HEAD] * rinv[pl.ds(h, 1), :]
            centre = jnp.sum(down * blended[e * HEAD : (e + 1) * HEAD], axis=0, keepdims=True)
            down = down.astype(BF)
            grad_query = []
            for j in range(3):
                at_j = slice(j * TILE, (j + 1) * TILE)
                mine = down[:, at_j]
                mine = jnp.concatenate([mine, blank] if e == 0 else [blank, mine], axis=0)
                total = jnp.zeros((HEAD, TILE), F32)
                for i in range(j + 1):
                    cols = slice((j - i) * TILE, (j - i + 1) * TILE)
                    slope = dg(values[i * TILE : (i + 1) * TILE], mine, 1, 0) - centre[:, at_j]
                    slope = (slope * probs[i][h, :, cols].astype(F32)).astype(BF)
                    dscores[i][:, cols] = slope
                    total = total + dg(key[:, i * TILE : (i + 1) * TILE], slope, 1, 0)
                grad_query.append(total * 0.125)
            grad_key, grad_value = [], []
            for i in range(3):
                grad_key.append(dg(query[:, i * TILE :], dscores[i][...], 1, 1) * LN2)
                grad_value.append(dg(down[:, i * TILE :], probs[i][h], 1, 1))
            done.append(
                [jnp.concatenate(pieces, axis=1) for pieces in (grad_query, grad_key, grad_value)]
            )
        for which in range(3):
            value = jnp.concatenate([done[0][which], done[1][which]], axis=0)
            if which < 2:
                value = turn(value, cos_ref[...], -sin_ref[...])
            qkvt[columns(hp * 384 + which * 128, 128), :] = value.astype(BF)

    def back_qkv(hp):
        value = dg(n1t[...], qkvt[columns(hp * 384, 384), :], 1, 1)
        put_natural(gq.at[hp], slice(0, 384), value.astype(BF))

    def back_norm_one(l, t):
        weight = jnp.concatenate([group_rows(wq[l].at[hp], t) for hp in range(PAIRS)], axis=1)
        dn1[:, columns(t * 128, 128)] = dg(weight, qkvt[...], 1, 0).astype(BF).T

    def norm_sums(l):
        def tile(k):
            rows = columns(k * TILE, TILE)
            u, _ = normed(l, rows)
            first = dn1[rows, :].astype(F32)
            second = acc[rows, :]
            dvec[0:1, :] += jnp.sum(first * u, axis=0, keepdims=True)
            dvec[1:2, :] += jnp.sum(first, axis=0, keepdims=True)
            dvec[2:3, :] += jnp.sum(second * u, axis=0, keepdims=True)
            dvec[3:4, :] += jnp.sum(second, axis=0, keepdims=True)

        loop(3, tile)

    def end_back(l):
        def tile(k):
            rows = columns(k * TILE, TILE)
            u, scale = normed(l, rows)
            first = dn1[rows, :].astype(F32)
            second = acc[rows, :]
            total = first * vd[0:1, :] + second * vd[2:3, :]
            centre = jnp.mean(total, axis=1, keepdims=True)
            along = jnp.mean(total * u, axis=1, keepdims=True)
            total = carried[rows, :].astype(F32) + scale * (total - centre - u * along)
            grad[l, rows, :] = total.astype(BF)

        loop(3, tile)

    def put_vectors(l):
        sums = dg(jnp.ones((8, T), BF), qkvt[...], 1, 1)
        for x in range(4):
            for k in range(3):
                which, hp = divmod(3 * x + k, PAIRS)
                row = 384 * hp + 128 * which
                vq[3 * x + k : 3 * x + k + 1, :] = sums[0:1, row : row + 128]
        for x in range(4):
            rest = jnp.concatenate([vq[3 * x : 3 * x + 3, :], jnp.zeros((5, 128), F32)], axis=0)
            for z in range(4):
                gvec[x, z, 0:8] = dvec[:, 128 * x : 128 * x + 128]
                gvec[x, z, 8:16] = rest
                gvec[x, z, 11:12] = fvec[x : x + 1, 128 * z : 128 * z + 128]

    restored = ((qkvt, st_qkv, 2), (p0, st_p0, 3), (p1, st_p1, 4), (p2, st_p2, 5), (bt, st_bt, 6), (rinv, st_rinv, 7))

    start_back(1)
    loop(4, back_out)
    send("1O0")
    loop(4, lambda c: back_wide(1, c))
    send("1O1")
    loop(4, lambda c: back_in(1, c))
    send("1I0")
    loop(2, lambda t: back_norm_two(1, t))
    local(st_act, act, 8).start()
    local(st_slo, slo, 9).start()
    back_dense(1)
    send("1D0", "1I1")
    back_attend(1, 0)
    back_qkv(0)
    send("1a0", "1D1")
    back_attend(1, 1)
    back_qkv(1)
    send("1b0", "1a1")
    back_attend(1, 2)
    back_qkv(2)
    send("1c0", "1b1", "1O2")
    back_attend(1, 3)
    back_qkv(3)
    send("1d0", "1c1", "1I2")
    loop(4, lambda t: back_norm_one(1, t))
    send("1d1", "1D2", "1O3")
    norm_sums(1)
    put_vectors(1)
    for a, b, k in restored:
        local(b, a, k).start()
    send("1V0", "1a2")
    end_back(1)

    unpack(0)
    norms(0)
    start_back(0)
    local(st_act, act, 8).wait()
    local(st_slo, slo, 9).wait()
    send("1b2", "1I3")
    loop(4, back_out)
    send("0O0", "1V1", "1D3", "1c2", "1d2", "1a3")
    loop(4, lambda c: back_wide(0, c))
    send("0O1", "1O4", "1b3")
    loop(4, lambda c: back_in(0, c))
    send("0I0", "1V2", "1c3", "1d3", "1D4")
    loop(2, lambda t: back_norm_two(0, t))
    send("0I1", "1I4", "1a4", "1b4")
    for a, b, k in restored:
        local(b, a, k).wait()
    back_dense(0)
    send("0D0")
    back_attend(0, 0)
    back_qkv(0)
    send("0a0", "0D1", "1V3", "1c4", "1d4")
    back_attend(0, 1)
    back_qkv(1)
    send("0b0", "0a1", "0O2")
    back_attend(0, 2)
    back_qkv(2)
    send("0c0", "0b1")
    back_attend(0, 3)
    back_qkv(3)
    send("0d0", "0c1")
    send("0D2", "0a2", "0O3")
    send("0I2")
    loop(2, lambda t: back_norm_one(0, t))
    send("0d1", "0b2")
    loop(2, lambda t: back_norm_one(0, t + 2))
    send("0c2")
    norm_sums(0)
    put_vectors(0)
    send("0V0", "0D3", "0a3", "0d2")
    send("0V1")
    send("0O4")
    send("0I3")
    end_back(0)
    grad_mine = local(grad.at[s], ig_out.at[s], 11)
    grad_theirs = remote(grad.at[1 - s], ig_out.at[s], ex_send.at[1], ex_recv.at[1], me.sibling())
    grad_mine.start()
    grad_theirs.start()
    send("0b3", "0c3", "0d3")
    send("0D4", "0a4")
    send("0V2")
    send("0b4", "0c4")
    send("0d4")
    send("0I4")
    send("0V3")
    for l in (1, 0):
        for c in range(PARTS):
            reduce[l][c].step5()
            reduce[l][c].finish()
    act_mine.wait()
    act_theirs.wait_send()
    remote(hid.at[2 - s], act_out.at[1 - s], ex_send.at[0], ex_recv.at[0], me.sibling()).wait_recv()
    grad_mine.wait()
    grad_theirs.wait_send()
    remote(grad.at[1 - s], ig_out.at[1 - s], ex_send.at[1], ex_recv.at[1], me.sibling()).wait_recv()


def scratch_shapes():
    def parts(lead, kind=None):
        return [pltpu.VMEM((PAIRS, *lead, HALF_ROWS[0], WIDTH[0]), kind or BF)] + [
            pltpu.VMEM((*lead, HALF_ROWS[c], WIDTH[c]), kind or KIND[c]) for c in range(PAIRS, PARTS)
        ]

    shapes = []
    for _ in (0, 1):
        shapes += parts((2, 16))
    for lead in ((2, 16), (16,), (16,), (3, 4), (3, 4), (3,), (3,), (4,), (4,)):
        shapes += parts(lead)[:-1]
    shapes += parts((), F32)[:-1]
    for lead in ((4, 4), (4, 4), (4, 4), (16,), (16,), (4,), (4,)):
        shapes.append(pltpu.VMEM((*lead, 16, 128), F32))
    shapes += [pltpu.VMEM((2, 8, 128), F32), pltpu.VMEM((8, 384), F32)]
    shapes += [
        pltpu.VMEM((3, T, D), BF),
        pltpu.VMEM((2, T, D), BF),
        pltpu.VMEM((D, T), BF),
        pltpu.VMEM((T, D), BF),
        pltpu.VMEM((T, D), F32),
        pltpu.VMEM((T, D), BF),
    ]
    shapes += [pltpu.VMEM(shape, kind) for shape, kind in KEPT]
    shapes += [
        pltpu.VMEM((TILE, 768), BF),
        pltpu.VMEM((TILE, 512), BF),
        pltpu.VMEM((TILE, 256), BF),
        pltpu.VMEM((T, D), BF),
    ]
    shapes += [
        pltpu.VMEM((8, D), F32),
        pltpu.VMEM((16, 128), F32),
        pltpu.VMEM((8, 512), F32),
        pltpu.VMEM((8, D), F32),
        pltpu.VMEM((8, 512), F32),
        pltpu.VMEM((T, 1), F32),
        pltpu.VMEM((6, TILE, TILE), F32),
        pltpu.VMEM((8, T), F32),
        pltpu.VMEM((8, T), F32),
    ]
    dma = pltpu.SemaphoreType.DMA
    shapes += [dma((2, PARTS, 5))] * 3
    shapes += [dma((PARTS,)), dma((12,)), dma((2,)), dma((2,))]
    return shapes


KEPT = (
    ((3 * D, T), BF),
    ((HEADS, TILE, 768), BF),
    ((HEADS, TILE, 512), BF),
    ((HEADS, TILE, 256), BF),
    ((D, T), BF),
    ((HEADS, T), F32),
    ((T, FF), BF),
    ((T, FF), BF),
)


def body(
    inputs,
    cotangent,
    lengths,
    norm1_gain,
    norm1_bias,
    qkv_weight,
    qkv_bias,
    dense_weight,
    norm2_gain,
    norm2_bias,
    fc_in_weight,
    fc_in_bias,
    fc_out_weight,
    out_bias,
):
    hbm = pl.BlockSpec(memory_space=pl.ANY)
    vmem = pl.BlockSpec(memory_space=pltpu.VMEM)
    shape = jax.ShapeDtypeStruct
    results = pl.pallas_call(
        kernel,
        out_shape=[shape((2, T, D), BF), shape((2, T, D), BF), shape((PAIRS, 2, 16, 384), F32)]
        + [shape((2, HALF_ROWS[c], WIDTH[c]), F32) for c in range(PAIRS, VEC)]
        + [shape((16, 128), F32)]
        + [shape(s, k) for s, k in KEPT],
        in_specs=[pl.BlockSpec(memory_space=pltpu.SMEM)] + [hbm] * 6 + [vmem] * 7,
        out_specs=[hbm] * 2 + [vmem] * 5 + [hbm] * len(KEPT),
        scratch_shapes=scratch_shapes(),
        compiler_params=pltpu.CompilerParams(
            collective_id=0, has_side_effects=True, vmem_limit_bytes=64 * 1024 * 1024
        ),
        name="layers",
    )(
        lengths,
        inputs,
        cotangent,
        qkv_weight,
        dense_weight,
        fc_in_weight,
        fc_out_weight,
        norm1_gain,
        norm1_bias,
        norm2_gain,
        norm2_bias,
        out_bias,
        qkv_bias,
        fc_in_bias,
    )
    vector, slab = shape((1, 32), F32), shape((1, 2, T, D), BF)
    return pl.pallas_call(
        hand_out,
        out_shape=[slab, slab, vector, vector, shape((1, 32, 1536), F32), shape((1, 96), F32)]
        + [shape((1, 32, 512), F32), vector, vector, shape((1, 32, 2048), F32), shape((1, 128), F32)]
        + [shape((1, 128, 512), F32), vector],
        in_specs=[hbm] * 7,
        out_specs=[hbm] * 2 + [vmem] * 11,
        scratch_shapes=[pltpu.VMEM((4, T, D), BF)]
        + [pltpu.VMEM(r.shape, r.dtype) for r in results[2:7]]
        + [pltpu.SemaphoreType.DMA((9,)), pltpu.SemaphoreType.DMA((4,))],
        compiler_params=pltpu.CompilerParams(vmem_limit_bytes=60 * 1024 * 1024),
        name="hand_out",
    )(*results[:7])


def hand_out(
    act, ig, hq, hd, hi, ho, hv, o_act, o_ig, o_g1, o_b1, o_qkv, o_qkvb, o_d, o_g2, o_b2, o_in, o_inb, o_out, o_last, held, gq, gd, gi, go, gv, arrive, leave
):
    z = lax.axis_index("shard") % 4
    pieces = [(act.at[m], o_act.at[0, m]) for m in (0, 1)] + [(ig.at[m], o_ig.at[0, m]) for m in (0, 1)]
    coming = [pltpu.make_async_copy(src, held.at[k], arrive.at[k]) for k, (src, _) in enumerate(pieces)]
    going = [pltpu.make_async_copy(held.at[k], dst, leave.at[k]) for k, (_, dst) in enumerate(pieces)]
    small = [
        pltpu.make_async_copy(src, dst, arrive.at[4 + k])
        for k, (src, dst) in enumerate(((hq, gq), (hd, gd), (hi, gi), (ho, go), (hv, gv)))
    ]
    for copy in coming + small:
        copy.start()
    for copy, after in zip(coming, going):
        copy.wait()
        after.start()
    for copy in small:
        copy.wait()
    for half in (0, 1):
        rows = slice(16 * half, 16 * half + 16)
        for hp in range(PAIRS):
            for which in range(3):
                column = 512 * which + 128 * hp
                o_qkv[0, rows, column : column + 128] = gq[hp, half, :, 128 * which : 128 * which + 128]
        o_d[0, rows, :] = gd[half]
        o_in[0, rows, :] = gi[half]
        o_out[0, 64 * half : 64 * half + 64, :] = go[half]

    def own(row, width):
        total = jnp.zeros((1, width), F32)
        for k in range(4):
            total = total + jnp.where(z == k, row[:, width * k : width * k + width], 0.0)
        return total

    for row, ref in enumerate((o_g1, o_b1, o_g2, o_b2, o_last)):
        ref[...] = own(gv[row : row + 1, :], 32)
    o_qkvb[...] = own(jnp.concatenate([gv[8 + k : 9 + k, :] for k in range(3)], axis=1), 96)
    o_inb[...] = gv[11:12, :]
    for copy in going:
        copy.wait()


def solution(mesh):
    rows = P(None, ("replica", "shard"), None)
    vector, matrix = P("section", "shard"), P("section", "shard", None)
    slabs = P("section", None, ("replica", "shard"), None)
    return jax.shard_map(
        body,
        mesh=mesh,
        in_specs=(
            rows, rows, rows, vector, vector, matrix, vector, matrix, vector, vector, matrix, vector, matrix, vector,
        ),
        out_specs=(
            slabs, slabs, vector, vector, matrix, vector, matrix, vector, vector, matrix, vector, matrix, vector,
        ),
        check_vma=False,
    )
```

```python
import math

import jax
import jax.numpy as jnp
from jax import lax
from jax.experimental import pallas as pl
from jax.experimental.pallas import tpu as pltpu
from jax.sharding import PartitionSpec as P

T = 768
D = 512
FF = 2048
HEADS = 8
HEAD = 64
ROT = 16
BLOCK = 128
SEQS = 4
TILE = 256
EPS = 1e-5
MASKED = -1e9
LOG2E = 1.0 / math.log(2.0)
LN2 = math.log(2.0)
MESH = pl.DeviceIdType.MESH
BF = jnp.bfloat16
F32 = jnp.float32

PAIRS = 4
DENSE, FIN, FOUT, VEC = 4, 5, 6, 7
PARTS = 8
LETTERS = "abcdDIOV"
HALF_ROWS = (16, 16, 16, 16, 16, 16, 64, 8)
WIDTH = (384, 384, 384, 384, 512, 2048, 512, 128)
KIND = (BF, BF, BF, BF, BF, BF, BF, F32)


def dg(a, b, ca, cb):
    return lax.dot_general(a, b, (((ca,), (cb,)), ((), ())), preferred_element_type=F32)


class Place:
    def __init__(self):
        self.s = lax.axis_index("section")
        self.y = lax.axis_index("replica")
        shard = lax.axis_index("shard")
        x, z = shard // 4, shard % 4
        self.shard, self.x, self.z = shard, x, z
        self.p = x + self.s * (z - x)
        self.q = z + self.s * (x - z)

    def at(self, p, q):
        return (1 - self.s) * (4 * p + q) + self.s * (4 * q + p)

    def sibling(self):
        return (1 - self.s, self.y, self.shard)

    def along_p(self, d):
        return (self.s, self.y, self.at((self.p + d) % 4, self.q))

    def along_q(self, d):
        return (self.s, self.y, self.at(self.p, (self.q + d) % 4))

    def along_y(self, d):
        return (self.s, (self.y + d) % 4, self.shard)


def remote(src, dst, send, recv, device):
    return pltpu.make_async_remote_copy(
        src_ref=src, dst_ref=dst, send_sem=send, recv_sem=recv, device_id=device, device_id_type=MESH
    )


class Gather:
    def __init__(self, me, layer, part, shard_ref, whole, send, recv, local):
        self.me, self.layer, self.part = me, layer, part
        self.shard_ref, self.w = shard_ref, whole
        self.send = lambda k: send.at[layer, part, k]
        self.recv = lambda k: recv.at[layer, part, k]
        self.local = local.at[part]
        self.rows = HALF_ROWS[part]
        self.direct = layer == 0 and part in (0, 1, 2, 3, VEC)
        self.ways = (1, 3, 2) if self.direct else (1, 3)

    def halves(self, h, target):
        if self.part == VEC:
            return [(self.shard_ref.at[h], target)]
        rows = pl.ds(pl.multiple_of(h * self.rows, self.rows), self.rows)
        if self.part < PAIRS:
            return [
                (
                    self.shard_ref.at[0, rows, pl.ds(512 * which + 128 * self.part, 128)],
                    target.at[:, pl.ds(128 * which, 128)],
                )
                for which in range(3)
            ]
        return [(self.shard_ref.at[0, rows, :], target)]

    def move(self, ref, sent, came, device):
        return remote(ref, ref, self.send(sent), self.recv(came), device)

    def shards(self, count):
        return self.move(self.w.at[self.me.s, pl.ds(0, count)], 1, 1, self.me.sibling())

    def row(self, half, p):
        return self.w.at[half, pl.ds(4 * p, 4)]

    def own(self, half, p, q):
        return self.w.at[half, 4 * p + q]

    def step0(self):
        me = self.me

        @pl.when(me.s == self.layer)
        def _():
            for src, dst in self.halves(me.s, self.own(me.s, me.p, me.q)):
                pltpu.make_async_copy(src, dst, self.local).start()
            for src, dst in self.halves(1 - me.s, self.own(1 - me.s, me.q, me.p)):
                remote(src, dst, self.send(0), self.recv(0), me.sibling()).start()

    def step1(self):
        me = self.me
        own = self.own(me.s, me.p, me.q)

        @pl.when(me.s == self.layer)
        def _():
            pltpu.make_async_copy(own, own, self.local).wait()

        @pl.when(me.s != self.layer)
        def _():
            self.move(own, 0, 0, me.sibling()).wait_recv()

        for d in (1, 3, 2):
            self.move(own, 1, 1, me.along_q(d)).start()

    def across(self, p):
        self.move(self.row(self.me.s, p), 2, 4, self.me.sibling()).start()

    def step2(self):
        me = self.me
        self.shards(3).wait_recv()
        for d in self.ways:
            self.move(self.row(me.s, me.p), 1, 2, me.along_p(d)).start()
        self.across(me.p)

    def step3(self):
        me = self.me
        ref = self.w.at[me.s, pl.ds(0, 4 * len(self.ways))]
        self.move(ref, 1, 2, me.sibling()).wait_recv()
        if not self.direct:
            for d in (1, 3):
                half = self.w.at[me.s, pl.ds(4 * ((me.p + 4 - d) % 4) + d - 1, 2)]
                self.move(half, 1, 3, me.along_p(d)).start()
        for d in self.ways:
            self.across((me.p + 4 - d) % 4)

    def step4(self):
        me = self.me
        if not self.direct:
            self.move(self.row(me.s, me.p), 1, 3, me.sibling()).wait_recv()
            self.across((me.p + 2) % 4)

    def step5(self):
        self.move(self.w.at[1 - self.me.s], 2, 4, self.me.sibling()).wait_recv()

    def finish(self):
        me = self.me

        @pl.when(me.s == self.layer)
        def _():
            self.move(self.own(1 - me.s, me.q, me.p), 0, 0, me.sibling()).wait_send()

        self.shards(15).wait_send()
        self.move(self.w.at[me.s], 2, 4, me.sibling()).wait_send()


class Reduce:
    def __init__(self, me, layer, part, terms, buffers, send, recv):
        self.me, self.layer, self.part = me, layer, part
        self.g = terms
        self.r, self.one, self.two, self.ys, self.f, self.out = buffers
        self.send = lambda k: send.at[layer, part, k]
        self.recv = lambda k: recv.at[layer, part, k]
        self.kind = KIND[part]

    def swap(self):
        me = self.me
        return remote(self.g.at[1 - me.s], self.r, self.send(0), self.recv(0), me.sibling())

    def first(self, d):
        me = self.me
        row = self.r.at[pl.ds(4 * ((me.p + d) % 4), 4)]
        return remote(row, self.one.at[d - 1], self.send(1), self.recv(1), me.along_p(d))

    def second(self, d):
        me = self.me
        shard = self.r.at[4 * me.p + (me.q + d) % 4]
        return remote(shard, self.two.at[d - 1], self.send(2), self.recv(2), me.along_q(d))

    def third(self, d):
        me = self.me
        return remote(self.ys.at[me.y], self.ys.at[me.y], self.send(3), self.recv(3), me.along_y(d))

    def all_of(self, ref, k):
        return remote(ref, ref, self.send(k), self.recv(k), self.me.sibling())

    def back(self):
        me = self.me
        return remote(self.f, self.out.at[me.s], self.send(4), self.recv(4), me.sibling())

    def step0(self):
        self.swap().start()

    def step1(self):
        me = self.me
        self.swap().wait_recv()

        def one(k, c):
            self.r[k] = (self.r[k].astype(F32) + self.g[me.s, k].astype(F32)).astype(self.kind)
            return c

        lax.fori_loop(0, 16, one, 0)
        for d in (1, 3, 2):
            self.first(d).start()
        self.swap().wait_send()

    def step2(self):
        me = self.me
        self.all_of(self.one, 1).wait_recv()

        def one(b, c):
            total = self.r[4 * me.p + b].astype(F32) + self.one[0, b].astype(F32)
            total = total + (self.one[1, b].astype(F32) + self.one[2, b].astype(F32))
            self.r[4 * me.p + b] = total.astype(self.kind)
            return c

        lax.fori_loop(0, 4, one, 0)
        for d in (1, 3, 2):
            self.second(d).start()

    def step3(self):
        me = self.me
        self.all_of(self.two, 2).wait_recv()
        total = self.r[4 * me.p + me.q].astype(F32) + self.two[0].astype(F32)
        total = total + (self.two[1].astype(F32) + self.two[2].astype(F32))
        self.ys[me.y] = total.astype(self.kind)
        for d in (1, 3, 2):
            self.third(d).start()

    def step4(self):
        me = self.me
        self.all_of(self.ys.at[pl.ds(0, 3)], 3).wait_recv()
        total = (self.ys[0].astype(F32) + self.ys[1].astype(F32)) + (
            self.ys[2].astype(F32) + self.ys[3].astype(F32)
        )

        @pl.when(me.s == self.layer)
        def _():
            self.out[me.s] = total

        @pl.when(me.s != self.layer)
        def _():
            self.f[...] = total
            self.back().start()

    def step5(self):
        me = self.me

        @pl.when(me.s == self.layer)
        def _():
            self.all_of(self.out.at[1 - me.s], 4).wait_recv()

    def finish(self):
        self.all_of(self.one, 1).wait_send()
        self.all_of(self.two, 2).wait_send()
        self.all_of(self.ys.at[pl.ds(0, 3)], 3).wait_send()

        @pl.when(self.me.s != self.layer)
        def _():
            self.back().wait_send()


class ReduceVectors:
    def __init__(self, me, layer, terms, buffers, send, recv):
        self.me, self.layer, self.g = me, layer, terms
        self.r, self.one, self.ys, self.out = buffers
        self.send = lambda k: send.at[layer, VEC, k]
        self.recv = lambda k: recv.at[layer, VEC, k]

    def swap(self):
        return remote(self.g, self.r, self.send(0), self.recv(0), self.me.sibling())

    def first(self, k):
        x, z = (self.me.x + k // 4) % 4, (self.me.z + k % 4) % 4
        device = (self.me.s, self.me.y, 4 * x + z)
        return remote(self.r.at[x, z], self.one.at[k], self.send(1), self.recv(1), device)

    def all_first(self):
        ref = self.one.at[pl.ds(1, 15)]
        return remote(ref, ref, self.send(1), self.recv(1), self.me.sibling())

    def third(self, d):
        me = self.me
        return remote(self.ys.at[me.y], self.ys.at[me.y], self.send(3), self.recv(3), me.along_y(d))

    def all_third(self):
        ref = self.ys.at[pl.ds(0, 3)]
        return remote(ref, ref, self.send(3), self.recv(3), self.me.sibling())

    def owner(self, step):
        pl.when(self.me.s == self.layer)(step)

    def step0(self):
        @pl.when(self.me.s != self.layer)
        def _():
            self.swap().start()

    def step1(self):
        def step():
            self.swap().wait_recv()
            self.r[...] += self.g[...]
            for k in (1, 4, 3, 12, 5, 7, 13, 15, 2, 8, 6, 9, 11, 14, 10):
                self.first(k).start()

        self.owner(step)

        @pl.when(self.me.s != self.layer)
        def _():
            self.swap().wait_send()

    def step2(self):
        def step():
            self.all_first().wait_recv()
            total = self.r[self.me.x, self.me.z]
            for k in range(1, 16):
                total = total + self.one[k]
            self.ys[self.me.y] = total
            for d in (1, 3, 2):
                self.third(d).start()

        self.owner(step)

    def step3(self):
        def step():
            self.all_third().wait_recv()
            self.out[...] = (self.ys[0] + self.ys[1]) + (self.ys[2] + self.ys[3])

        self.owner(step)

    def step5(self):
        pass

    def finish(self):
        def step():
            self.all_first().wait_send()
            self.all_third().wait_send()

        self.owner(step)


def natural_rows(ref, columns):
    pieces = []
    for x in range(4):
        for z in range(4):
            pieces.append(ref[0, 4 * x + z, :, columns])
            pieces.append(ref[1, 4 * z + x, :, columns])
    return jnp.concatenate(pieces, axis=0)


def group_rows(ref, x):
    pieces = []
    for z in range(4):
        pieces.append(ref[0, 4 * x + z])
        pieces.append(ref[1, 4 * z + x])
    return jnp.concatenate(pieces, axis=0)


def put_natural(ref, columns, value):
    for x in range(4):
        for z in range(4):
            row = 32 * (4 * x + z)
            ref[0, 4 * x + z, :, columns] = value[row : row + 16]
            ref[1, 4 * z + x, :, columns] = value[row + 16 : row + 32]


def put_group(ref, x, value, rows):
    for z in range(4):
        row = 2 * rows * z
        ref[0, 4 * x + z] = value[row : row + rows]
        ref[1, 4 * z + x] = value[row + rows : row + 2 * rows]


def to_column(row):
    here = lax.broadcasted_iota(jnp.int32, (128, 128), 0) == lax.broadcasted_iota(
        jnp.int32, (128, 128), 1
    )
    return jnp.sum(jnp.where(here, row, 0.0), axis=1, keepdims=True)


def turn(rows, cosine, sine):
    pieces = []
    for e in (0, 64):
        low, high = rows[e : e + 8], rows[e + 8 : e + 16]
        pieces += [low * cosine - high * sine, high * cosine + low * sine, rows[e + 16 : e + 64]]
    return jnp.concatenate(pieces, axis=0)


def columns(start, size):
    return pl.ds(pl.multiple_of(start, size), size)


def loop(count, step):
    def one(k, c):
        step(k)
        return c

    lax.fori_loop(0, count, one, 0)


def kernel(
    lengths,
    x_ref,
    cot_ref,
    wq_ref,
    wd_ref,
    wi_ref,
    wo_ref,
    gain1_ref,
    shift1_ref,
    gain2_ref,
    shift2_ref,
    last_ref,
    qkvb_ref,
    finb_ref,
    act_out,
    ig_out,
    gq_out,
    gd_out,
    gi_out,
    go_out,
    gv_out,
    st_qkv,
    st_p0,
    st_p1,
    st_p2,
    st_bt,
    st_rinv,
    st_act,
    st_slo,
    *scratch,
):
    scratch = list(scratch)

    def take(count):
        taken, scratch[:count] = scratch[:count], []
        return taken

    def take_parts(count=4):
        pairs, *rest = take(count)
        return [pairs] + [pairs.at[k] for k in range(PAIRS)] + rest

    (wq0, *w0), (wq1, *w1) = take_parts(5), take_parts(5)
    w, wq = (w0, w1), (wq0, wq1)
    gq, *g = take_parts()
    r, one, two, ys = [(take_parts()[1:], take_parts()[1:]) for _ in range(4)]
    f = take_parts()[1:]
    gvec, *rvec = take(3)
    vecs, yvec, (vsrc, vrow) = take(2), take(2), take(2)
    hid, grad, n1t, n2, acc, carried = take(6)
    qkvt, p0, p1, p2, bt, rinv, act, slo = take(8)
    d0, d1, d2, scores_one = take(4)
    dn1 = n2
    vd, vq, vf, dvec, fvec, live, bias, cos_ref, sin_ref = take(9)
    sends, ag_recv, rs_recv, ag_local, sems, ex_send, ex_recv = take(7)
    probs = (p0, p1, p2)
    dscores = (d0, d1, d2)
    outs = [gq_out.at[k] for k in range(PAIRS)] + [gd_out, gi_out, go_out]
    shards = [wq_ref] * PAIRS + [wd_ref, wi_ref, wo_ref, vsrc]

    me = Place()
    s = me.s
    barrier = pltpu.get_barrier_semaphore()
    partners = [me.sibling()]
    for d in (1, 2, 3):
        partners += [me.along_q(d), me.along_p(d), me.along_y(d)]
        for e in (1, 2, 3):
            partners.append((s, me.y, 4 * ((me.x + d) % 4) + (me.z + e) % 4))
    for device in partners:
        pl.semaphore_signal(barrier, inc=1, device_id=device, device_id_type=MESH)
    pl.semaphore_wait(barrier, len(partners))

    gather = [
        [Gather(me, l, c, shards[c], w[l][c], sends, ag_recv, ag_local) for c in range(PARTS)]
        for l in (0, 1)
    ]
    reduce = [
        [
            Reduce(
                me, l, c, g[c], (r[l][c], one[l][c], two[l][c], ys[l][c], f[c], outs[c]), sends, rs_recv
            )
            for c in range(VEC)
        ]
        + [ReduceVectors(me, l, gvec, (rvec[l], vecs[l], yvec[l], gv_out), sends, rs_recv)]
        for l in (0, 1)
    ]

    def fetch(*plan):
        for word in plan:
            item = gather[int(word[0])][LETTERS.index(word[1])]
            getattr(item, "step" + word[2])()

    def send(*plan):
        for word in plan:
            item = reduce[int(word[0])][LETTERS.index(word[1])]
            getattr(item, "step" + word[2])()

    vsrc[...] = jnp.zeros((2, 8, 128), F32)
    for k in range(4):
        here = me.z == k
        for row, ref in enumerate((gain1_ref, shift1_ref, gain2_ref, shift2_ref, last_ref)):
            vsrc[0, row : row + 1, 32 * k : 32 * k + 32] = jnp.where(here, ref[...].astype(F32), 0.0)
        vrow[0:1, 96 * k : 96 * k + 96] = jnp.where(here, qkvb_ref[...].astype(F32), 0.0)
    for k in range(3):
        vsrc[1, k : k + 1, :] = vrow[0:1, 128 * k : 128 * k + 128]
    vsrc[1, 3:4, :] = finb_ref[...].astype(F32)

    x_in = pltpu.make_async_copy(x_ref.at[s], hid.at[0], sems.at[0])
    cot_in = pltpu.make_async_copy(cot_ref.at[s], grad.at[0], sems.at[1])
    x_in.start()
    fetch("0V0", "0a0", "0b0", "0c0", "0d0", "0I0", "0D0", "0O0", "1V0", "1a0", "1b0", "1c0", "1d0", "1I0", "1D0", "1O0")
    fetch("0V1", "0a1", "0b1", "0c1", "0d1", "0D1", "0I1", "0O1")
    cot_in.start()

    starts, ends, at = [], [], jnp.int32(0)
    for k in range(SEQS):
        size = lengths[s, 0, k]
        starts.append(at)
        ends.append(at + size)
        at = at + (size + BLOCK - 1) // BLOCK * BLOCK

    def inside(places):
        return [(places >= a) & (places < b) for a, b in zip(starts, ends)]

    def live_tile(k):
        places = lax.broadcasted_iota(jnp.int32, (TILE, 1), 0) + k * TILE
        total = jnp.zeros((TILE, 1), F32)
        for found in inside(places):
            total = total + jnp.where(found, 1.0, 0.0)
        live[columns(k * TILE, TILE), :] = total

    loop(3, live_tile)
    places = lax.broadcasted_iota(jnp.int32, (8, T), 1)
    begin = jnp.zeros((8, T), jnp.int32)
    offset = jnp.zeros((8, T), jnp.int32)
    for found, a in zip(inside(places), starts):
        begin = begin + jnp.where(found, a, 0)
        offset = offset + jnp.where(found, places - a, 0)
    rates = jnp.exp(
        lax.broadcasted_iota(jnp.int32, (8, T), 0).astype(F32) * (-2.0 * math.log(10000.0) / ROT)
    )
    angles = offset.astype(F32) * rates
    cos_ref[...] = jnp.cos(angles)
    sin_ref[...] = jnp.sin(angles)
    for j in range(3):
        for i in range(j + 1):
            keys = lax.broadcasted_iota(jnp.int32, (TILE, TILE), 0) + i * TILE
            queries = lax.broadcasted_iota(jnp.int32, (TILE, TILE), 1) + j * TILE
            fits = (keys >= begin[0:1, j * TILE : (j + 1) * TILE]) & (keys <= queries)
            bias[j * (j + 1) // 2 + i] = jnp.where(fits, 0.0, MASKED)

    def unpack(l):
        ref = w[l][VEC]
        for x in range(4):
            vd[:, 128 * x : 128 * x + 128] = (ref[0, 4 * x] + ref[0, 4 * x + 1]) + (
                ref[0, 4 * x + 2] + ref[0, 4 * x + 3]
            )
            group = (ref[1, x] + ref[1, 4 + x]) + (ref[1, 8 + x] + ref[1, 12 + x])
            for k in range(3):
                vq[3 * x + k : 3 * x + k + 1, :] = group[k : k + 1]
            for z in range(4):
                vf[x : x + 1, 128 * z : 128 * z + 128] = ref[1, 4 * z + x][3:4]

    def normed(l, rows):
        v = hid[l, rows, :].astype(F32)
        centred = v - jnp.mean(v, axis=1, keepdims=True)
        scale = lax.rsqrt(jnp.mean(centred * centred, axis=1, keepdims=True) + EPS)
        return centred * scale, scale

    def norms(l):
        def tile(k):
            rows = columns(k * TILE, TILE)
            u, _ = normed(l, rows)
            n1t[:, rows] = (u * vd[0:1, :] + vd[1:2, :]).astype(BF).T
            n2[rows, :] = (u * vd[2:3, :] + vd[3:4, :]).astype(BF)

        loop(3, tile)

    def project(l, hp):
        value = dg(natural_rows(wq[l].at[hp], slice(0, 384)), n1t[...], 0, 0)
        pair = []
        for which in range(3):
            part = value[128 * which : 128 * which + 128] + to_column(vq[pl.ds(which * 4 + hp, 1), :])
            if which < 2:
                part = turn(part, cos_ref[...], sin_ref[...])
            if which == 0:
                part = part * (LOG2E / 8.0)
            pair.append(part.astype(BF))
            qkvt[columns(hp * 384 + which * 128, 128), :] = pair[which]
        return pair

    def score_block(e, k):
        if e:
            return scores_one.at[k]
        return acc.at[pl.ds(TILE * (k // 2), TILE), pl.ds(TILE * (k % 2), TILE)]

    def attend(l, hp):
        pair = project(l, hp)
        keys = pair[1].T
        blank = jnp.zeros((HEAD, T), BF)
        peaks = ([None] * 3, [None] * 3)
        for e in (0, 1):
            mine = pair[0][e * HEAD : (e + 1) * HEAD]
            mine = jnp.concatenate([mine, blank] if e == 0 else [blank, mine], axis=0)
            for i in range(3):
                for j in range(i, 3):
                    k = j * (j + 1) // 2 + i
                    scores = dg(keys[i * TILE : (i + 1) * TILE], mine[:, j * TILE : (j + 1) * TILE], 1, 0)
                    scores = scores + bias[k]
                    score_block(e, k)[...] = scores
                    peak = jnp.max(scores, axis=0, keepdims=True)
                    peaks[e][j] = peak if i == 0 else jnp.maximum(peaks[e][j], peak)
        for e in (0, 1):
            h = 2 * hp + e
            value = jnp.concatenate([pair[2][e * HEAD : (e + 1) * HEAD], jnp.ones((8, T), BF)], axis=0)
            for j in range(3):
                at_j = slice(j * TILE, (j + 1) * TILE)
                blended = jnp.zeros((HEAD + 8, TILE), F32)
                for i in range(j + 1):
                    raised = jnp.exp2(score_block(e, j * (j + 1) // 2 + i)[...] - peaks[e][j]).astype(BF)
                    probs[i][h, :, (j - i) * TILE : (j - i + 1) * TILE] = raised
                    blended = blended + dg(value[:, i * TILE : (i + 1) * TILE], raised, 1, 0)
                inverse = 1.0 / blended[HEAD : HEAD + 1]
                rinv[pl.ds(h, 1), at_j] = inverse
                bt[columns(hp * 128 + e * HEAD, HEAD), at_j] = (blended[:HEAD] * inverse).astype(BF)

    def widen(l, c):
        cols = columns(c * 512, 512)
        weight = natural_rows(w[l][FIN], cols)
        shift = vf[pl.ds(c, 1), :]

        def tile(k):
            rows = columns(k * TILE, TILE)
            v = dg(n2[rows, :], weight, 1, 0) + shift
            below = 0.5 + 0.5 * lax.erf(v * (1.0 / math.sqrt(2.0)))
            act[rows, cols] = (v * below).astype(BF)
            slope = below + v * (jnp.exp(-0.5 * v * v) * (1.0 / math.sqrt(2.0 * math.pi)))
            slo[rows, cols] = slope.astype(BF)

        for k in range(3):
            tile(k)

    def join(l):
        def part(t):
            cols = columns(t * TILE, TILE)
            weight = jnp.concatenate(
                [
                    piece
                    for x in range(4)
                    for z in range(4)
                    for piece in (w[l][FOUT][0, 4 * x + z, :, cols], w[l][FOUT][1, 4 * z + x, :, cols])
                ],
                axis=0,
            )
            total = dg(act[...], weight, 1, 0)
            total = total + dg(bt[...], natural_rows(w[l][DENSE], cols), 0, 0)
            total = total + hid[l, :, cols].astype(F32) + vd[4:5, cols]
            hid[l + 1, :, cols] = (total * live[...]).astype(BF)

        loop(2, part)

    def local(src, dst, k):
        return pltpu.make_async_copy(src, dst, sems.at[k])

    attention_kept = [
        (qkvt, st_qkv, 2),
        (p0, st_p0, 3),
        (p1, st_p1, 4),
        (p2, st_p2, 5),
        (bt, st_bt, 6),
        (rinv, st_rinv, 7),
    ]
    wide_kept = [(act, st_act, 8), (slo, st_slo, 9)]

    fetch("0V2", "0a2", "0b2", "0c2", "0d2")
    x_in.wait()
    fetch("0V3", "0a3")
    fetch("0D2", "0I2")
    fetch("0V5")
    unpack(0)
    norms(0)
    fetch("0b3", "0O2", "0a5")
    attend(0, 0)
    fetch("0c3", "0b5")
    attend(0, 1)
    fetch("0d3", "0D3", "0I3", "0c5")
    fetch("1V1", "1a1", "1b1", "1c1", "1d1")
    attend(0, 2)
    fetch("0O3", "0d5")
    fetch("1I1", "1D1", "1O1")
    attend(0, 3)
    for a, b, k in attention_kept:
        local(a, b, k).start()
    fetch("0D4", "0I4", "1V2", "1a2", "1b2")
    fetch("0I5")
    loop(2, lambda c: widen(0, c))
    fetch("0O4")
    fetch("1c2", "1d2", "1V3", "1a3")
    loop(2, lambda c: widen(0, c + 2))
    fetch("1b3", "1c3", "1d3", "1I2", "1D2", "1O2", "0D5", "0O5")
    join(0)
    for a, b, k in wide_kept:
        local(a, b, k).start()

    fetch("1V4", "1a4", "1b4")
    fetch("1V5")
    unpack(1)
    norms(1)
    fetch("1c4", "1d4", "1a5")
    for a, b, k in attention_kept:
        local(a, b, k).wait()
    attend(1, 0)
    fetch("1I3", "1D3", "1b5")
    attend(1, 1)
    fetch("1O3", "1c5")
    attend(1, 2)
    fetch("1I4", "1D4", "1d5")
    attend(1, 3)
    fetch("1O4", "1I5")
    for a, b, k in wide_kept:
        local(a, b, k).wait()
    loop(4, lambda c: widen(1, c))
    fetch("1D5", "1O5")
    join(1)
    for l in (0, 1):
        for c in range(PARTS):
            gather[l][c].finish()
    act_mine = local(hid.at[1 + s], act_out.at[s], 10)
    act_theirs = remote(hid.at[2 - s], act_out.at[s], ex_send.at[0], ex_recv.at[0], me.sibling())
    act_mine.start()
    act_theirs.start()
    cot_in.wait()

    def start_back(l):
        def tile(k):
            rows = columns(k * TILE, TILE)
            v = grad[1 - l, rows, :].astype(F32) * live[rows, :]
            carried[rows, :] = v.astype(BF)
            here = jnp.sum(v, axis=0, keepdims=True)
            dvec[4:5, :] = here + jnp.where(k == 0, 0.0, dvec[4:5, :])

        dvec[...] = jnp.zeros((8, D), F32)
        loop(3, tile)

    def back_out(c):
        cols = columns(c * 512, 512)
        put_group(g[FOUT], c, dg(act[:, cols], carried[...], 0, 0).astype(BF), 64)

    def back_wide(l, c):
        cols = columns(c * 512, 512)
        weight = group_rows(w[l][FOUT], c)
        total = jnp.zeros((1, 512), F32)
        for k in range(3):
            rows = slice(k * TILE, (k + 1) * TILE)
            v = dg(carried[rows, :], weight, 1, 1) * slo[rows, cols].astype(F32)
            v = v.astype(BF)
            slo[rows, cols] = v
            total = total + jnp.sum(v.astype(F32), axis=0, keepdims=True)
        fvec[pl.ds(c, 1), :] = total

    def back_in(l, c):
        cols = columns(c * 512, 512)
        put_natural(g[FIN], cols, dg(n2[...], slo[:, cols], 0, 0).astype(BF))

    def back_norm_two(l, t):
        low = w[l][FIN][0, pl.ds(8 * t, 8)]
        high = [w[l][FIN][1, pl.ds(4 * z + 2 * t, 2)] for z in range(4)]
        pieces = []
        for x in range(2):
            for z in range(4):
                pieces += [low[4 * x + z], high[z][x]]
        acc[:, columns(t * TILE, TILE)] = dg(slo[...], jnp.concatenate(pieces, axis=0), 1, 1)

    def back_dense(l):
        put_natural(g[DENSE], slice(0, 512), dg(bt[...], carried[...], 1, 0).astype(BF))

    def back_attend(l, hp):
        weight = group_rows(w[l][DENSE], hp)
        below = dg(weight, carried[...], 1, 1)
        queries = qkvt[columns(hp * 384, 128), :]
        keys = qkvt[columns(hp * 384 + 128, 128), :]
        values = qkvt[columns(hp * 384 + 256, 128), :].T
        blended = bt[columns(hp * 128, 128), :].astype(F32)
        blank = jnp.zeros((HEAD, TILE), BF)
        downs = []
        for e in (0, 1):
            h = 2 * hp + e
            down = below[e * HEAD : (e + 1) * HEAD] * rinv[pl.ds(h, 1), :]
            centre = jnp.sum(down * blended[e * HEAD : (e + 1) * HEAD], axis=0, keepdims=True)
            down = down.astype(BF)
            downs.append(down)
            for j in range(3):
                at_j = slice(j * TILE, (j + 1) * TILE)
                mine = down[:, at_j]
                mine = jnp.concatenate([mine, blank] if e == 0 else [blank, mine], axis=0)
                for i in range(j + 1):
                    cols = slice((j - i) * TILE, (j - i + 1) * TILE)
                    slope = dg(values[i * TILE : (i + 1) * TILE], mine, 1, 0) - centre[:, at_j]
                    slope = slope * probs[i][h, :, cols].astype(F32)
                    dscores[i][e, :, cols] = slope.astype(BF)
        done = []
        for e in (0, 1):
            h = 2 * hp + e
            query = queries[e * HEAD : (e + 1) * HEAD]
            key = keys[e * HEAD : (e + 1) * HEAD]
            grad_query, grad_key, grad_value = [], [], []
            for j in range(3):
                total = jnp.zeros((HEAD, TILE), F32)
                for i in range(j + 1):
                    cols = slice((j - i) * TILE, (j - i + 1) * TILE)
                    total = total + dg(key[:, i * TILE : (i + 1) * TILE], dscores[i][e, :, cols], 1, 0)
                grad_query.append(total * 0.125)
            for i in range(3):
                grad_key.append(dg(query[:, i * TILE :], dscores[i][e], 1, 1) * LN2)
                grad_value.append(dg(downs[e][:, i * TILE :], probs[i][h], 1, 1))
            done.append(
                [jnp.concatenate(pieces, axis=1) for pieces in (grad_query, grad_key, grad_value)]
            )
        for which in range(3):
            value = jnp.concatenate([done[0][which], done[1][which]], axis=0)
            if which < 2:
                value = turn(value, cos_ref[...], -sin_ref[...])
            qkvt[columns(hp * 384 + which * 128, 128), :] = value.astype(BF)

    def back_qkv(hp):
        value = dg(n1t[...], qkvt[columns(hp * 384, 384), :], 1, 1)
        put_natural(gq.at[hp], slice(0, 384), value.astype(BF))

    def back_norm_one(l, t):
        weight = jnp.concatenate([group_rows(wq[l].at[hp], t) for hp in range(PAIRS)], axis=1)
        dn1[:, columns(t * 128, 128)] = dg(weight, qkvt[...], 1, 0).astype(BF).T

    def norm_sums(l):
        def tile(k):
            rows = columns(k * TILE, TILE)
            u, _ = normed(l, rows)
            first = dn1[rows, :].astype(F32)
            second = acc[rows, :]
            dvec[0:1, :] += jnp.sum(first * u, axis=0, keepdims=True)
            dvec[1:2, :] += jnp.sum(first, axis=0, keepdims=True)
            dvec[2:3, :] += jnp.sum(second * u, axis=0, keepdims=True)
            dvec[3:4, :] += jnp.sum(second, axis=0, keepdims=True)

        loop(3, tile)

    def end_back(l):
        def tile(k):
            rows = columns(k * TILE, TILE)
            u, scale = normed(l, rows)
            first = dn1[rows, :].astype(F32)
            second = acc[rows, :]
            total = first * vd[0:1, :] + second * vd[2:3, :]
            centre = jnp.mean(total, axis=1, keepdims=True)
            along = jnp.mean(total * u, axis=1, keepdims=True)
            total = carried[rows, :].astype(F32) + scale * (total - centre - u * along)
            grad[l, rows, :] = total.astype(BF)

        loop(3, tile)

    def put_vectors(l):
        sums = dg(jnp.ones((8, T), BF), qkvt[...], 1, 1)
        for x in range(4):
            for k in range(3):
                which, hp = divmod(3 * x + k, PAIRS)
                row = 384 * hp + 128 * which
                vq[3 * x + k : 3 * x + k + 1, :] = sums[0:1, row : row + 128]
        for x in range(4):
            rest = jnp.concatenate([vq[3 * x : 3 * x + 3, :], jnp.zeros((5, 128), F32)], axis=0)
            for z in range(4):
                gvec[x, z, 0:8] = dvec[:, 128 * x : 128 * x + 128]
                gvec[x, z, 8:16] = rest
                gvec[x, z, 11:12] = fvec[x : x + 1, 128 * z : 128 * z + 128]

    restored = ((qkvt, st_qkv, 2), (p0, st_p0, 3), (p1, st_p1, 4), (p2, st_p2, 5), (bt, st_bt, 6), (rinv, st_rinv, 7))

    start_back(1)
    loop(4, back_out)
    send("1O0")
    loop(4, lambda c: back_wide(1, c))
    send("1O1")
    loop(4, lambda c: back_in(1, c))
    send("1I0")
    loop(2, lambda t: back_norm_two(1, t))
    local(st_act, act, 8).start()
    local(st_slo, slo, 9).start()
    back_dense(1)
    send("1D0", "1I1")
    back_attend(1, 0)
    back_qkv(0)
    send("1a0", "1D1")
    back_attend(1, 1)
    back_qkv(1)
    send("1b0", "1a1")
    back_attend(1, 2)
    back_qkv(2)
    send("1c0", "1b1", "1O2")
    back_attend(1, 3)
    back_qkv(3)
    send("1d0", "1c1", "1I2")
    loop(4, lambda t: back_norm_one(1, t))
    send("1d1", "1D2", "1O3")
    norm_sums(1)
    put_vectors(1)
    for a, b, k in restored:
        local(b, a, k).start()
    send("1V0", "1a2")
    end_back(1)

    unpack(0)
    norms(0)
    start_back(0)
    local(st_act, act, 8).wait()
    local(st_slo, slo, 9).wait()
    send("1b2", "1I3")
    loop(4, back_out)
    send("0O0", "1V1", "1D3", "1c2", "1d2", "1a3")
    loop(4, lambda c: back_wide(0, c))
    send("0O1", "1O4", "1b3")
    loop(4, lambda c: back_in(0, c))
    send("0I0", "1V2", "1c3", "1d3", "1D4")
    loop(2, lambda t: back_norm_two(0, t))
    send("0I1", "1I4", "1a4", "1b4")
    for a, b, k in restored:
        local(b, a, k).wait()
    back_dense(0)
    send("0D0")
    back_attend(0, 0)
    back_qkv(0)
    send("0a0", "0D1", "1V3", "1c4", "1d4")
    back_attend(0, 1)
    back_qkv(1)
    send("0b0", "0a1", "0O2")
    back_attend(0, 2)
    back_qkv(2)
    send("0c0", "0b1")
    back_attend(0, 3)
    back_qkv(3)
    send("0d0", "0c1")
    send("0D2", "0a2", "0O3")
    send("0I2")
    loop(2, lambda t: back_norm_one(0, t))
    send("0d1", "0b2")
    loop(2, lambda t: back_norm_one(0, t + 2))
    send("0c2")
    norm_sums(0)
    put_vectors(0)
    send("0V0", "0D3", "0a3", "0d2")
    send("0V1")
    send("0O4")
    send("0I3")
    end_back(0)
    grad_mine = local(grad.at[s], ig_out.at[s], 11)
    grad_theirs = remote(grad.at[1 - s], ig_out.at[s], ex_send.at[1], ex_recv.at[1], me.sibling())
    grad_mine.start()
    grad_theirs.start()
    send("0b3", "0c3", "0d3")
    send("0D4", "0a4")
    send("0V2")
    send("0b4", "0c4")
    send("0d4")
    send("0I4")
    send("0V3")
    for l in (1, 0):
        for c in range(PARTS):
            reduce[l][c].step5()
            reduce[l][c].finish()
    act_mine.wait()
    act_theirs.wait_send()
    remote(hid.at[2 - s], act_out.at[1 - s], ex_send.at[0], ex_recv.at[0], me.sibling()).wait_recv()
    grad_mine.wait()
    grad_theirs.wait_send()
    remote(grad.at[1 - s], ig_out.at[1 - s], ex_send.at[1], ex_recv.at[1], me.sibling()).wait_recv()


def scratch_shapes():
    def parts(lead, kind=None):
        return [pltpu.VMEM((PAIRS, *lead, HALF_ROWS[0], WIDTH[0]), kind or BF)] + [
            pltpu.VMEM((*lead, HALF_ROWS[c], WIDTH[c]), kind or KIND[c]) for c in range(PAIRS, PARTS)
        ]

    shapes = []
    for _ in (0, 1):
        shapes += parts((2, 16))
    for lead in ((2, 16), (16,), (16,), (3, 4), (3, 4), (3,), (3,), (4,), (4,)):
        shapes += parts(lead)[:-1]
    shapes += parts((), F32)[:-1]
    for lead in ((4, 4), (4, 4), (4, 4), (16,), (16,), (4,), (4,)):
        shapes.append(pltpu.VMEM((*lead, 16, 128), F32))
    shapes += [pltpu.VMEM((2, 8, 128), F32), pltpu.VMEM((8, 384), F32)]
    shapes += [
        pltpu.VMEM((3, T, D), BF),
        pltpu.VMEM((2, T, D), BF),
        pltpu.VMEM((D, T), BF),
        pltpu.VMEM((T, D), BF),
        pltpu.VMEM((T, D), F32),
        pltpu.VMEM((T, D), BF),
    ]
    shapes += [pltpu.VMEM(shape, kind) for shape, kind in KEPT]
    shapes += [
        pltpu.VMEM((2, TILE, 768), BF),
        pltpu.VMEM((2, TILE, 512), BF),
        pltpu.VMEM((2, TILE, 256), BF),
        pltpu.VMEM((6, TILE, TILE), F32),
    ]
    shapes += [
        pltpu.VMEM((8, D), F32),
        pltpu.VMEM((16, 128), F32),
        pltpu.VMEM((8, 512), F32),
        pltpu.VMEM((8, D), F32),
        pltpu.VMEM((8, 512), F32),
        pltpu.VMEM((T, 1), F32),
        pltpu.VMEM((6, TILE, TILE), F32),
        pltpu.VMEM((8, T), F32),
        pltpu.VMEM((8, T), F32),
    ]
    dma = pltpu.SemaphoreType.DMA
    shapes += [dma((2, PARTS, 5))] * 3
    shapes += [dma((PARTS,)), dma((12,)), dma((2,)), dma((2,))]
    return shapes


KEPT = (
    ((3 * D, T), BF),
    ((HEADS, TILE, 768), BF),
    ((HEADS, TILE, 512), BF),
    ((HEADS, TILE, 256), BF),
    ((D, T), BF),
    ((HEADS, T), F32),
    ((T, FF), BF),
    ((T, FF), BF),
)


def body(
    inputs,
    cotangent,
    lengths,
    norm1_gain,
    norm1_bias,
    qkv_weight,
    qkv_bias,
    dense_weight,
    norm2_gain,
    norm2_bias,
    fc_in_weight,
    fc_in_bias,
    fc_out_weight,
    out_bias,
):
    hbm = pl.BlockSpec(memory_space=pl.ANY)
    vmem = pl.BlockSpec(memory_space=pltpu.VMEM)
    shape = jax.ShapeDtypeStruct
    results = pl.pallas_call(
        kernel,
        out_shape=[shape((2, T, D), BF), shape((2, T, D), BF), shape((PAIRS, 2, 16, 384), F32)]
        + [shape((2, HALF_ROWS[c], WIDTH[c]), F32) for c in range(PAIRS, VEC)]
        + [shape((16, 128), F32)]
        + [shape(s, k) for s, k in KEPT],
        in_specs=[pl.BlockSpec(memory_space=pltpu.SMEM)] + [hbm] * 6 + [vmem] * 7,
        out_specs=[hbm] * 2 + [vmem] * 5 + [hbm] * len(KEPT),
        scratch_shapes=scratch_shapes(),
        compiler_params=pltpu.CompilerParams(
            collective_id=0, has_side_effects=True, vmem_limit_bytes=64 * 1024 * 1024
        ),
        name="layers",
    )(
        lengths,
        inputs,
        cotangent,
        qkv_weight,
        dense_weight,
        fc_in_weight,
        fc_out_weight,
        norm1_gain,
        norm1_bias,
        norm2_gain,
        norm2_bias,
        out_bias,
        qkv_bias,
        fc_in_bias,
    )
    vector, slab = shape((1, 32), F32), shape((1, 2, T, D), BF)
    return pl.pallas_call(
        hand_out,
        out_shape=[slab, slab, vector, vector, shape((1, 32, 1536), F32), shape((1, 96), F32)]
        + [shape((1, 32, 512), F32), vector, vector, shape((1, 32, 2048), F32), shape((1, 128), F32)]
        + [shape((1, 128, 512), F32), vector],
        in_specs=[hbm] * 7,
        out_specs=[hbm] * 2 + [vmem] * 11,
        scratch_shapes=[pltpu.VMEM((4, T, D), BF)]
        + [pltpu.VMEM(r.shape, r.dtype) for r in results[2:7]]
        + [pltpu.SemaphoreType.DMA((9,)), pltpu.SemaphoreType.DMA((4,))],
        compiler_params=pltpu.CompilerParams(vmem_limit_bytes=60 * 1024 * 1024),
        name="hand_out",
    )(*results[:7])


def hand_out(
    act, ig, hq, hd, hi, ho, hv, o_act, o_ig, o_g1, o_b1, o_qkv, o_qkvb, o_d, o_g2, o_b2, o_in, o_inb, o_out, o_last, held, gq, gd, gi, go, gv, arrive, leave
):
    z = lax.axis_index("shard") % 4
    pieces = [(act.at[m], o_act.at[0, m]) for m in (0, 1)] + [(ig.at[m], o_ig.at[0, m]) for m in (0, 1)]
    coming = [pltpu.make_async_copy(src, held.at[k], arrive.at[k]) for k, (src, _) in enumerate(pieces)]
    going = [pltpu.make_async_copy(held.at[k], dst, leave.at[k]) for k, (_, dst) in enumerate(pieces)]
    small = [
        pltpu.make_async_copy(src, dst, arrive.at[4 + k])
        for k, (src, dst) in enumerate(((hq, gq), (hd, gd), (hi, gi), (ho, go), (hv, gv)))
    ]
    for copy in coming + small:
        copy.start()
    for copy, after in zip(coming, going):
        copy.wait()
        after.start()
    for copy in small:
        copy.wait()
    for half in (0, 1):
        rows = slice(16 * half, 16 * half + 16)
        for hp in range(PAIRS):
            for which in range(3):
                column = 512 * which + 128 * hp
                o_qkv[0, rows, column : column + 128] = gq[hp, half, :, 128 * which : 128 * which + 128]
        o_d[0, rows, :] = gd[half]
        o_in[0, rows, :] = gi[half]
        o_out[0, 64 * half : 64 * half + 64, :] = go[half]

    def own(row, width):
        total = jnp.zeros((1, width), F32)
        for k in range(4):
            total = total + jnp.where(z == k, row[:, width * k : width * k + width], 0.0)
        return total

    for row, ref in enumerate((o_g1, o_b1, o_g2, o_b2, o_last)):
        ref[...] = own(gv[row : row + 1, :], 32)
    o_qkvb[...] = own(jnp.concatenate([gv[8 + k : 9 + k, :] for k in range(3)], axis=1), 96)
    o_inb[...] = gv[11:12, :]
    for copy in going:
        copy.wait()


def solution(mesh):
    rows = P(None, ("replica", "shard"), None)
    vector, matrix = P("section", "shard"), P("section", "shard", None)
    slabs = P("section", None, ("replica", "shard"), None)
    return jax.shard_map(
        body,
        mesh=mesh,
        in_specs=(
            rows, rows, rows, vector, vector, matrix, vector, matrix, vector, vector, matrix, vector, matrix, vector,
        ),
        out_specs=(
            slabs, slabs, vector, vector, matrix, vector, matrix, vector, vector, matrix, vector, matrix, vector,
        ),
        check_vma=False,
    )
```

```python
import math

import jax
import jax.numpy as jnp
from jax import lax
from jax.experimental import pallas as pl
from jax.experimental.pallas import tpu as pltpu
from jax.sharding import PartitionSpec as P

T = 768
D = 512
FF = 2048
HEADS = 8
HEAD = 64
ROT = 16
BLOCK = 128
SEQS = 4
TILE = 256
EPS = 1e-5
MASKED = -1e9
LOG2E = 1.0 / math.log(2.0)
LN2 = math.log(2.0)
MESH = pl.DeviceIdType.MESH
BF = jnp.bfloat16
F32 = jnp.float32

PAIRS = 4
DENSE, FIN, FOUT, VEC = 4, 5, 6, 7
PARTS = 8
LETTERS = "abcdDIOV"
HALF_ROWS = (16, 16, 16, 16, 16, 16, 64, 8)
WIDTH = (384, 384, 384, 384, 512, 2048, 512, 128)
KIND = (BF, BF, BF, BF, BF, BF, BF, F32)


def dg(a, b, ca, cb):
    return lax.dot_general(a, b, (((ca,), (cb,)), ((), ())), preferred_element_type=F32)


class Place:
    def __init__(self):
        self.s = lax.axis_index("section")
        self.y = lax.axis_index("replica")
        shard = lax.axis_index("shard")
        x, z = shard // 4, shard % 4
        self.shard, self.x, self.z = shard, x, z
        self.p = x + self.s * (z - x)
        self.q = z + self.s * (x - z)

    def at(self, p, q):
        return (1 - self.s) * (4 * p + q) + self.s * (4 * q + p)

    def sibling(self):
        return (1 - self.s, self.y, self.shard)

    def along_p(self, d):
        return (self.s, self.y, self.at((self.p + d) % 4, self.q))

    def along_q(self, d):
        return (self.s, self.y, self.at(self.p, (self.q + d) % 4))

    def along_y(self, d):
        return (self.s, (self.y + d) % 4, self.shard)


def remote(src, dst, send, recv, device):
    return pltpu.make_async_remote_copy(
        src_ref=src, dst_ref=dst, send_sem=send, recv_sem=recv, device_id=device, device_id_type=MESH
    )


class Gather:
    def __init__(self, me, layer, part, shard_ref, whole, send, recv, local):
        self.me, self.layer, self.part = me, layer, part
        self.shard_ref, self.w = shard_ref, whole
        self.send = lambda k: send.at[layer, part, k]
        self.recv = lambda k: recv.at[layer, part, k]
        self.local = local.at[part]
        self.rows = HALF_ROWS[part]
        self.direct = layer == 0 and part in (0, 1, 2, 3, VEC)
        self.ways = (1, 3, 2) if self.direct else (1, 3)

    def halves(self, h, target):
        if self.part == VEC:
            return [(self.shard_ref.at[h], target)]
        rows = pl.ds(pl.multiple_of(h * self.rows, self.rows), self.rows)
        if self.part < PAIRS:
            return [
                (
                    self.shard_ref.at[0, rows, pl.ds(512 * which + 128 * self.part, 128)],
                    target.at[:, pl.ds(128 * which, 128)],
                )
                for which in range(3)
            ]
        return [(self.shard_ref.at[0, rows, :], target)]

    def move(self, ref, sent, came, device):
        return remote(ref, ref, self.send(sent), self.recv(came), device)

    def shards(self, count):
        return self.move(self.w.at[self.me.s, pl.ds(0, count)], 1, 1, self.me.sibling())

    def row(self, half, p):
        return self.w.at[half, pl.ds(4 * p, 4)]

    def own(self, half, p, q):
        return self.w.at[half, 4 * p + q]

    def step0(self):
        me = self.me

        @pl.when(me.s == self.layer)
        def _():
            for src, dst in self.halves(me.s, self.own(me.s, me.p, me.q)):
                pltpu.make_async_copy(src, dst, self.local).start()
            for src, dst in self.halves(1 - me.s, self.own(1 - me.s, me.q, me.p)):
                remote(src, dst, self.send(0), self.recv(0), me.sibling()).start()

    def step1(self):
        me = self.me
        own = self.own(me.s, me.p, me.q)

        @pl.when(me.s == self.layer)
        def _():
            pltpu.make_async_copy(own, own, self.local).wait()

        @pl.when(me.s != self.layer)
        def _():
            self.move(own, 0, 0, me.sibling()).wait_recv()

        for d in (1, 3, 2):
            self.move(own, 1, 1, me.along_q(d)).start()

    def across(self, p):
        self.move(self.row(self.me.s, p), 2, 4, self.me.sibling()).start()

    def step2(self):
        me = self.me
        self.shards(3).wait_recv()
        for d in self.ways:
            self.move(self.row(me.s, me.p), 1, 2, me.along_p(d)).start()
        self.across(me.p)

    def step3(self):
        me = self.me
        ref = self.w.at[me.s, pl.ds(0, 4 * len(self.ways))]
        self.move(ref, 1, 2, me.sibling()).wait_recv()
        if not self.direct:
            for d in (1, 3):
                half = self.w.at[me.s, pl.ds(4 * ((me.p + 4 - d) % 4) + d - 1, 2)]
                self.move(half, 1, 3, me.along_p(d)).start()
        for d in self.ways:
            self.across((me.p + 4 - d) % 4)

    def step4(self):
        me = self.me
        if not self.direct:
            self.move(self.row(me.s, me.p), 1, 3, me.sibling()).wait_recv()
            self.across((me.p + 2) % 4)

    def step5(self):
        self.move(self.w.at[1 - self.me.s], 2, 4, self.me.sibling()).wait_recv()

    def finish(self):
        me = self.me

        @pl.when(me.s == self.layer)
        def _():
            self.move(self.own(1 - me.s, me.q, me.p), 0, 0, me.sibling()).wait_send()

        self.shards(15).wait_send()
        self.move(self.w.at[me.s], 2, 4, me.sibling()).wait_send()


class Reduce:
    def __init__(self, me, layer, part, terms, buffers, send, recv):
        self.me, self.layer, self.part = me, layer, part
        self.g = terms
        self.r, self.one, self.two, self.ys, self.f, self.out = buffers
        self.send = lambda k: send.at[layer, part, k]
        self.recv = lambda k: recv.at[layer, part, k]
        self.kind = KIND[part]

    def swap(self):
        me = self.me
        return remote(self.g.at[1 - me.s], self.r, self.send(0), self.recv(0), me.sibling())

    def first(self, d):
        me = self.me
        row = self.r.at[pl.ds(4 * ((me.p + d) % 4), 4)]
        return remote(row, self.one.at[d - 1], self.send(1), self.recv(1), me.along_p(d))

    def second(self, d):
        me = self.me
        shard = self.r.at[4 * me.p + (me.q + d) % 4]
        return remote(shard, self.two.at[d - 1], self.send(2), self.recv(2), me.along_q(d))

    def third(self, d):
        me = self.me
        return remote(self.ys.at[me.y], self.ys.at[me.y], self.send(3), self.recv(3), me.along_y(d))

    def all_of(self, ref, k):
        return remote(ref, ref, self.send(k), self.recv(k), self.me.sibling())

    def back(self):
        me = self.me
        return remote(self.f, self.out.at[me.s], self.send(4), self.recv(4), me.sibling())

    def step0(self):
        self.swap().start()

    def step1(self):
        me = self.me
        self.swap().wait_recv()

        def one(k, c):
            self.r[k] = (self.r[k].astype(F32) + self.g[me.s, k].astype(F32)).astype(self.kind)
            return c

        lax.fori_loop(0, 16, one, 0)
        for d in (1, 3, 2):
            self.first(d).start()
        self.swap().wait_send()

    def step2(self):
        me = self.me
        self.all_of(self.one, 1).wait_recv()

        def one(b, c):
            total = self.r[4 * me.p + b].astype(F32) + self.one[0, b].astype(F32)
            total = total + (self.one[1, b].astype(F32) + self.one[2, b].astype(F32))
            self.r[4 * me.p + b] = total.astype(self.kind)
            return c

        lax.fori_loop(0, 4, one, 0)
        for d in (1, 3, 2):
            self.second(d).start()

    def step3(self):
        me = self.me
        self.all_of(self.two, 2).wait_recv()
        total = self.r[4 * me.p + me.q].astype(F32) + self.two[0].astype(F32)
        total = total + (self.two[1].astype(F32) + self.two[2].astype(F32))
        self.ys[me.y] = total.astype(self.kind)
        for d in (1, 3, 2):
            self.third(d).start()

    def step4(self):
        me = self.me
        self.all_of(self.ys.at[pl.ds(0, 3)], 3).wait_recv()
        total = (self.ys[0].astype(F32) + self.ys[1].astype(F32)) + (
            self.ys[2].astype(F32) + self.ys[3].astype(F32)
        )

        @pl.when(me.s == self.layer)
        def _():
            self.out[me.s] = total

        @pl.when(me.s != self.layer)
        def _():
            self.f[...] = total
            self.back().start()

    def step5(self):
        me = self.me

        @pl.when(me.s == self.layer)
        def _():
            self.all_of(self.out.at[1 - me.s], 4).wait_recv()

    def finish(self):
        self.all_of(self.one, 1).wait_send()
        self.all_of(self.two, 2).wait_send()
        self.all_of(self.ys.at[pl.ds(0, 3)], 3).wait_send()

        @pl.when(self.me.s != self.layer)
        def _():
            self.back().wait_send()


class ReduceVectors:
    def __init__(self, me, layer, terms, buffers, send, recv):
        self.me, self.layer, self.g = me, layer, terms
        self.r, self.one, self.ys, self.out = buffers
        self.send = lambda k: send.at[layer, VEC, k]
        self.recv = lambda k: recv.at[layer, VEC, k]

    def swap(self):
        return remote(self.g, self.r, self.send(0), self.recv(0), self.me.sibling())

    def first(self, k):
        x, z = (self.me.x + k // 4) % 4, (self.me.z + k % 4) % 4
        device = (self.me.s, self.me.y, 4 * x + z)
        return remote(self.r.at[x, z], self.one.at[k], self.send(1), self.recv(1), device)

    def all_first(self):
        ref = self.one.at[pl.ds(1, 15)]
        return remote(ref, ref, self.send(1), self.recv(1), self.me.sibling())

    def third(self, d):
        me = self.me
        return remote(self.ys.at[me.y], self.ys.at[me.y], self.send(3), self.recv(3), me.along_y(d))

    def all_third(self):
        ref = self.ys.at[pl.ds(0, 3)]
        return remote(ref, ref, self.send(3), self.recv(3), self.me.sibling())

    def owner(self, step):
        pl.when(self.me.s == self.layer)(step)

    def step0(self):
        @pl.when(self.me.s != self.layer)
        def _():
            self.swap().start()

    def step1(self):
        def step():
            self.swap().wait_recv()
            self.r[...] += self.g[...]
            for k in (1, 4, 3, 12, 5, 7, 13, 15, 2, 8, 6, 9, 11, 14, 10):
                self.first(k).start()

        self.owner(step)

        @pl.when(self.me.s != self.layer)
        def _():
            self.swap().wait_send()

    def step2(self):
        def step():
            self.all_first().wait_recv()
            total = self.r[self.me.x, self.me.z]
            for k in range(1, 16):
                total = total + self.one[k]
            self.ys[self.me.y] = total
            for d in (1, 3, 2):
                self.third(d).start()

        self.owner(step)

    def step3(self):
        def step():
            self.all_third().wait_recv()
            self.out[...] = (self.ys[0] + self.ys[1]) + (self.ys[2] + self.ys[3])

        self.owner(step)

    def step5(self):
        pass

    def finish(self):
        def step():
            self.all_first().wait_send()
            self.all_third().wait_send()

        self.owner(step)


def natural_rows(ref, columns):
    pieces = []
    for x in range(4):
        for z in range(4):
            pieces.append(ref[0, 4 * x + z, :, columns])
            pieces.append(ref[1, 4 * z + x, :, columns])
    return jnp.concatenate(pieces, axis=0)


def group_rows(ref, x):
    pieces = []
    for z in range(4):
        pieces.append(ref[0, 4 * x + z])
        pieces.append(ref[1, 4 * z + x])
    return jnp.concatenate(pieces, axis=0)


def put_natural(ref, columns, value):
    for x in range(4):
        for z in range(4):
            row = 32 * (4 * x + z)
            ref[0, 4 * x + z, :, columns] = value[row : row + 16]
            ref[1, 4 * z + x, :, columns] = value[row + 16 : row + 32]


def put_group(ref, x, value, rows):
    for z in range(4):
        row = 2 * rows * z
        ref[0, 4 * x + z] = value[row : row + rows]
        ref[1, 4 * z + x] = value[row + rows : row + 2 * rows]


def to_column(row):
    here = lax.broadcasted_iota(jnp.int32, (128, 128), 0) == lax.broadcasted_iota(
        jnp.int32, (128, 128), 1
    )
    return jnp.sum(jnp.where(here, row, 0.0), axis=1, keepdims=True)


def turn(rows, cosine, sine):
    pieces = []
    for e in (0, 64):
        low, high = rows[e : e + 8], rows[e + 8 : e + 16]
        pieces += [low * cosine - high * sine, high * cosine + low * sine, rows[e + 16 : e + 64]]
    return jnp.concatenate(pieces, axis=0)


def columns(start, size):
    return pl.ds(pl.multiple_of(start, size), size)


def loop(count, step):
    def one(k, c):
        step(k)
        return c

    lax.fori_loop(0, count, one, 0)


def kernel(
    lengths,
    x_ref,
    cot_ref,
    wq_ref,
    wd_ref,
    wi_ref,
    wo_ref,
    gain1_ref,
    shift1_ref,
    gain2_ref,
    shift2_ref,
    last_ref,
    qkvb_ref,
    finb_ref,
    act_out,
    ig_out,
    gq_out,
    gd_out,
    gi_out,
    go_out,
    gv_out,
    st_qkv,
    st_p0,
    st_p1,
    st_p2,
    st_bt,
    st_rinv,
    st_act,
    st_slo,
    *scratch,
):
    scratch = list(scratch)

    def take(count):
        taken, scratch[:count] = scratch[:count], []
        return taken

    def take_parts(count=4):
        pairs, *rest = take(count)
        return [pairs] + [pairs.at[k] for k in range(PAIRS)] + rest

    (wq0, *w0), (wq1, *w1) = take_parts(5), take_parts(5)
    w, wq = (w0, w1), (wq0, wq1)
    gq, *g = take_parts()
    r, one, two, ys = [(take_parts(), take_parts()) for _ in range(4)]
    rq = [parts.pop(0) for parts in r]
    for both in (one, two, ys):
        for parts in both:
            parts.pop(0)
    f = take_parts()[1:]
    gvec, *rvec = take(3)
    vecs, yvec, (vsrc, vrow) = take(2), take(2), take(2)
    hid, grad, n1t, n2, acc, carried = take(6)
    qkvt, p0, p1, p2, bt, rinv, act, slo = take(8)
    d0, d1, d2, scores_one = take(4)
    dn1 = n2
    vd, vq, vf, dvec, fvec, live, bias, cos_ref, sin_ref = take(9)
    sends, ag_recv, rs_recv, ag_local, sems, ex_send, ex_recv = take(7)
    probs = (p0, p1, p2)
    dscores = (d0, d1, d2)
    outs = [gq_out.at[k] for k in range(PAIRS)] + [gd_out, gi_out, go_out]
    shards = [wq_ref] * PAIRS + [wd_ref, wi_ref, wo_ref, vsrc]

    me = Place()
    s = me.s
    barrier = pltpu.get_barrier_semaphore()
    partners = [me.sibling()]
    for d in (1, 2, 3):
        partners += [me.along_q(d), me.along_p(d), me.along_y(d)]
        for e in (1, 2, 3):
            partners.append((s, me.y, 4 * ((me.x + d) % 4) + (me.z + e) % 4))
    for device in partners:
        pl.semaphore_signal(barrier, inc=1, device_id=device, device_id_type=MESH)
    pl.semaphore_wait(barrier, len(partners))

    gather = [
        [Gather(me, l, c, shards[c], w[l][c], sends, ag_recv, ag_local) for c in range(PARTS)]
        for l in (0, 1)
    ]
    reduce = [
        [
            Reduce(
                me, l, c, g[c], (r[l][c], one[l][c], two[l][c], ys[l][c], f[c], outs[c]), sends, rs_recv
            )
            for c in range(VEC)
        ]
        + [ReduceVectors(me, l, gvec, (rvec[l], vecs[l], yvec[l], gv_out), sends, rs_recv)]
        for l in (0, 1)
    ]

    def fetch(*plan):
        for word in plan:
            item = gather[int(word[0])][LETTERS.index(word[1])]
            getattr(item, "step" + word[2])()

    def back_pairs(l, first):
        def step(k):
            hp = first + k
            back_attend(l, hp)
            back_qkv(hp)
            remote(
                gq.at[hp, 1 - s], rq[l].at[hp], sends.at[l, hp, 0], rs_recv.at[l, hp, 0], me.sibling()
            ).start()

        loop(2, step)

    def send(*plan):
        for word in plan:
            item = reduce[int(word[0])][LETTERS.index(word[1])]
            getattr(item, "step" + word[2])()

    vsrc[...] = jnp.zeros((2, 8, 128), F32)
    for k in range(4):
        here = me.z == k
        for row, ref in enumerate((gain1_ref, shift1_ref, gain2_ref, shift2_ref, last_ref)):
            vsrc[0, row : row + 1, 32 * k : 32 * k + 32] = jnp.where(here, ref[...].astype(F32), 0.0)
        vrow[0:1, 96 * k : 96 * k + 96] = jnp.where(here, qkvb_ref[...].astype(F32), 0.0)
    for k in range(3):
        vsrc[1, k : k + 1, :] = vrow[0:1, 128 * k : 128 * k + 128]
    vsrc[1, 3:4, :] = finb_ref[...].astype(F32)

    x_in = pltpu.make_async_copy(x_ref.at[s], hid.at[0], sems.at[0])
    cot_in = pltpu.make_async_copy(cot_ref.at[s], grad.at[0], sems.at[1])
    x_in.start()
    fetch("0V0", "0a0", "0b0", "0c0", "0d0", "0I0", "0D0", "0O0", "1V0", "1a0", "1b0", "1c0", "1d0", "1I0", "1D0", "1O0")
    fetch("0V1", "0a1", "0b1", "0c1", "0d1", "0D1", "0I1", "0O1")
    cot_in.start()

    starts, ends, at = [], [], jnp.int32(0)
    for k in range(SEQS):
        size = lengths[s, 0, k]
        starts.append(at)
        ends.append(at + size)
        at = at + (size + BLOCK - 1) // BLOCK * BLOCK

    def inside(places):
        return [(places >= a) & (places < b) for a, b in zip(starts, ends)]

    def live_tile(k):
        places = lax.broadcasted_iota(jnp.int32, (TILE, 1), 0) + k * TILE
        total = jnp.zeros((TILE, 1), F32)
        for found in inside(places):
            total = total + jnp.where(found, 1.0, 0.0)
        live[columns(k * TILE, TILE), :] = total

    loop(3, live_tile)
    places = lax.broadcasted_iota(jnp.int32, (8, T), 1)
    begin = jnp.zeros((8, T), jnp.int32)
    offset = jnp.zeros((8, T), jnp.int32)
    for found, a in zip(inside(places), starts):
        begin = begin + jnp.where(found, a, 0)
        offset = offset + jnp.where(found, places - a, 0)
    rates = jnp.exp(
        lax.broadcasted_iota(jnp.int32, (8, T), 0).astype(F32) * (-2.0 * math.log(10000.0) / ROT)
    )
    angles = offset.astype(F32) * rates
    cos_ref[...] = jnp.cos(angles)
    sin_ref[...] = jnp.sin(angles)
    for j in range(3):
        for i in range(j + 1):
            keys = lax.broadcasted_iota(jnp.int32, (TILE, TILE), 0) + i * TILE
            queries = lax.broadcasted_iota(jnp.int32, (TILE, TILE), 1) + j * TILE
            fits = (keys >= begin[0:1, j * TILE : (j + 1) * TILE]) & (keys <= queries)
            bias[j * (j + 1) // 2 + i] = jnp.where(fits, 0.0, MASKED)

    def unpack(l):
        ref = w[l][VEC]
        for x in range(4):
            vd[:, 128 * x : 128 * x + 128] = (ref[0, 4 * x] + ref[0, 4 * x + 1]) + (
                ref[0, 4 * x + 2] + ref[0, 4 * x + 3]
            )
            group = (ref[1, x] + ref[1, 4 + x]) + (ref[1, 8 + x] + ref[1, 12 + x])
            for k in range(3):
                vq[3 * x + k : 3 * x + k + 1, :] = group[k : k + 1]
            for z in range(4):
                vf[x : x + 1, 128 * z : 128 * z + 128] = ref[1, 4 * z + x][3:4]

    def normed(l, rows):
        v = hid[l, rows, :].astype(F32)
        centred = v - jnp.mean(v, axis=1, keepdims=True)
        scale = lax.rsqrt(jnp.mean(centred * centred, axis=1, keepdims=True) + EPS)
        return centred * scale, scale

    def norms(l):
        def tile(k):
            rows = columns(k * TILE, TILE)
            u, _ = normed(l, rows)
            n1t[:, rows] = (u * vd[0:1, :] + vd[1:2, :]).astype(BF).T
            n2[rows, :] = (u * vd[2:3, :] + vd[3:4, :]).astype(BF)

        loop(3, tile)

    def project(l, hp):
        value = dg(natural_rows(wq[l].at[hp], slice(0, 384)), n1t[...], 0, 0)
        pair = []
        for which in range(3):
            part = value[128 * which : 128 * which + 128] + to_column(vq[pl.ds(which * 4 + hp, 1), :])
            if which < 2:
                part = turn(part, cos_ref[...], sin_ref[...])
            if which == 0:
                part = part * (LOG2E / 8.0)
            pair.append(part.astype(BF))
            qkvt[columns(hp * 384 + which * 128, 128), :] = pair[which]
        return pair

    def score_block(e, k):
        if e:
            return scores_one.at[k]
        return acc.at[pl.ds(TILE * (k // 2), TILE), pl.ds(TILE * (k % 2), TILE)]

    def attend(l, hp):
        pair = project(l, hp)
        keys = pair[1].T
        blank = jnp.zeros((HEAD, T), BF)
        peaks = ([None] * 3, [None] * 3)
        for e in (0, 1):
            mine = pair[0][e * HEAD : (e + 1) * HEAD]
            mine = jnp.concatenate([mine, blank] if e == 0 else [blank, mine], axis=0)
            for i in range(3):
                for j in range(i, 3):
                    k = j * (j + 1) // 2 + i
                    scores = dg(keys[i * TILE : (i + 1) * TILE], mine[:, j * TILE : (j + 1) * TILE], 1, 0)
                    scores = scores + bias[k]
                    score_block(e, k)[...] = scores
                    peak = jnp.max(scores, axis=0, keepdims=True)
                    peaks[e][j] = peak if i == 0 else jnp.maximum(peaks[e][j], peak)
        for e in (0, 1):
            h = 2 * hp + e
            value = jnp.concatenate([pair[2][e * HEAD : (e + 1) * HEAD], jnp.ones((8, T), BF)], axis=0)
            for j in range(3):
                at_j = slice(j * TILE, (j + 1) * TILE)
                blended = jnp.zeros((HEAD + 8, TILE), F32)
                for i in range(j + 1):
                    raised = jnp.exp2(score_block(e, j * (j + 1) // 2 + i)[...] - peaks[e][j]).astype(BF)
                    probs[i][h, :, (j - i) * TILE : (j - i + 1) * TILE] = raised
                    blended = blended + dg(value[:, i * TILE : (i + 1) * TILE], raised, 1, 0)
                inverse = 1.0 / blended[HEAD : HEAD + 1]
                rinv[pl.ds(h, 1), at_j] = inverse
                bt[columns(hp * 128 + e * HEAD, HEAD), at_j] = (blended[:HEAD] * inverse).astype(BF)

    def widen(l, c):
        cols = columns(c * 512, 512)
        weight = natural_rows(w[l][FIN], cols)
        shift = vf[pl.ds(c, 1), :]

        def tile(k):
            rows = columns(k * TILE, TILE)
            v = dg(n2[rows, :], weight, 1, 0) + shift
            below = 0.5 + 0.5 * lax.erf(v * (1.0 / math.sqrt(2.0)))
            act[rows, cols] = (v * below).astype(BF)
            slope = below + v * (jnp.exp(-0.5 * v * v) * (1.0 / math.sqrt(2.0 * math.pi)))
            slo[rows, cols] = slope.astype(BF)

        for k in range(3):
            tile(k)

    def join(l):
        def part(t):
            cols = columns(t * TILE, TILE)
            weight = jnp.concatenate(
                [
                    piece
                    for x in range(4)
                    for z in range(4)
                    for piece in (w[l][FOUT][0, 4 * x + z, :, cols], w[l][FOUT][1, 4 * z + x, :, cols])
                ],
                axis=0,
            )
            total = dg(act[...], weight, 1, 0)
            total = total + dg(bt[...], natural_rows(w[l][DENSE], cols), 0, 0)
            total = total + hid[l, :, cols].astype(F32) + vd[4:5, cols]
            hid[l + 1, :, cols] = (total * live[...]).astype(BF)

        loop(2, part)

    def local(src, dst, k):
        return pltpu.make_async_copy(src, dst, sems.at[k])

    attention_kept = [
        (qkvt, st_qkv, 2),
        (p0, st_p0, 3),
        (p1, st_p1, 4),
        (p2, st_p2, 5),
        (bt, st_bt, 6),
        (rinv, st_rinv, 7),
    ]
    wide_kept = [(act, st_act, 8), (slo, st_slo, 9)]

    fetch("0V2", "0a2", "0b2", "0c2", "0d2")
    x_in.wait()
    fetch("0V3", "0a3")
    fetch("0D2", "0I2")
    fetch("0V5")
    unpack(0)
    norms(0)
    fetch("0b3", "0O2", "0a5")
    fetch("0c3", "0b5")
    loop(2, lambda hp: attend(0, hp))
    fetch("0d3", "0c5")
    fetch("0D3", "0I3")
    fetch("1V1", "1a1", "1b1", "1c1", "1d1", "0d5")
    loop(2, lambda hp: attend(0, hp + 2))
    for a, b, k in attention_kept:
        local(a, b, k).start()
    fetch("0O3")
    fetch("1I1", "1D1", "1O1")
    fetch("0D4", "0I4", "1V2", "1a2", "1b2")
    fetch("0I5")
    loop(2, lambda c: widen(0, c))
    fetch("0O4")
    fetch("1c2", "1d2", "1V3", "1a3")
    loop(2, lambda c: widen(0, c + 2))
    fetch("1b3", "1c3", "1d3", "1I2", "1D2", "1O2", "0D5", "0O5")
    join(0)
    for a, b, k in wide_kept:
        local(a, b, k).start()

    fetch("1V4", "1a4", "1b4")
    fetch("1V5")
    unpack(1)
    norms(1)
    fetch("1c4", "1d4", "1a5", "1b5")
    for a, b, k in attention_kept:
        local(a, b, k).wait()
    loop(2, lambda hp: attend(1, hp))
    fetch("1I3", "1D3", "1c5", "1d5")
    loop(2, lambda hp: attend(1, hp + 2))
    fetch("1O3", "1I4", "1D4")
    fetch("1I5")
    for a, b, k in wide_kept:
        local(a, b, k).wait()
    loop(2, lambda c: widen(1, c))
    fetch("1O4")
    loop(2, lambda c: widen(1, c + 2))
    fetch("1D5", "1O5")
    join(1)
    for l in (0, 1):
        for c in range(PARTS):
            gather[l][c].finish()
    act_mine = local(hid.at[1 + s], act_out.at[s], 10)
    act_theirs = remote(hid.at[2 - s], act_out.at[s], ex_send.at[0], ex_recv.at[0], me.sibling())
    act_mine.start()
    act_theirs.start()
    cot_in.wait()

    def start_back(l):
        def tile(k):
            rows = columns(k * TILE, TILE)
            v = grad[1 - l, rows, :].astype(F32) * live[rows, :]
            carried[rows, :] = v.astype(BF)
            here = jnp.sum(v, axis=0, keepdims=True)
            dvec[4:5, :] = here + jnp.where(k == 0, 0.0, dvec[4:5, :])

        dvec[...] = jnp.zeros((8, D), F32)
        loop(3, tile)

    def back_out(c):
        cols = columns(c * 512, 512)
        put_group(g[FOUT], c, dg(act[:, cols], carried[...], 0, 0).astype(BF), 64)

    def back_wide(l, c):
        cols = columns(c * 512, 512)
        weight = group_rows(w[l][FOUT], c)
        total = jnp.zeros((1, 512), F32)
        for k in range(3):
            rows = slice(k * TILE, (k + 1) * TILE)
            v = dg(carried[rows, :], weight, 1, 1) * slo[rows, cols].astype(F32)
            v = v.astype(BF)
            slo[rows, cols] = v
            total = total + jnp.sum(v.astype(F32), axis=0, keepdims=True)
        fvec[pl.ds(c, 1), :] = total

    def back_in(l, c):
        cols = columns(c * 512, 512)
        put_natural(g[FIN], cols, dg(n2[...], slo[:, cols], 0, 0).astype(BF))

    def back_norm_two(l, t):
        low = w[l][FIN][0, pl.ds(8 * t, 8)]
        high = [w[l][FIN][1, pl.ds(4 * z + 2 * t, 2)] for z in range(4)]
        pieces = []
        for x in range(2):
            for z in range(4):
                pieces += [low[4 * x + z], high[z][x]]
        acc[:, columns(t * TILE, TILE)] = dg(slo[...], jnp.concatenate(pieces, axis=0), 1, 1)

    def back_dense(l):
        put_natural(g[DENSE], slice(0, 512), dg(bt[...], carried[...], 1, 0).astype(BF))

    def back_attend(l, hp):
        weight = group_rows(w[l][DENSE], hp)
        below = dg(weight, carried[...], 1, 1)
        queries = qkvt[columns(hp * 384, 128), :]
        keys = qkvt[columns(hp * 384 + 128, 128), :]
        values = qkvt[columns(hp * 384 + 256, 128), :].T
        blended = bt[columns(hp * 128, 128), :].astype(F32)
        blank = jnp.zeros((HEAD, TILE), BF)
        downs = []
        for e in (0, 1):
            h = 2 * hp + e
            down = below[e * HEAD : (e + 1) * HEAD] * rinv[pl.ds(h, 1), :]
            centre = jnp.sum(down * blended[e * HEAD : (e + 1) * HEAD], axis=0, keepdims=True)
            down = down.astype(BF)
            downs.append(down)
            for j in range(3):
                at_j = slice(j * TILE, (j + 1) * TILE)
                mine = down[:, at_j]
                mine = jnp.concatenate([mine, blank] if e == 0 else [blank, mine], axis=0)
                for i in range(j + 1):
                    cols = slice((j - i) * TILE, (j - i + 1) * TILE)
                    slope = dg(values[i * TILE : (i + 1) * TILE], mine, 1, 0) - centre[:, at_j]
                    slope = slope * probs[i][h, :, cols].astype(F32)
                    dscores[i][e, :, cols] = slope.astype(BF)
        done = []
        for e in (0, 1):
            h = 2 * hp + e
            query = queries[e * HEAD : (e + 1) * HEAD]
            key = keys[e * HEAD : (e + 1) * HEAD]
            grad_query, grad_key, grad_value = [], [], []
            for j in range(3):
                total = jnp.zeros((HEAD, TILE), F32)
                for i in range(j + 1):
                    cols = slice((j - i) * TILE, (j - i + 1) * TILE)
                    total = total + dg(key[:, i * TILE : (i + 1) * TILE], dscores[i][e, :, cols], 1, 0)
                grad_query.append(total * 0.125)
            for i in range(3):
                grad_key.append(dg(query[:, i * TILE :], dscores[i][e], 1, 1) * LN2)
                grad_value.append(dg(downs[e][:, i * TILE :], probs[i][h], 1, 1))
            done.append(
                [jnp.concatenate(pieces, axis=1) for pieces in (grad_query, grad_key, grad_value)]
            )
        for which in range(3):
            value = jnp.concatenate([done[0][which], done[1][which]], axis=0)
            if which < 2:
                value = turn(value, cos_ref[...], -sin_ref[...])
            qkvt[columns(hp * 384 + which * 128, 128), :] = value.astype(BF)

    def back_qkv(hp):
        value = dg(n1t[...], qkvt[columns(hp * 384, 384), :], 1, 1)
        put_natural(gq.at[hp], slice(0, 384), value.astype(BF))

    def back_norm_one(l, t):
        weight = jnp.concatenate([group_rows(wq[l].at[hp], t) for hp in range(PAIRS)], axis=1)
        dn1[:, columns(t * 128, 128)] = dg(weight, qkvt[...], 1, 0).astype(BF).T

    def norm_sums(l):
        def tile(k):
            rows = columns(k * TILE, TILE)
            u, _ = normed(l, rows)
            first = dn1[rows, :].astype(F32)
            second = acc[rows, :]
            dvec[0:1, :] += jnp.sum(first * u, axis=0, keepdims=True)
            dvec[1:2, :] += jnp.sum(first, axis=0, keepdims=True)
            dvec[2:3, :] += jnp.sum(second * u, axis=0, keepdims=True)
            dvec[3:4, :] += jnp.sum(second, axis=0, keepdims=True)

        loop(3, tile)

    def end_back(l):
        def tile(k):
            rows = columns(k * TILE, TILE)
            u, scale = normed(l, rows)
            first = dn1[rows, :].astype(F32)
            second = acc[rows, :]
            total = first * vd[0:1, :] + second * vd[2:3, :]
            centre = jnp.mean(total, axis=1, keepdims=True)
            along = jnp.mean(total * u, axis=1, keepdims=True)
            total = carried[rows, :].astype(F32) + scale * (total - centre - u * along)
            grad[l, rows, :] = total.astype(BF)

        loop(3, tile)

    def put_vectors(l):
        sums = dg(jnp.ones((8, T), BF), qkvt[...], 1, 1)
        for x in range(4):
            for k in range(3):
                which, hp = divmod(3 * x + k, PAIRS)
                row = 384 * hp + 128 * which
                vq[3 * x + k : 3 * x + k + 1, :] = sums[0:1, row : row + 128]
        for x in range(4):
            rest = jnp.concatenate([vq[3 * x : 3 * x + 3, :], jnp.zeros((5, 128), F32)], axis=0)
            for z in range(4):
                gvec[x, z, 0:8] = dvec[:, 128 * x : 128 * x + 128]
                gvec[x, z, 8:16] = rest
                gvec[x, z, 11:12] = fvec[x : x + 1, 128 * z : 128 * z + 128]

    restored = ((qkvt, st_qkv, 2), (p0, st_p0, 3), (p1, st_p1, 4), (p2, st_p2, 5), (bt, st_bt, 6), (rinv, st_rinv, 7))

    start_back(1)
    loop(4, back_out)
    send("1O0")
    loop(4, lambda c: back_wide(1, c))
    send("1O1")
    loop(4, lambda c: back_in(1, c))
    send("1I0")
    loop(2, lambda t: back_norm_two(1, t))
    local(st_act, act, 8).start()
    local(st_slo, slo, 9).start()
    back_dense(1)
    send("1D0", "1I1")
    back_pairs(1, 0)
    send("1D1", "1a1", "1O2")
    back_pairs(1, 2)
    send("1b1", "1c1", "1I2")
    loop(4, lambda t: back_norm_one(1, t))
    send("1d1", "1D2", "1O3")
    norm_sums(1)
    put_vectors(1)
    for a, b, k in restored:
        local(b, a, k).start()
    send("1V0", "1a2")
    end_back(1)

    unpack(0)
    norms(0)
    start_back(0)
    local(st_act, act, 8).wait()
    local(st_slo, slo, 9).wait()
    send("1b2", "1I3")
    loop(4, back_out)
    send("0O0", "1V1", "1D3", "1c2", "1d2", "1a3")
    loop(4, lambda c: back_wide(0, c))
    send("0O1", "1O4", "1b3")
    loop(4, lambda c: back_in(0, c))
    send("0I0", "1V2", "1c3", "1d3", "1D4")
    loop(2, lambda t: back_norm_two(0, t))
    send("0I1", "1I4", "1a4", "1b4")
    for a, b, k in restored:
        local(b, a, k).wait()
    back_dense(0)
    send("0D0")
    back_attend(0, 0)
    back_qkv(0)
    send("0a0", "0D1", "1V3", "1c4", "1d4")
    back_attend(0, 1)
    back_qkv(1)
    send("0b0", "0a1", "0O2")
    back_attend(0, 2)
    back_qkv(2)
    send("0c0", "0b1")
    back_attend(0, 3)
    back_qkv(3)
    send("0d0", "0c1")
    send("0I2", "0D2", "0a2", "0O3")
    loop(2, lambda t: back_norm_one(0, t))
    send("0d1", "0b2")
    loop(2, lambda t: back_norm_one(0, t + 2))
    norm_sums(0)
    put_vectors(0)
    send("0V0")
    send("0I3", "0c2", "0D3", "0a3", "0O4")
    send("0d2")
    send("0V1")
    end_back(0)
    grad_mine = local(grad.at[s], ig_out.at[s], 11)
    grad_theirs = remote(grad.at[1 - s], ig_out.at[s], ex_send.at[1], ex_recv.at[1], me.sibling())
    grad_mine.start()
    grad_theirs.start()
    send("0b3", "0c3", "0d3")
    send("0D4", "0a4")
    send("0V2")
    send("0b4", "0c4")
    send("0d4")
    send("0I4")
    send("0V3")
    for l in (1, 0):
        for c in range(PARTS):
            reduce[l][c].step5()
            reduce[l][c].finish()
    act_mine.wait()
    act_theirs.wait_send()
    remote(hid.at[2 - s], act_out.at[1 - s], ex_send.at[0], ex_recv.at[0], me.sibling()).wait_recv()
    grad_mine.wait()
    grad_theirs.wait_send()
    remote(grad.at[1 - s], ig_out.at[1 - s], ex_send.at[1], ex_recv.at[1], me.sibling()).wait_recv()


def scratch_shapes():
    def parts(lead, kind=None):
        return [pltpu.VMEM((PAIRS, *lead, HALF_ROWS[0], WIDTH[0]), kind or BF)] + [
            pltpu.VMEM((*lead, HALF_ROWS[c], WIDTH[c]), kind or KIND[c]) for c in range(PAIRS, PARTS)
        ]

    shapes = []
    for _ in (0, 1):
        shapes += parts((2, 16))
    for lead in ((2, 16), (16,), (16,), (3, 4), (3, 4), (3,), (3,), (4,), (4,)):
        shapes += parts(lead)[:-1]
    shapes += parts((), F32)[:-1]
    for lead in ((4, 4), (4, 4), (4, 4), (16,), (16,), (4,), (4,)):
        shapes.append(pltpu.VMEM((*lead, 16, 128), F32))
    shapes += [pltpu.VMEM((2, 8, 128), F32), pltpu.VMEM((8, 384), F32)]
    shapes += [
        pltpu.VMEM((3, T, D), BF),
        pltpu.VMEM((2, T, D), BF),
        pltpu.VMEM((D, T), BF),
        pltpu.VMEM((T, D), BF),
        pltpu.VMEM((T, D), F32),
        pltpu.VMEM((T, D), BF),
    ]
    shapes += [pltpu.VMEM(shape, kind) for shape, kind in KEPT]
    shapes += [
        pltpu.VMEM((2, TILE, 768), BF),
        pltpu.VMEM((2, TILE, 512), BF),
        pltpu.VMEM((2, TILE, 256), BF),
        pltpu.VMEM((6, TILE, TILE), F32),
    ]
    shapes += [
        pltpu.VMEM((8, D), F32),
        pltpu.VMEM((16, 128), F32),
        pltpu.VMEM((8, 512), F32),
        pltpu.VMEM((8, D), F32),
        pltpu.VMEM((8, 512), F32),
        pltpu.VMEM((T, 1), F32),
        pltpu.VMEM((6, TILE, TILE), F32),
        pltpu.VMEM((8, T), F32),
        pltpu.VMEM((8, T), F32),
    ]
    dma = pltpu.SemaphoreType.DMA
    shapes += [dma((2, PARTS, 5))] * 3
    shapes += [dma((PARTS,)), dma((12,)), dma((2,)), dma((2,))]
    return shapes


KEPT = (
    ((3 * D, T), BF),
    ((HEADS, TILE, 768), BF),
    ((HEADS, TILE, 512), BF),
    ((HEADS, TILE, 256), BF),
    ((D, T), BF),
    ((HEADS, T), F32),
    ((T, FF), BF),
    ((T, FF), BF),
)


def body(
    inputs,
    cotangent,
    lengths,
    norm1_gain,
    norm1_bias,
    qkv_weight,
    qkv_bias,
    dense_weight,
    norm2_gain,
    norm2_bias,
    fc_in_weight,
    fc_in_bias,
    fc_out_weight,
    out_bias,
):
    hbm = pl.BlockSpec(memory_space=pl.ANY)
    vmem = pl.BlockSpec(memory_space=pltpu.VMEM)
    shape = jax.ShapeDtypeStruct
    results = pl.pallas_call(
        kernel,
        out_shape=[shape((2, T, D), BF), shape((2, T, D), BF), shape((PAIRS, 2, 16, 384), F32)]
        + [shape((2, HALF_ROWS[c], WIDTH[c]), F32) for c in range(PAIRS, VEC)]
        + [shape((16, 128), F32)]
        + [shape(s, k) for s, k in KEPT],
        in_specs=[pl.BlockSpec(memory_space=pltpu.SMEM)] + [hbm] * 6 + [vmem] * 7,
        out_specs=[hbm] * 2 + [vmem] * 5 + [hbm] * len(KEPT),
        scratch_shapes=scratch_shapes(),
        compiler_params=pltpu.CompilerParams(
            collective_id=0, has_side_effects=True, vmem_limit_bytes=64 * 1024 * 1024
        ),
        name="layers",
    )(
        lengths,
        inputs,
        cotangent,
        qkv_weight,
        dense_weight,
        fc_in_weight,
        fc_out_weight,
        norm1_gain,
        norm1_bias,
        norm2_gain,
        norm2_bias,
        out_bias,
        qkv_bias,
        fc_in_bias,
    )
    vector, slab = shape((1, 32), F32), shape((1, 2, T, D), BF)
    return pl.pallas_call(
        hand_out,
        out_shape=[slab, slab, vector, vector, shape((1, 32, 1536), F32), shape((1, 96), F32)]
        + [shape((1, 32, 512), F32), vector, vector, shape((1, 32, 2048), F32), shape((1, 128), F32)]
        + [shape((1, 128, 512), F32), vector],
        in_specs=[hbm] * 7,
        out_specs=[hbm] * 2 + [vmem] * 11,
        scratch_shapes=[pltpu.VMEM((4, T, D), BF)]
        + [pltpu.VMEM(r.shape, r.dtype) for r in results[2:7]]
        + [pltpu.SemaphoreType.DMA((9,)), pltpu.SemaphoreType.DMA((4,))],
        compiler_params=pltpu.CompilerParams(vmem_limit_bytes=60 * 1024 * 1024),
        name="hand_out",
    )(*results[:7])


def hand_out(
    act, ig, hq, hd, hi, ho, hv, o_act, o_ig, o_g1, o_b1, o_qkv, o_qkvb, o_d, o_g2, o_b2, o_in, o_inb, o_out, o_last, held, gq, gd, gi, go, gv, arrive, leave
):
    z = lax.axis_index("shard") % 4
    pieces = [(act.at[m], o_act.at[0, m]) for m in (0, 1)] + [(ig.at[m], o_ig.at[0, m]) for m in (0, 1)]
    coming = [pltpu.make_async_copy(src, held.at[k], arrive.at[k]) for k, (src, _) in enumerate(pieces)]
    going = [pltpu.make_async_copy(held.at[k], dst, leave.at[k]) for k, (_, dst) in enumerate(pieces)]
    small = [
        pltpu.make_async_copy(src, dst, arrive.at[4 + k])
        for k, (src, dst) in enumerate(((hq, gq), (hd, gd), (hi, gi), (ho, go), (hv, gv)))
    ]
    for copy in coming + small:
        copy.start()
    for copy, after in zip(coming, going):
        copy.wait()
        after.start()
    for copy in small:
        copy.wait()
    for half in (0, 1):
        rows = slice(16 * half, 16 * half + 16)
        for hp in range(PAIRS):
            for which in range(3):
                column = 512 * which + 128 * hp
                o_qkv[0, rows, column : column + 128] = gq[hp, half, :, 128 * which : 128 * which + 128]
        o_d[0, rows, :] = gd[half]
        o_in[0, rows, :] = gi[half]
        o_out[0, 64 * half : 64 * half + 64, :] = go[half]

    def own(row, width):
        total = jnp.zeros((1, width), F32)
        for k in range(4):
            total = total + jnp.where(z == k, row[:, width * k : width * k + width], 0.0)
        return total

    for row, ref in enumerate((o_g1, o_b1, o_g2, o_b2, o_last)):
        ref[...] = own(gv[row : row + 1, :], 32)
    o_qkvb[...] = own(jnp.concatenate([gv[8 + k : 9 + k, :] for k in range(3)], axis=1), 96)
    o_inb[...] = gv[11:12, :]
    for copy in going:
        copy.wait()


def solution(mesh):
    rows = P(None, ("replica", "shard"), None)
    vector, matrix = P("section", "shard"), P("section", "shard", None)
    slabs = P("section", None, ("replica", "shard"), None)
    return jax.shard_map(
        body,
        mesh=mesh,
        in_specs=(
            rows, rows, rows, vector, vector, matrix, vector, matrix, vector, vector, matrix, vector, matrix, vector,
        ),
        out_specs=(
            slabs, slabs, vector, vector, matrix, vector, matrix, vector, vector, matrix, vector, matrix, vector,
        ),
        check_vma=False,
    )
```

```python
import math

import jax
import jax.numpy as jnp
from jax import lax
from jax.experimental import pallas as pl
from jax.experimental.pallas import tpu as pltpu
from jax.sharding import PartitionSpec as P

T = 768
D = 512
FF = 2048
HEADS = 8
HEAD = 64
ROT = 16
BLOCK = 128
SEQS = 4
TILE = 256
EPS = 1e-5
MASKED = -1e9
LOG2E = 1.0 / math.log(2.0)
LN2 = math.log(2.0)
MESH = pl.DeviceIdType.MESH
BF = jnp.bfloat16
F32 = jnp.float32

PAIRS = 4
DENSE, FIN, FOUT, VEC = 4, 5, 6, 7
PARTS = 8
LETTERS = "abcdDIOV"
HALF_ROWS = (16, 16, 16, 16, 16, 16, 64, 8)
WIDTH = (384, 384, 384, 384, 512, 2048, 512, 128)
KIND = (BF, BF, BF, BF, BF, BF, BF, F32)


def dg(a, b, ca, cb):
    return lax.dot_general(a, b, (((ca,), (cb,)), ((), ())), preferred_element_type=F32)


class Place:
    def __init__(self):
        self.s = lax.axis_index("section")
        self.y = lax.axis_index("replica")
        shard = lax.axis_index("shard")
        x, z = shard // 4, shard % 4
        self.shard, self.x, self.z = shard, x, z
        self.p = x + self.s * (z - x)
        self.q = z + self.s * (x - z)

    def at(self, p, q):
        return (1 - self.s) * (4 * p + q) + self.s * (4 * q + p)

    def sibling(self):
        return (1 - self.s, self.y, self.shard)

    def along_p(self, d):
        return (self.s, self.y, self.at((self.p + d) % 4, self.q))

    def along_q(self, d):
        return (self.s, self.y, self.at(self.p, (self.q + d) % 4))

    def along_y(self, d):
        return (self.s, (self.y + d) % 4, self.shard)


def remote(src, dst, send, recv, device):
    return pltpu.make_async_remote_copy(
        src_ref=src, dst_ref=dst, send_sem=send, recv_sem=recv, device_id=device, device_id_type=MESH
    )


class Gather:
    def __init__(self, me, layer, part, shard_ref, whole, send, recv, local):
        self.me, self.layer, self.part = me, layer, part
        self.shard_ref, self.w = shard_ref, whole
        self.send = lambda k: send.at[layer, part, k]
        self.recv = lambda k: recv.at[layer, part, k]
        self.local = local.at[part]
        self.rows = HALF_ROWS[part]
        self.direct = layer == 0 and part in (0, 1, 2, 3, VEC)
        self.ways = (1, 3, 2) if self.direct else (1, 3)

    def halves(self, h, target):
        if self.part == VEC:
            return [(self.shard_ref.at[h], target)]
        rows = pl.ds(pl.multiple_of(h * self.rows, self.rows), self.rows)
        if self.part < PAIRS:
            return [
                (
                    self.shard_ref.at[0, rows, pl.ds(512 * which + 128 * self.part, 128)],
                    target.at[:, pl.ds(128 * which, 128)],
                )
                for which in range(3)
            ]
        return [(self.shard_ref.at[0, rows, :], target)]

    def move(self, ref, sent, came, device):
        return remote(ref, ref, self.send(sent), self.recv(came), device)

    def shards(self, count):
        return self.move(self.w.at[self.me.s, pl.ds(0, count)], 1, 1, self.me.sibling())

    def row(self, half, p):
        return self.w.at[half, pl.ds(4 * p, 4)]

    def own(self, half, p, q):
        return self.w.at[half, 4 * p + q]

    def step0(self):
        me = self.me

        @pl.when(me.s == self.layer)
        def _():
            for src, dst in self.halves(me.s, self.own(me.s, me.p, me.q)):
                pltpu.make_async_copy(src, dst, self.local).start()
            for src, dst in self.halves(1 - me.s, self.own(1 - me.s, me.q, me.p)):
                remote(src, dst, self.send(0), self.recv(0), me.sibling()).start()

    def step1(self):
        me = self.me
        own = self.own(me.s, me.p, me.q)

        @pl.when(me.s == self.layer)
        def _():
            pltpu.make_async_copy(own, own, self.local).wait()

        @pl.when(me.s != self.layer)
        def _():
            self.move(own, 0, 0, me.sibling()).wait_recv()

        for d in (1, 3, 2):
            self.move(own, 1, 1, me.along_q(d)).start()

    def across(self, p):
        self.move(self.row(self.me.s, p), 2, 4, self.me.sibling()).start()

    def step2(self):
        me = self.me
        self.shards(3).wait_recv()
        for d in self.ways:
            self.move(self.row(me.s, me.p), 1, 2, me.along_p(d)).start()
        self.across(me.p)

    def step3(self):
        me = self.me
        ref = self.w.at[me.s, pl.ds(0, 4 * len(self.ways))]
        self.move(ref, 1, 2, me.sibling()).wait_recv()
        if not self.direct:
            for d in (1, 3):
                half = self.w.at[me.s, pl.ds(4 * ((me.p + 4 - d) % 4) + d - 1, 2)]
                self.move(half, 1, 3, me.along_p(d)).start()
        for d in self.ways:
            self.across((me.p + 4 - d) % 4)

    def step4(self):
        me = self.me
        if not self.direct:
            self.move(self.row(me.s, me.p), 1, 3, me.sibling()).wait_recv()
            self.across((me.p + 2) % 4)

    def step5(self):
        self.move(self.w.at[1 - self.me.s], 2, 4, self.me.sibling()).wait_recv()

    def finish(self):
        me = self.me

        @pl.when(me.s == self.layer)
        def _():
            self.move(self.own(1 - me.s, me.q, me.p), 0, 0, me.sibling()).wait_send()

        self.shards(15).wait_send()
        self.move(self.w.at[me.s], 2, 4, me.sibling()).wait_send()


class Reduce:
    def __init__(self, me, layer, part, terms, buffers, send, recv):
        self.me, self.layer, self.part = me, layer, part
        self.g = terms
        self.r, self.one, self.two, self.ys, self.f, self.out = buffers
        self.send = lambda k: send.at[layer, part, k]
        self.recv = lambda k: recv.at[layer, part, k]
        self.kind = KIND[part]

    def swap(self):
        me = self.me
        return remote(self.g.at[1 - me.s], self.r, self.send(0), self.recv(0), me.sibling())

    def first(self, d):
        me = self.me
        row = self.r.at[pl.ds(4 * ((me.p + d) % 4), 4)]
        return remote(row, self.one.at[d - 1], self.send(1), self.recv(1), me.along_p(d))

    def second(self, d):
        me = self.me
        shard = self.r.at[4 * me.p + (me.q + d) % 4]
        return remote(shard, self.two.at[d - 1], self.send(2), self.recv(2), me.along_q(d))

    def third(self, d):
        me = self.me
        return remote(self.ys.at[me.y], self.ys.at[me.y], self.send(3), self.recv(3), me.along_y(d))

    def all_of(self, ref, k):
        return remote(ref, ref, self.send(k), self.recv(k), self.me.sibling())

    def back(self):
        me = self.me
        return remote(self.f, self.out.at[me.s], self.send(4), self.recv(4), me.sibling())

    def step0(self):
        self.swap().start()

    def step1(self):
        me = self.me
        self.swap().wait_recv()

        def one(k, c):
            self.r[k] = (self.r[k].astype(F32) + self.g[me.s, k].astype(F32)).astype(self.kind)
            return c

        lax.fori_loop(0, 16, one, 0)
        for d in (1, 3, 2):
            self.first(d).start()
        self.swap().wait_send()

    def step2(self):
        me = self.me
        self.all_of(self.one, 1).wait_recv()

        def one(b, c):
            total = self.r[4 * me.p + b].astype(F32) + self.one[0, b].astype(F32)
            total = total + (self.one[1, b].astype(F32) + self.one[2, b].astype(F32))
            self.r[4 * me.p + b] = total.astype(self.kind)
            return c

        lax.fori_loop(0, 4, one, 0)
        for d in (1, 3, 2):
            self.second(d).start()

    def step3(self):
        me = self.me
        self.all_of(self.two, 2).wait_recv()
        total = self.r[4 * me.p + me.q].astype(F32) + self.two[0].astype(F32)
        total = total + (self.two[1].astype(F32) + self.two[2].astype(F32))
        self.ys[me.y] = total.astype(self.kind)
        for d in (1, 3, 2):
            self.third(d).start()

    def step4(self):
        me = self.me
        self.all_of(self.ys.at[pl.ds(0, 3)], 3).wait_recv()
        total = (self.ys[0].astype(F32) + self.ys[1].astype(F32)) + (
            self.ys[2].astype(F32) + self.ys[3].astype(F32)
        )

        @pl.when(me.s == self.layer)
        def _():
            self.out[me.s] = total

        @pl.when(me.s != self.layer)
        def _():
            self.f[...] = total
            self.back().start()

    def step5(self):
        me = self.me

        @pl.when(me.s == self.layer)
        def _():
            self.all_of(self.out.at[1 - me.s], 4).wait_recv()

    def finish(self):
        self.all_of(self.one, 1).wait_send()
        self.all_of(self.two, 2).wait_send()
        self.all_of(self.ys.at[pl.ds(0, 3)], 3).wait_send()

        @pl.when(self.me.s != self.layer)
        def _():
            self.back().wait_send()


class ReduceVectors:
    def __init__(self, me, layer, terms, buffers, send, recv):
        self.me, self.layer, self.g = me, layer, terms
        self.r, self.one, self.ys, self.out = buffers
        self.send = lambda k: send.at[layer, VEC, k]
        self.recv = lambda k: recv.at[layer, VEC, k]

    def swap(self):
        return remote(self.g, self.r, self.send(0), self.recv(0), self.me.sibling())

    def first(self, k):
        x, z = (self.me.x + k // 4) % 4, (self.me.z + k % 4) % 4
        device = (self.me.s, self.me.y, 4 * x + z)
        return remote(self.r.at[x, z], self.one.at[k], self.send(1), self.recv(1), device)

    def all_first(self):
        ref = self.one.at[pl.ds(1, 15)]
        return remote(ref, ref, self.send(1), self.recv(1), self.me.sibling())

    def third(self, d):
        me = self.me
        return remote(self.ys.at[me.y], self.ys.at[me.y], self.send(3), self.recv(3), me.along_y(d))

    def all_third(self):
        ref = self.ys.at[pl.ds(0, 3)]
        return remote(ref, ref, self.send(3), self.recv(3), self.me.sibling())

    def owner(self, step):
        pl.when(self.me.s == self.layer)(step)

    def step0(self):
        @pl.when(self.me.s != self.layer)
        def _():
            self.swap().start()

    def step1(self):
        def step():
            self.swap().wait_recv()
            self.r[...] += self.g[...]
            for k in (1, 4, 3, 12, 5, 7, 13, 15, 2, 8, 6, 9, 11, 14, 10):
                self.first(k).start()

        self.owner(step)

        @pl.when(self.me.s != self.layer)
        def _():
            self.swap().wait_send()

    def step2(self):
        def step():
            self.all_first().wait_recv()
            total = self.r[self.me.x, self.me.z]
            for k in range(1, 16):
                total = total + self.one[k]
            self.ys[self.me.y] = total
            for d in (1, 3, 2):
                self.third(d).start()

        self.owner(step)

    def step3(self):
        def step():
            self.all_third().wait_recv()
            self.out[...] = (self.ys[0] + self.ys[1]) + (self.ys[2] + self.ys[3])

        self.owner(step)

    def step5(self):
        pass

    def finish(self):
        def step():
            self.all_first().wait_send()
            self.all_third().wait_send()

        self.owner(step)


def natural_rows(ref, columns):
    pieces = []
    for x in range(4):
        for z in range(4):
            pieces.append(ref[0, 4 * x + z, :, columns])
            pieces.append(ref[1, 4 * z + x, :, columns])
    return jnp.concatenate(pieces, axis=0)


def group_rows(ref, x):
    pieces = []
    for z in range(4):
        pieces.append(ref[0, 4 * x + z])
        pieces.append(ref[1, 4 * z + x])
    return jnp.concatenate(pieces, axis=0)


def put_natural(ref, columns, value):
    for x in range(4):
        for z in range(4):
            row = 32 * (4 * x + z)
            ref[0, 4 * x + z, :, columns] = value[row : row + 16]
            ref[1, 4 * z + x, :, columns] = value[row + 16 : row + 32]


def put_group(ref, x, value, rows):
    for z in range(4):
        row = 2 * rows * z
        ref[0, 4 * x + z] = value[row : row + rows]
        ref[1, 4 * z + x] = value[row + rows : row + 2 * rows]


def to_column(row):
    here = lax.broadcasted_iota(jnp.int32, (128, 128), 0) == lax.broadcasted_iota(
        jnp.int32, (128, 128), 1
    )
    return jnp.sum(jnp.where(here, row, 0.0), axis=1, keepdims=True)


def turn(rows, cosine, sine):
    pieces = []
    for e in (0, 64):
        low, high = rows[e : e + 8], rows[e + 8 : e + 16]
        pieces += [low * cosine - high * sine, high * cosine + low * sine, rows[e + 16 : e + 64]]
    return jnp.concatenate(pieces, axis=0)


def columns(start, size):
    return pl.ds(pl.multiple_of(start, size), size)


def loop(count, step):
    def one(k, c):
        step(k)
        return c

    lax.fori_loop(0, count, one, 0)


def kernel(
    lengths,
    x_ref,
    cot_ref,
    wq_ref,
    wd_ref,
    wi_ref,
    wo_ref,
    gain1_ref,
    shift1_ref,
    gain2_ref,
    shift2_ref,
    last_ref,
    qkvb_ref,
    finb_ref,
    act_out,
    ig_out,
    gq_out,
    gd_out,
    gi_out,
    go_out,
    gv_out,
    st_qkv,
    st_p0,
    st_p1,
    st_p2,
    st_bt,
    st_rinv,
    st_act,
    st_slo,
    st_n1t,
    st_n2,
    *scratch,
):
    scratch = list(scratch)

    def take(count):
        taken, scratch[:count] = scratch[:count], []
        return taken

    def take_parts(count=4):
        pairs, *rest = take(count)
        return [pairs] + [pairs.at[k] for k in range(PAIRS)] + rest

    (wq0, *w0), (wq1, *w1) = take_parts(5), take_parts(5)
    w, wq = (w0, w1), (wq0, wq1)
    gq, *g = take_parts()
    r, one, two, ys = [(take_parts(), take_parts()) for _ in range(4)]
    rq = [parts.pop(0) for parts in r]
    for both in (one, two, ys):
        for parts in both:
            parts.pop(0)
    f = take_parts()[1:]
    gvec, *rvec = take(3)
    vecs, yvec, (vsrc, vrow) = take(2), take(2), take(2)
    hid, grad, n1t, n2, acc, carried = take(6)
    qkvt, p0, p1, p2, bt, rinv, act, slo = take(8)
    d0, d1, d2, scores_one = take(4)
    dn1 = n2
    vd, vq, vf, dvec, fvec, live, bias, cos_ref, sin_ref = take(9)
    sends, ag_recv, rs_recv, ag_local, sems, ex_send, ex_recv = take(7)
    probs = (p0, p1, p2)
    dscores = (d0, d1, d2)
    outs = [gq_out.at[k] for k in range(PAIRS)] + [gd_out, gi_out, go_out]
    shards = [wq_ref] * PAIRS + [wd_ref, wi_ref, wo_ref, vsrc]

    me = Place()
    s = me.s
    barrier = pltpu.get_barrier_semaphore()
    partners = [me.sibling()]
    for d in (1, 2, 3):
        partners += [me.along_q(d), me.along_p(d), me.along_y(d)]
        for e in (1, 2, 3):
            partners.append((s, me.y, 4 * ((me.x + d) % 4) + (me.z + e) % 4))
    for device in partners:
        pl.semaphore_signal(barrier, inc=1, device_id=device, device_id_type=MESH)
    pl.semaphore_wait(barrier, len(partners))

    gather = [
        [Gather(me, l, c, shards[c], w[l][c], sends, ag_recv, ag_local) for c in range(PARTS)]
        for l in (0, 1)
    ]
    reduce = [
        [
            Reduce(
                me, l, c, g[c], (r[l][c], one[l][c], two[l][c], ys[l][c], f[c], outs[c]), sends, rs_recv
            )
            for c in range(VEC)
        ]
        + [ReduceVectors(me, l, gvec, (rvec[l], vecs[l], yvec[l], gv_out), sends, rs_recv)]
        for l in (0, 1)
    ]

    def fetch(*plan):
        for word in plan:
            item = gather[int(word[0])][LETTERS.index(word[1])]
            getattr(item, "step" + word[2])()

    def back_pairs(l, first):
        def step(k):
            hp = first + k
            back_attend(l, hp)
            back_qkv(hp)
            remote(
                gq.at[hp, 1 - s], rq[l].at[hp], sends.at[l, hp, 0], rs_recv.at[l, hp, 0], me.sibling()
            ).start()

        loop(2, step)

    def send(*plan):
        for word in plan:
            item = reduce[int(word[0])][LETTERS.index(word[1])]
            getattr(item, "step" + word[2])()

    vsrc[...] = jnp.zeros((2, 8, 128), F32)
    for k in range(4):
        here = me.z == k
        for row, ref in enumerate((gain1_ref, shift1_ref, gain2_ref, shift2_ref, last_ref)):
            vsrc[0, row : row + 1, 32 * k : 32 * k + 32] = jnp.where(here, ref[...].astype(F32), 0.0)
        vrow[0:1, 96 * k : 96 * k + 96] = jnp.where(here, qkvb_ref[...].astype(F32), 0.0)
    for k in range(3):
        vsrc[1, k : k + 1, :] = vrow[0:1, 128 * k : 128 * k + 128]
    vsrc[1, 3:4, :] = finb_ref[...].astype(F32)

    x_in = pltpu.make_async_copy(x_ref.at[s], hid.at[0], sems.at[0])
    cot_in = pltpu.make_async_copy(cot_ref.at[s], grad.at[0], sems.at[1])
    x_in.start()
    fetch("0V0", "0a0", "0b0", "0c0", "0d0", "0I0", "0D0", "0O0", "1V0", "1a0", "1b0", "1c0", "1d0", "1I0", "1D0", "1O0")
    fetch("0V1", "0a1", "0b1", "0c1", "0d1", "0D1", "0I1", "0O1")
    cot_in.start()

    starts, ends, at = [], [], jnp.int32(0)
    for k in range(SEQS):
        size = lengths[s, 0, k]
        starts.append(at)
        ends.append(at + size)
        at = at + (size + BLOCK - 1) // BLOCK * BLOCK

    def inside(places):
        return [(places >= a) & (places < b) for a, b in zip(starts, ends)]

    def live_tile(k):
        places = lax.broadcasted_iota(jnp.int32, (TILE, 1), 0) + k * TILE
        total = jnp.zeros((TILE, 1), F32)
        for found in inside(places):
            total = total + jnp.where(found, 1.0, 0.0)
        live[columns(k * TILE, TILE), :] = total

    loop(3, live_tile)
    places = lax.broadcasted_iota(jnp.int32, (8, T), 1)
    begin = jnp.zeros((8, T), jnp.int32)
    offset = jnp.zeros((8, T), jnp.int32)
    for found, a in zip(inside(places), starts):
        begin = begin + jnp.where(found, a, 0)
        offset = offset + jnp.where(found, places - a, 0)
    rates = jnp.exp(
        lax.broadcasted_iota(jnp.int32, (8, T), 0).astype(F32) * (-2.0 * math.log(10000.0) / ROT)
    )
    angles = offset.astype(F32) * rates
    cos_ref[...] = jnp.cos(angles)
    sin_ref[...] = jnp.sin(angles)
    for j in range(3):
        for i in range(j + 1):
            keys = lax.broadcasted_iota(jnp.int32, (TILE, TILE), 0) + i * TILE
            queries = lax.broadcasted_iota(jnp.int32, (TILE, TILE), 1) + j * TILE
            fits = (keys >= begin[0:1, j * TILE : (j + 1) * TILE]) & (keys <= queries)
            bias[j * (j + 1) // 2 + i] = jnp.where(fits, 0.0, MASKED)

    def unpack(l):
        ref = w[l][VEC]
        for x in range(4):
            vd[:, 128 * x : 128 * x + 128] = (ref[0, 4 * x] + ref[0, 4 * x + 1]) + (
                ref[0, 4 * x + 2] + ref[0, 4 * x + 3]
            )
            group = (ref[1, x] + ref[1, 4 + x]) + (ref[1, 8 + x] + ref[1, 12 + x])
            for k in range(3):
                vq[3 * x + k : 3 * x + k + 1, :] = group[k : k + 1]
            for z in range(4):
                vf[x : x + 1, 128 * z : 128 * z + 128] = ref[1, 4 * z + x][3:4]

    def normed(l, rows):
        v = hid[l, rows, :].astype(F32)
        centred = v - jnp.mean(v, axis=1, keepdims=True)
        scale = lax.rsqrt(jnp.mean(centred * centred, axis=1, keepdims=True) + EPS)
        return centred * scale, scale

    def norms(l):
        def tile(k):
            rows = columns(k * TILE, TILE)
            u, _ = normed(l, rows)
            n1t[:, rows] = (u * vd[0:1, :] + vd[1:2, :]).astype(BF).T
            n2[rows, :] = (u * vd[2:3, :] + vd[3:4, :]).astype(BF)

        loop(3, tile)

    def project(l, hp):
        value = dg(natural_rows(wq[l].at[hp], slice(0, 384)), n1t[...], 0, 0)
        pair = []
        for which in range(3):
            part = value[128 * which : 128 * which + 128] + to_column(vq[pl.ds(which * 4 + hp, 1), :])
            if which < 2:
                part = turn(part, cos_ref[...], sin_ref[...])
            if which == 0:
                part = part * (LOG2E / 8.0)
            pair.append(part.astype(BF))
            qkvt[columns(hp * 384 + which * 128, 128), :] = pair[which]
        return pair

    def score_block(e, k):
        if e:
            return scores_one.at[k]
        return acc.at[pl.ds(TILE * (k // 2), TILE), pl.ds(TILE * (k % 2), TILE)]

    def attend(l, hp):
        pair = project(l, hp)
        keys = pair[1].T
        blank = jnp.zeros((HEAD, T), BF)
        peaks = ([None] * 3, [None] * 3)
        for e in (0, 1):
            mine = pair[0][e * HEAD : (e + 1) * HEAD]
            mine = jnp.concatenate([mine, blank] if e == 0 else [blank, mine], axis=0)
            for i in range(3):
                for j in range(i, 3):
                    k = j * (j + 1) // 2 + i
                    scores = dg(keys[i * TILE : (i + 1) * TILE], mine[:, j * TILE : (j + 1) * TILE], 1, 0)
                    scores = scores + bias[k]
                    score_block(e, k)[...] = scores
                    peak = jnp.max(scores, axis=0, keepdims=True)
                    peaks[e][j] = peak if i == 0 else jnp.maximum(peaks[e][j], peak)
        for e in (0, 1):
            h = 2 * hp + e
            value = jnp.concatenate([pair[2][e * HEAD : (e + 1) * HEAD], jnp.ones((8, T), BF)], axis=0)
            for j in range(3):
                at_j = slice(j * TILE, (j + 1) * TILE)
                blended = jnp.zeros((HEAD + 8, TILE), F32)
                for i in range(j + 1):
                    raised = jnp.exp2(score_block(e, j * (j + 1) // 2 + i)[...] - peaks[e][j]).astype(BF)
                    probs[i][h, :, (j - i) * TILE : (j - i + 1) * TILE] = raised
                    blended = blended + dg(value[:, i * TILE : (i + 1) * TILE], raised, 1, 0)
                inverse = 1.0 / blended[HEAD : HEAD + 1]
                rinv[pl.ds(h, 1), at_j] = inverse
                bt[columns(hp * 128 + e * HEAD, HEAD), at_j] = (blended[:HEAD] * inverse).astype(BF)

    def widen(l, c):
        cols = columns(c * 512, 512)
        weight = natural_rows(w[l][FIN], cols)
        shift = vf[pl.ds(c, 1), :]

        def tile(k):
            rows = columns(k * TILE, TILE)
            v = dg(n2[rows, :], weight, 1, 0) + shift
            below = 0.5 + 0.5 * lax.erf(v * (1.0 / math.sqrt(2.0)))
            act[rows, cols] = (v * below).astype(BF)
            slope = below + v * (jnp.exp(-0.5 * v * v) * (1.0 / math.sqrt(2.0 * math.pi)))
            slo[rows, cols] = slope.astype(BF)

        for k in range(3):
            tile(k)

    def join(l):
        def part(t):
            cols = columns(t * TILE, TILE)
            weight = jnp.concatenate(
                [
                    piece
                    for x in range(4)
                    for z in range(4)
                    for piece in (w[l][FOUT][0, 4 * x + z, :, cols], w[l][FOUT][1, 4 * z + x, :, cols])
                ],
                axis=0,
            )
            total = dg(act[...], weight, 1, 0)
            total = total + dg(bt[...], natural_rows(w[l][DENSE], cols), 0, 0)
            total = total + hid[l, :, cols].astype(F32) + vd[4:5, cols]
            hid[l + 1, :, cols] = (total * live[...]).astype(BF)

        loop(2, part)

    def local(src, dst, k):
        return pltpu.make_async_copy(src, dst, sems.at[k])

    attention_kept = [
        (qkvt, st_qkv, 2),
        (p0, st_p0, 3),
        (p1, st_p1, 4),
        (p2, st_p2, 5),
        (bt, st_bt, 6),
        (rinv, st_rinv, 7),
    ]
    norms_kept = [(n1t, st_n1t, 12), (n2, st_n2, 13)]
    wide_kept = [(act, st_act, 8), (slo, st_slo, 9)]

    fetch("0V2", "0a2", "0b2", "0c2", "0d2")
    x_in.wait()
    fetch("0V3", "0a3")
    fetch("0D2", "0I2")
    fetch("0V5")
    unpack(0)
    norms(0)
    for a, b, k in norms_kept:
        local(a, b, k).start()
    fetch("0b3", "0O2", "0a5")
    fetch("0c3", "0b5")
    loop(2, lambda hp: attend(0, hp))
    fetch("0d3", "0c5")
    fetch("0D3", "0I3")
    fetch("1V1", "1a1", "1b1", "1c1", "1d1", "0d5")
    loop(2, lambda hp: attend(0, hp + 2))
    for a, b, k in attention_kept:
        local(a, b, k).start()
    fetch("0O3")
    fetch("1I1", "1D1", "1O1")
    fetch("0D4", "0I4", "1V2", "1a2", "1b2")
    fetch("0I5")
    loop(2, lambda c: widen(0, c))
    fetch("0O4")
    fetch("1c2", "1d2", "1V3", "1a3")
    loop(2, lambda c: widen(0, c + 2))
    fetch("1b3", "1c3", "1d3", "1I2", "1D2", "1O2", "0D5", "0O5")
    join(0)
    for a, b, k in wide_kept:
        local(a, b, k).start()

    fetch("1V4", "1a4", "1b4")
    fetch("1V5")
    unpack(1)
    for a, b, k in norms_kept:
        local(a, b, k).wait()
    norms(1)
    fetch("1c4", "1d4", "1a5", "1b5")
    for a, b, k in attention_kept:
        local(a, b, k).wait()
    loop(2, lambda hp: attend(1, hp))
    fetch("1I3", "1D3", "1c5", "1d5")
    loop(2, lambda hp: attend(1, hp + 2))
    fetch("1O3", "1I4", "1D4")
    fetch("1I5")
    for a, b, k in wide_kept:
        local(a, b, k).wait()
    loop(2, lambda c: widen(1, c))
    fetch("1O4")
    loop(2, lambda c: widen(1, c + 2))
    fetch("1D5", "1O5")
    join(1)
    for l in (0, 1):
        for c in range(PARTS):
            gather[l][c].finish()
    act_mine = local(hid.at[1 + s], act_out.at[s], 10)
    act_theirs = remote(hid.at[2 - s], act_out.at[s], ex_send.at[0], ex_recv.at[0], me.sibling())
    act_mine.start()
    act_theirs.start()
    cot_in.wait()

    def start_back(l):
        def tile(k):
            rows = columns(k * TILE, TILE)
            v = grad[1 - l, rows, :].astype(F32) * live[rows, :]
            carried[rows, :] = v.astype(BF)
            here = jnp.sum(v, axis=0, keepdims=True)
            dvec[4:5, :] = here + jnp.where(k == 0, 0.0, dvec[4:5, :])

        dvec[...] = jnp.zeros((8, D), F32)
        loop(3, tile)

    def back_out(c):
        cols = columns(c * 512, 512)
        put_group(g[FOUT], c, dg(act[:, cols], carried[...], 0, 0).astype(BF), 64)

    def back_wide(l, c):
        cols = columns(c * 512, 512)
        weight = group_rows(w[l][FOUT], c)
        total = jnp.zeros((1, 512), F32)
        for k in range(3):
            rows = slice(k * TILE, (k + 1) * TILE)
            v = dg(carried[rows, :], weight, 1, 1) * slo[rows, cols].astype(F32)
            v = v.astype(BF)
            slo[rows, cols] = v
            total = total + jnp.sum(v.astype(F32), axis=0, keepdims=True)
        fvec[pl.ds(c, 1), :] = total

    def back_in(l, c):
        cols = columns(c * 512, 512)
        put_natural(g[FIN], cols, dg(n2[...], slo[:, cols], 0, 0).astype(BF))

    def back_norm_two(l, t):
        low = w[l][FIN][0, pl.ds(8 * t, 8)]
        high = [w[l][FIN][1, pl.ds(4 * z + 2 * t, 2)] for z in range(4)]
        pieces = []
        for x in range(2):
            for z in range(4):
                pieces += [low[4 * x + z], high[z][x]]
        acc[:, columns(t * TILE, TILE)] = dg(slo[...], jnp.concatenate(pieces, axis=0), 1, 1)

    def back_dense(l):
        put_natural(g[DENSE], slice(0, 512), dg(bt[...], carried[...], 1, 0).astype(BF))

    def back_attend(l, hp):
        weight = group_rows(w[l][DENSE], hp)
        below = dg(weight, carried[...], 1, 1)
        queries = qkvt[columns(hp * 384, 128), :]
        keys = qkvt[columns(hp * 384 + 128, 128), :]
        values = qkvt[columns(hp * 384 + 256, 128), :].T
        blended = bt[columns(hp * 128, 128), :].astype(F32)
        blank = jnp.zeros((HEAD, TILE), BF)
        downs = []
        for e in (0, 1):
            h = 2 * hp + e
            down = below[e * HEAD : (e + 1) * HEAD] * rinv[pl.ds(h, 1), :]
            centre = jnp.sum(down * blended[e * HEAD : (e + 1) * HEAD], axis=0, keepdims=True)
            down = down.astype(BF)
            downs.append(down)
            for j in range(3):
                at_j = slice(j * TILE, (j + 1) * TILE)
                mine = down[:, at_j]
                mine = jnp.concatenate([mine, blank] if e == 0 else [blank, mine], axis=0)
                for i in range(j + 1):
                    cols = slice((j - i) * TILE, (j - i + 1) * TILE)
                    slope = dg(values[i * TILE : (i + 1) * TILE], mine, 1, 0) - centre[:, at_j]
                    slope = slope * probs[i][h, :, cols].astype(F32)
                    dscores[i][e, :, cols] = slope.astype(BF)
        done = []
        for e in (0, 1):
            h = 2 * hp + e
            query = queries[e * HEAD : (e + 1) * HEAD]
            key = keys[e * HEAD : (e + 1) * HEAD]
            grad_query, grad_key, grad_value = [], [], []
            for j in range(3):
                total = jnp.zeros((HEAD, TILE), F32)
                for i in range(j + 1):
                    cols = slice((j - i) * TILE, (j - i + 1) * TILE)
                    total = total + dg(key[:, i * TILE : (i + 1) * TILE], dscores[i][e, :, cols], 1, 0)
                grad_query.append(total * 0.125)
            for i in range(3):
                grad_key.append(dg(query[:, i * TILE :], dscores[i][e], 1, 1) * LN2)
                grad_value.append(dg(downs[e][:, i * TILE :], probs[i][h], 1, 1))
            done.append(
                [jnp.concatenate(pieces, axis=1) for pieces in (grad_query, grad_key, grad_value)]
            )
        for which in range(3):
            value = jnp.concatenate([done[0][which], done[1][which]], axis=0)
            if which < 2:
                value = turn(value, cos_ref[...], -sin_ref[...])
            qkvt[columns(hp * 384 + which * 128, 128), :] = value.astype(BF)

    def back_qkv(hp):
        value = dg(n1t[...], qkvt[columns(hp * 384, 384), :], 1, 1)
        put_natural(gq.at[hp], slice(0, 384), value.astype(BF))

    def back_norm_one(l, t):
        weight = jnp.concatenate([group_rows(wq[l].at[hp], t) for hp in range(PAIRS)], axis=1)
        dn1[:, columns(t * 128, 128)] = dg(weight, qkvt[...], 1, 0).astype(BF).T

    def add_sums(u, first, second):
        dvec[0:1, :] += jnp.sum(first * u, axis=0, keepdims=True)
        dvec[1:2, :] += jnp.sum(first, axis=0, keepdims=True)
        dvec[2:3, :] += jnp.sum(second * u, axis=0, keepdims=True)
        dvec[3:4, :] += jnp.sum(second, axis=0, keepdims=True)

    def norm_sums(l):
        def tile(k):
            rows = columns(k * TILE, TILE)
            add_sums(normed(l, rows)[0], dn1[rows, :].astype(F32), acc[rows, :])

        loop(3, tile)

    def end_back(l, with_sums):
        def tile(k):
            rows = columns(k * TILE, TILE)
            u, scale = normed(l, rows)
            first = dn1[rows, :].astype(F32)
            second = acc[rows, :]
            if with_sums:
                add_sums(u, first, second)
            total = first * vd[0:1, :] + second * vd[2:3, :]
            centre = jnp.mean(total, axis=1, keepdims=True)
            along = jnp.mean(total * u, axis=1, keepdims=True)
            total = carried[rows, :].astype(F32) + scale * (total - centre - u * along)
            grad[l, rows, :] = total.astype(BF)

        loop(3, tile)

    def put_biases():
        sums = dg(jnp.ones((8, T), BF), qkvt[...], 1, 1)
        for x in range(4):
            for k in range(3):
                which, hp = divmod(3 * x + k, PAIRS)
                row = 384 * hp + 128 * which
                vq[3 * x + k : 3 * x + k + 1, :] = sums[0:1, row : row + 128]
        for x in range(4):
            rest = jnp.concatenate([vq[3 * x : 3 * x + 3, :], jnp.zeros((5, 128), F32)], axis=0)
            for z in range(4):
                gvec[x, z, 8:16] = rest
                gvec[x, z, 11:12] = fvec[x : x + 1, 128 * z : 128 * z + 128]

    def put_norms():
        for x in range(4):
            for z in range(4):
                gvec[x, z, 0:8] = dvec[:, 128 * x : 128 * x + 128]

    restored = ((qkvt, st_qkv, 2), (p0, st_p0, 3), (p1, st_p1, 4), (p2, st_p2, 5), (bt, st_bt, 6), (rinv, st_rinv, 7))

    start_back(1)
    loop(4, back_out)
    send("1O0")
    loop(4, lambda c: back_wide(1, c))
    send("1O1")
    loop(4, lambda c: back_in(1, c))
    send("1I0")
    loop(2, lambda t: back_norm_two(1, t))
    local(st_act, act, 8).start()
    local(st_slo, slo, 9).start()
    back_dense(1)
    send("1D0", "1I1")
    back_pairs(1, 0)
    send("1D1", "1a1", "1O2")
    back_pairs(1, 2)
    local(st_n1t, n1t, 12).start()
    send("1b1", "1c1", "1I2")
    loop(4, lambda t: back_norm_one(1, t))
    send("1d1", "1D2", "1O3")
    put_biases()
    for a, b, k in restored:
        local(b, a, k).start()
    end_back(1, True)
    put_norms()
    send("1V0", "1a2")
    local(st_n2, n2, 13).start()

    unpack(0)
    start_back(0)
    local(st_act, act, 8).wait()
    local(st_slo, slo, 9).wait()
    send("1b2", "1I3")
    loop(4, back_out)
    send("0O0", "1V1", "1D3", "1c2", "1d2", "1a3")
    loop(4, lambda c: back_wide(0, c))
    send("0O1", "1O4", "1b3")
    local(st_n2, n2, 13).wait()
    loop(4, lambda c: back_in(0, c))
    send("0I0", "1V2", "1c3", "1d3", "1D4")
    loop(2, lambda t: back_norm_two(0, t))
    send("0I1", "1I4", "1a4", "1b4")
    for a, b, k in restored:
        local(b, a, k).wait()
    local(st_n1t, n1t, 12).wait()
    back_dense(0)
    send("0D0")
    back_attend(0, 0)
    back_qkv(0)
    send("0a0", "0D1", "1V3", "1c4", "1d4")
    back_attend(0, 1)
    back_qkv(1)
    send("0b0", "0a1", "0O2")
    back_attend(0, 2)
    back_qkv(2)
    send("0c0", "0b1")
    back_attend(0, 3)
    back_qkv(3)
    send("0d0", "0c1")
    put_biases()
    send("0I2", "0D2", "0a2", "0O3")
    loop(2, lambda t: back_norm_one(0, t))
    send("0d1", "0b2")
    loop(2, lambda t: back_norm_one(0, t + 2))
    norm_sums(0)
    put_norms()
    send("0V0")
    send("0I3")
    send("0V1")
    send("0c2", "0d2")
    end_back(0, False)
    grad_mine = local(grad.at[s], ig_out.at[s], 11)
    grad_theirs = remote(grad.at[1 - s], ig_out.at[s], ex_send.at[1], ex_recv.at[1], me.sibling())
    grad_mine.start()
    grad_theirs.start()
    send("0D3", "0a3", "0b3", "0O4")
    send("0c3", "0d3")
    send("0V2")
    send("0D4", "0a4", "0b4")
    send("0I4")
    send("0c4", "0d4")
    send("0V3")
    for l in (1, 0):
        for c in range(PARTS):
            reduce[l][c].step5()
            reduce[l][c].finish()
    act_mine.wait()
    act_theirs.wait_send()
    remote(hid.at[2 - s], act_out.at[1 - s], ex_send.at[0], ex_recv.at[0], me.sibling()).wait_recv()
    grad_mine.wait()
    grad_theirs.wait_send()
    remote(grad.at[1 - s], ig_out.at[1 - s], ex_send.at[1], ex_recv.at[1], me.sibling()).wait_recv()


def scratch_shapes():
    def parts(lead, kind=None):
        return [pltpu.VMEM((PAIRS, *lead, HALF_ROWS[0], WIDTH[0]), kind or BF)] + [
            pltpu.VMEM((*lead, HALF_ROWS[c], WIDTH[c]), kind or KIND[c]) for c in range(PAIRS, PARTS)
        ]

    shapes = []
    for _ in (0, 1):
        shapes += parts((2, 16))
    for lead in ((2, 16), (16,), (16,), (3, 4), (3, 4), (3,), (3,), (4,), (4,)):
        shapes += parts(lead)[:-1]
    shapes += parts((), F32)[:-1]
    for lead in ((4, 4), (4, 4), (4, 4), (16,), (16,), (4,), (4,)):
        shapes.append(pltpu.VMEM((*lead, 16, 128), F32))
    shapes += [pltpu.VMEM((2, 8, 128), F32), pltpu.VMEM((8, 384), F32)]
    shapes += [
        pltpu.VMEM((3, T, D), BF),
        pltpu.VMEM((2, T, D), BF),
        pltpu.VMEM((D, T), BF),
        pltpu.VMEM((T, D), BF),
        pltpu.VMEM((T, D), F32),
        pltpu.VMEM((T, D), BF),
    ]
    shapes += [pltpu.VMEM(shape, kind) for shape, kind in KEPT[:8]]
    shapes += [
        pltpu.VMEM((2, TILE, 768), BF),
        pltpu.VMEM((2, TILE, 512), BF),
        pltpu.VMEM((2, TILE, 256), BF),
        pltpu.VMEM((6, TILE, TILE), F32),
    ]
    shapes += [
        pltpu.VMEM((8, D), F32),
        pltpu.VMEM((16, 128), F32),
        pltpu.VMEM((8, 512), F32),
        pltpu.VMEM((8, D), F32),
        pltpu.VMEM((8, 512), F32),
        pltpu.VMEM((T, 1), F32),
        pltpu.VMEM((6, TILE, TILE), F32),
        pltpu.VMEM((8, T), F32),
        pltpu.VMEM((8, T), F32),
    ]
    dma = pltpu.SemaphoreType.DMA
    shapes += [dma((2, PARTS, 5))] * 3
    shapes += [dma((PARTS,)), dma((14,)), dma((2,)), dma((2,))]
    return shapes


KEPT = (
    ((3 * D, T), BF),
    ((HEADS, TILE, 768), BF),
    ((HEADS, TILE, 512), BF),
    ((HEADS, TILE, 256), BF),
    ((D, T), BF),
    ((HEADS, T), F32),
    ((T, FF), BF),
    ((T, FF), BF),
    ((D, T), BF),
    ((T, D), BF),
)


def body(
    inputs,
    cotangent,
    lengths,
    norm1_gain,
    norm1_bias,
    qkv_weight,
    qkv_bias,
    dense_weight,
    norm2_gain,
    norm2_bias,
    fc_in_weight,
    fc_in_bias,
    fc_out_weight,
    out_bias,
):
    hbm = pl.BlockSpec(memory_space=pl.ANY)
    vmem = pl.BlockSpec(memory_space=pltpu.VMEM)
    shape = jax.ShapeDtypeStruct
    results = pl.pallas_call(
        kernel,
        out_shape=[shape((2, T, D), BF), shape((2, T, D), BF), shape((PAIRS, 2, 16, 384), F32)]
        + [shape((2, HALF_ROWS[c], WIDTH[c]), F32) for c in range(PAIRS, VEC)]
        + [shape((16, 128), F32)]
        + [shape(s, k) for s, k in KEPT],
        in_specs=[pl.BlockSpec(memory_space=pltpu.SMEM)] + [hbm] * 6 + [vmem] * 7,
        out_specs=[hbm] * 2 + [vmem] * 5 + [hbm] * len(KEPT),
        scratch_shapes=scratch_shapes(),
        compiler_params=pltpu.CompilerParams(
            collective_id=0, has_side_effects=True, vmem_limit_bytes=64 * 1024 * 1024
        ),
        name="layers",
    )(
        lengths,
        inputs,
        cotangent,
        qkv_weight,
        dense_weight,
        fc_in_weight,
        fc_out_weight,
        norm1_gain,
        norm1_bias,
        norm2_gain,
        norm2_bias,
        out_bias,
        qkv_bias,
        fc_in_bias,
    )
    vector, slab = shape((1, 32), F32), shape((1, 2, T, D), BF)
    return pl.pallas_call(
        hand_out,
        out_shape=[slab, slab, vector, vector, shape((1, 32, 1536), F32), shape((1, 96), F32)]
        + [shape((1, 32, 512), F32), vector, vector, shape((1, 32, 2048), F32), shape((1, 128), F32)]
        + [shape((1, 128, 512), F32), vector],
        in_specs=[hbm] * 7,
        out_specs=[hbm] * 2 + [vmem] * 11,
        scratch_shapes=[pltpu.VMEM((4, T, D), BF)]
        + [pltpu.VMEM(r.shape, r.dtype) for r in results[2:7]]
        + [pltpu.SemaphoreType.DMA((9,)), pltpu.SemaphoreType.DMA((4,))],
        compiler_params=pltpu.CompilerParams(vmem_limit_bytes=60 * 1024 * 1024),
        name="hand_out",
    )(*results[:7])


def hand_out(
    act, ig, hq, hd, hi, ho, hv, o_act, o_ig, o_g1, o_b1, o_qkv, o_qkvb, o_d, o_g2, o_b2, o_in, o_inb, o_out, o_last, held, gq, gd, gi, go, gv, arrive, leave
):
    z = lax.axis_index("shard") % 4
    pieces = [(act.at[m], o_act.at[0, m]) for m in (0, 1)] + [(ig.at[m], o_ig.at[0, m]) for m in (0, 1)]
    coming = [pltpu.make_async_copy(src, held.at[k], arrive.at[k]) for k, (src, _) in enumerate(pieces)]
    going = [pltpu.make_async_copy(held.at[k], dst, leave.at[k]) for k, (_, dst) in enumerate(pieces)]
    small = [
        pltpu.make_async_copy(src, dst, arrive.at[4 + k])
        for k, (src, dst) in enumerate(((hq, gq), (hd, gd), (hi, gi), (ho, go), (hv, gv)))
    ]
    for copy in coming + small:
        copy.start()
    for copy, after in zip(coming, going):
        copy.wait()
        after.start()
    for copy in small:
        copy.wait()
    for half in (0, 1):
        rows = slice(16 * half, 16 * half + 16)
        for hp in range(PAIRS):
            for which in range(3):
                column = 512 * which + 128 * hp
                o_qkv[0, rows, column : column + 128] = gq[hp, half, :, 128 * which : 128 * which + 128]
        o_d[0, rows, :] = gd[half]
        o_in[0, rows, :] = gi[half]
        o_out[0, 64 * half : 64 * half + 64, :] = go[half]

    def own(row, width):
        total = jnp.zeros((1, width), F32)
        for k in range(4):
            total = total + jnp.where(z == k, row[:, width * k : width * k + width], 0.0)
        return total

    for row, ref in enumerate((o_g1, o_b1, o_g2, o_b2, o_last)):
        ref[...] = own(gv[row : row + 1, :], 32)
    o_qkvb[...] = own(jnp.concatenate([gv[8 + k : 9 + k, :] for k in range(3)], axis=1), 96)
    o_inb[...] = gv[11:12, :]
    for copy in going:
        copy.wait()


def solution(mesh):
    rows = P(None, ("replica", "shard"), None)
    vector, matrix = P("section", "shard"), P("section", "shard", None)
    slabs = P("section", None, ("replica", "shard"), None)
    return jax.shard_map(
        body,
        mesh=mesh,
        in_specs=(
            rows, rows, rows, vector, vector, matrix, vector, matrix, vector, vector, matrix, vector, matrix, vector,
        ),
        out_specs=(
            slabs, slabs, vector, vector, matrix, vector, matrix, vector, vector, matrix, vector, matrix, vector,
        ),
        check_vma=False,
    )
```

```python
import math

import jax
import jax.numpy as jnp
from jax import lax
from jax.experimental import pallas as pl
from jax.experimental.pallas import tpu as pltpu
from jax.sharding import PartitionSpec as P

T = 768
D = 512
FF = 2048
HEADS = 8
HEAD = 64
ROT = 16
BLOCK = 128
SEQS = 4
TILE = 256
EPS = 1e-5
MASKED = -1e9
LOG2E = 1.0 / math.log(2.0)
LN2 = math.log(2.0)
MESH = pl.DeviceIdType.MESH
BF = jnp.bfloat16
F32 = jnp.float32

PAIRS = 4
DENSE, FIN, FOUT, VEC = 4, 5, 6, 7
PARTS = 8
LETTERS = "abcdDIOV"
HALF_ROWS = (16, 16, 16, 16, 16, 16, 64, 8)
WIDTH = (384, 384, 384, 384, 512, 2048, 512, 128)
KIND = (BF, BF, BF, BF, BF, BF, BF, F32)


def dg(a, b, ca, cb):
    return lax.dot_general(a, b, (((ca,), (cb,)), ((), ())), preferred_element_type=F32)


class Place:
    def __init__(self):
        self.s = lax.axis_index("section")
        self.y = lax.axis_index("replica")
        shard = lax.axis_index("shard")
        x, z = shard // 4, shard % 4
        self.shard, self.x, self.z = shard, x, z
        self.p = x + self.s * (z - x)
        self.q = z + self.s * (x - z)

    def at(self, p, q):
        return (1 - self.s) * (4 * p + q) + self.s * (4 * q + p)

    def sibling(self):
        return (1 - self.s, self.y, self.shard)

    def along_p(self, d):
        return (self.s, self.y, self.at((self.p + d) % 4, self.q))

    def along_q(self, d):
        return (self.s, self.y, self.at(self.p, (self.q + d) % 4))

    def along_y(self, d):
        return (self.s, (self.y + d) % 4, self.shard)


def remote(src, dst, send, recv, device):
    return pltpu.make_async_remote_copy(
        src_ref=src, dst_ref=dst, send_sem=send, recv_sem=recv, device_id=device, device_id_type=MESH
    )


class Gather:
    def __init__(self, me, layer, part, shard_ref, whole, send, recv, local):
        self.me, self.layer, self.part = me, layer, part
        self.shard_ref, self.w = shard_ref, whole
        self.send = lambda k: send.at[layer, part, k]
        self.recv = lambda k: recv.at[layer, part, k]
        self.local = local.at[part]
        self.rows = HALF_ROWS[part]
        self.direct = layer == 0 and part in (0, 1, 2, 3, VEC)
        self.ways = (1, 3, 2) if self.direct else (1, 3)

    def halves(self, h, target):
        if self.part == VEC:
            return [(self.shard_ref.at[h], target)]
        rows = pl.ds(pl.multiple_of(h * self.rows, self.rows), self.rows)
        if self.part < PAIRS:
            return [
                (
                    self.shard_ref.at[0, rows, pl.ds(512 * which + 128 * self.part, 128)],
                    target.at[:, pl.ds(128 * which, 128)],
                )
                for which in range(3)
            ]
        return [(self.shard_ref.at[0, rows, :], target)]

    def move(self, ref, sent, came, device):
        return remote(ref, ref, self.send(sent), self.recv(came), device)

    def shards(self, count):
        return self.move(self.w.at[self.me.s, pl.ds(0, count)], 1, 1, self.me.sibling())

    def row(self, half, p):
        return self.w.at[half, pl.ds(4 * p, 4)]

    def own(self, half, p, q):
        return self.w.at[half, 4 * p + q]

    def step0(self):
        me = self.me

        @pl.when(me.s == self.layer)
        def _():
            for src, dst in self.halves(me.s, self.own(me.s, me.p, me.q)):
                pltpu.make_async_copy(src, dst, self.local).start()
            for src, dst in self.halves(1 - me.s, self.own(1 - me.s, me.q, me.p)):
                remote(src, dst, self.send(0), self.recv(0), me.sibling()).start()

    def step1(self):
        me = self.me
        own = self.own(me.s, me.p, me.q)

        @pl.when(me.s == self.layer)
        def _():
            pltpu.make_async_copy(own, own, self.local).wait()

        @pl.when(me.s != self.layer)
        def _():
            self.move(own, 0, 0, me.sibling()).wait_recv()

        for d in (1, 3, 2):
            self.move(own, 1, 1, me.along_q(d)).start()

    def across(self, p):
        self.move(self.row(self.me.s, p), 2, 4, self.me.sibling()).start()

    def step2(self):
        me = self.me
        self.shards(3).wait_recv()
        for d in self.ways:
            self.move(self.row(me.s, me.p), 1, 2, me.along_p(d)).start()
        self.across(me.p)

    def step3(self):
        me = self.me
        ref = self.w.at[me.s, pl.ds(0, 4 * len(self.ways))]
        self.move(ref, 1, 2, me.sibling()).wait_recv()
        if not self.direct:
            for d in (1, 3):
                half = self.w.at[me.s, pl.ds(4 * ((me.p + 4 - d) % 4) + d - 1, 2)]
                self.move(half, 1, 3, me.along_p(d)).start()
        for d in self.ways:
            self.across((me.p + 4 - d) % 4)

    def step4(self):
        me = self.me
        if not self.direct:
            self.move(self.row(me.s, me.p), 1, 3, me.sibling()).wait_recv()
            self.across((me.p + 2) % 4)

    def step5(self):
        self.move(self.w.at[1 - self.me.s], 2, 4, self.me.sibling()).wait_recv()

    def finish(self):
        me = self.me

        @pl.when(me.s == self.layer)
        def _():
            self.move(self.own(1 - me.s, me.q, me.p), 0, 0, me.sibling()).wait_send()

        self.shards(15).wait_send()
        self.move(self.w.at[me.s], 2, 4, me.sibling()).wait_send()


class Reduce:
    def __init__(self, me, layer, part, terms, buffers, send, recv):
        self.me, self.layer, self.part = me, layer, part
        self.g = terms
        self.r, self.one, self.two, self.ys, self.f, self.out = buffers
        self.send = lambda k: send.at[layer, part, k]
        self.recv = lambda k: recv.at[layer, part, k]
        self.kind = KIND[part]

    def swap(self):
        me = self.me
        return remote(self.g.at[1 - me.s], self.r, self.send(0), self.recv(0), me.sibling())

    def first(self, d):
        me = self.me
        row = self.r.at[pl.ds(4 * ((me.p + d) % 4), 4)]
        return remote(row, self.one.at[d - 1], self.send(1), self.recv(1), me.along_p(d))

    def second(self, d):
        me = self.me
        shard = self.r.at[4 * me.p + (me.q + d) % 4]
        return remote(shard, self.two.at[d - 1], self.send(2), self.recv(2), me.along_q(d))

    def third(self, d):
        me = self.me
        return remote(self.ys.at[me.y], self.ys.at[me.y], self.send(3), self.recv(3), me.along_y(d))

    def all_of(self, ref, k):
        return remote(ref, ref, self.send(k), self.recv(k), self.me.sibling())

    def back(self):
        me = self.me
        return remote(self.f, self.out.at[me.s], self.send(4), self.recv(4), me.sibling())

    def step0(self):
        self.swap().start()

    def step1(self):
        me = self.me
        self.swap().wait_recv()

        def one(k, c):
            self.r[k] = (self.r[k].astype(F32) + self.g[me.s, k].astype(F32)).astype(self.kind)
            return c

        lax.fori_loop(0, 16, one, 0)
        for d in (1, 3, 2):
            self.first(d).start()
        self.swap().wait_send()

    def step2(self):
        me = self.me
        self.all_of(self.one, 1).wait_recv()

        def one(b, c):
            total = self.r[4 * me.p + b].astype(F32) + self.one[0, b].astype(F32)
            total = total + (self.one[1, b].astype(F32) + self.one[2, b].astype(F32))
            self.r[4 * me.p + b] = total.astype(self.kind)
            return c

        lax.fori_loop(0, 4, one, 0)
        for d in (1, 3, 2):
            self.second(d).start()

    def step3(self):
        me = self.me
        self.all_of(self.two, 2).wait_recv()
        total = self.r[4 * me.p + me.q].astype(F32) + self.two[0].astype(F32)
        total = total + (self.two[1].astype(F32) + self.two[2].astype(F32))
        self.ys[me.y] = total.astype(self.kind)
        for d in (1, 3, 2):
            self.third(d).start()

    def step4(self):
        me = self.me
        self.all_of(self.ys.at[pl.ds(0, 3)], 3).wait_recv()
        total = (self.ys[0].astype(F32) + self.ys[1].astype(F32)) + (
            self.ys[2].astype(F32) + self.ys[3].astype(F32)
        )

        @pl.when(me.s == self.layer)
        def _():
            self.out[me.s] = total

        @pl.when(me.s != self.layer)
        def _():
            self.f[...] = total
            self.back().start()

    def step5(self):
        me = self.me

        @pl.when(me.s == self.layer)
        def _():
            self.all_of(self.out.at[1 - me.s], 4).wait_recv()

    def finish(self):
        self.all_of(self.one, 1).wait_send()
        self.all_of(self.two, 2).wait_send()
        self.all_of(self.ys.at[pl.ds(0, 3)], 3).wait_send()

        @pl.when(self.me.s != self.layer)
        def _():
            self.back().wait_send()


class ReduceVectors:
    def __init__(self, me, layer, terms, buffers, send, recv):
        self.me, self.layer, self.g = me, layer, terms
        self.r, self.one, self.ys, self.out = buffers
        self.send = lambda k: send.at[layer, VEC, k]
        self.recv = lambda k: recv.at[layer, VEC, k]

    def swap(self):
        return remote(self.g, self.r, self.send(0), self.recv(0), self.me.sibling())

    def first(self, k):
        x, z = (self.me.x + k // 4) % 4, (self.me.z + k % 4) % 4
        device = (self.me.s, self.me.y, 4 * x + z)
        return remote(self.r.at[x, z], self.one.at[k], self.send(1), self.recv(1), device)

    def all_first(self):
        ref = self.one.at[pl.ds(1, 15)]
        return remote(ref, ref, self.send(1), self.recv(1), self.me.sibling())

    def third(self, d):
        me = self.me
        return remote(self.ys.at[me.y], self.ys.at[me.y], self.send(3), self.recv(3), me.along_y(d))

    def all_third(self):
        ref = self.ys.at[pl.ds(0, 3)]
        return remote(ref, ref, self.send(3), self.recv(3), self.me.sibling())

    def owner(self, step):
        pl.when(self.me.s == self.layer)(step)

    def step0(self):
        @pl.when(self.me.s != self.layer)
        def _():
            self.swap().start()

    def step1(self):
        def step():
            self.swap().wait_recv()
            self.r[...] += self.g[...]
            for k in (1, 4, 3, 12, 5, 7, 13, 15, 2, 8, 6, 9, 11, 14, 10):
                self.first(k).start()

        self.owner(step)

        @pl.when(self.me.s != self.layer)
        def _():
            self.swap().wait_send()

    def step2(self):
        def step():
            self.all_first().wait_recv()
            total = self.r[self.me.x, self.me.z]
            for k in range(1, 16):
                total = total + self.one[k]
            self.ys[self.me.y] = total
            for d in (1, 3, 2):
                self.third(d).start()

        self.owner(step)

    def step3(self):
        def step():
            self.all_third().wait_recv()
            self.out[...] = (self.ys[0] + self.ys[1]) + (self.ys[2] + self.ys[3])

        self.owner(step)

    def step5(self):
        pass

    def finish(self):
        def step():
            self.all_first().wait_send()
            self.all_third().wait_send()

        self.owner(step)


def natural_rows(ref, columns):
    pieces = []
    for x in range(4):
        for z in range(4):
            pieces.append(ref[0, 4 * x + z, :, columns])
            pieces.append(ref[1, 4 * z + x, :, columns])
    return jnp.concatenate(pieces, axis=0)


def group_rows(ref, x):
    pieces = []
    for z in range(4):
        pieces.append(ref[0, 4 * x + z])
        pieces.append(ref[1, 4 * z + x])
    return jnp.concatenate(pieces, axis=0)


def put_natural(ref, columns, value):
    for x in range(4):
        for z in range(4):
            row = 32 * (4 * x + z)
            ref[0, 4 * x + z, :, columns] = value[row : row + 16]
            ref[1, 4 * z + x, :, columns] = value[row + 16 : row + 32]


def put_group(ref, x, value, rows):
    for z in range(4):
        row = 2 * rows * z
        ref[0, 4 * x + z] = value[row : row + rows]
        ref[1, 4 * z + x] = value[row + rows : row + 2 * rows]


def to_column(row):
    here = lax.broadcasted_iota(jnp.int32, (128, 128), 0) == lax.broadcasted_iota(
        jnp.int32, (128, 128), 1
    )
    return jnp.sum(jnp.where(here, row, 0.0), axis=1, keepdims=True)


def turn(rows, cosine, sine):
    pieces = []
    for e in (0, 64):
        low, high = rows[e : e + 8], rows[e + 8 : e + 16]
        pieces += [low * cosine - high * sine, high * cosine + low * sine, rows[e + 16 : e + 64]]
    return jnp.concatenate(pieces, axis=0)


def columns(start, size):
    return pl.ds(pl.multiple_of(start, size), size)


def loop(count, step):
    def one(k, c):
        step(k)
        return c

    lax.fori_loop(0, count, one, 0)


def kernel(
    lengths,
    x_ref,
    cot_ref,
    wq_ref,
    wd_ref,
    wi_ref,
    wo_ref,
    gain1_ref,
    shift1_ref,
    gain2_ref,
    shift2_ref,
    last_ref,
    qkvb_ref,
    finb_ref,
    act_out,
    ig_out,
    gq_out,
    gd_out,
    gi_out,
    go_out,
    gv_out,
    st_qkv,
    st_p0,
    st_p1,
    st_p2,
    st_bt,
    st_rinv,
    st_act,
    st_slo,
    st_n1t,
    st_n2,
    *scratch,
):
    scratch = list(scratch)

    def take(count):
        taken, scratch[:count] = scratch[:count], []
        return taken

    def take_parts(count=4):
        pairs, *rest = take(count)
        return [pairs] + [pairs.at[k] for k in range(PAIRS)] + rest

    (wq0, *w0), (wq1, *w1) = take_parts(5), take_parts(5)
    w, wq = (w0, w1), (wq0, wq1)
    gq, *g = take_parts()
    r, one, two, ys = [(take_parts(), take_parts()) for _ in range(4)]
    rq = [parts.pop(0) for parts in r]
    for both in (one, two, ys):
        for parts in both:
            parts.pop(0)
    f = take_parts()[1:]
    gvec, *rvec = take(3)
    vecs, yvec, (vsrc, vrow) = take(2), take(2), take(2)
    hid, grad, n1t, n2, acc, carried = take(6)
    qkvt, p0, p1, p2, bt, rinv, act, slo = take(8)
    d0, d1, d2, scores_one = take(4)
    dn1 = n2
    vd, vq, vf, dvec, fvec, live, bias, cos_ref, sin_ref = take(9)
    sends, ag_recv, rs_recv, ag_local, sems, ex_send, ex_recv = take(7)
    probs = (p0, p1, p2)
    dscores = (d0, d1, d2)
    outs = [gq_out.at[k] for k in range(PAIRS)] + [gd_out, gi_out, go_out]
    shards = [wq_ref] * PAIRS + [wd_ref, wi_ref, wo_ref, vsrc]

    me = Place()
    s = me.s
    barrier = pltpu.get_barrier_semaphore()
    partners = [me.sibling()]
    for d in (1, 2, 3):
        partners += [me.along_q(d), me.along_p(d), me.along_y(d)]
        for e in (1, 2, 3):
            partners.append((s, me.y, 4 * ((me.x + d) % 4) + (me.z + e) % 4))
    for device in partners:
        pl.semaphore_signal(barrier, inc=1, device_id=device, device_id_type=MESH)
    pl.semaphore_wait(barrier, len(partners))

    gather = [
        [Gather(me, l, c, shards[c], w[l][c], sends, ag_recv, ag_local) for c in range(PARTS)]
        for l in (0, 1)
    ]
    reduce = [
        [
            Reduce(
                me, l, c, g[c], (r[l][c], one[l][c], two[l][c], ys[l][c], f[c], outs[c]), sends, rs_recv
            )
            for c in range(VEC)
        ]
        + [ReduceVectors(me, l, gvec, (rvec[l], vecs[l], yvec[l], gv_out), sends, rs_recv)]
        for l in (0, 1)
    ]

    def fetch(*plan):
        for word in plan:
            item = gather[int(word[0])][LETTERS.index(word[1])]
            getattr(item, "step" + word[2])()

    def back_pairs(l, first):
        def step(k):
            hp = first + k
            back_attend(l, hp)
            back_qkv(hp)
            remote(
                gq.at[hp, 1 - s], rq[l].at[hp], sends.at[l, hp, 0], rs_recv.at[l, hp, 0], me.sibling()
            ).start()

        loop(2, step)

    def send(*plan):
        for word in plan:
            item = reduce[int(word[0])][LETTERS.index(word[1])]
            getattr(item, "step" + word[2])()

    vsrc[...] = jnp.zeros((2, 8, 128), F32)
    for k in range(4):
        here = me.z == k
        for row, ref in enumerate((gain1_ref, shift1_ref, gain2_ref, shift2_ref, last_ref)):
            vsrc[0, row : row + 1, 32 * k : 32 * k + 32] = jnp.where(here, ref[...].astype(F32), 0.0)
        vrow[0:1, 96 * k : 96 * k + 96] = jnp.where(here, qkvb_ref[...].astype(F32), 0.0)
    for k in range(3):
        vsrc[1, k : k + 1, :] = vrow[0:1, 128 * k : 128 * k + 128]
    vsrc[1, 3:4, :] = finb_ref[...].astype(F32)

    x_in = pltpu.make_async_copy(x_ref.at[s], hid.at[0], sems.at[0])
    cot_in = pltpu.make_async_copy(cot_ref.at[s], grad.at[0], sems.at[1])
    x_in.start()
    fetch("0V0", "0a0", "0b0", "0c0", "0d0", "0I0", "0D0", "0O0", "1V0", "1a0", "1b0", "1c0", "1d0", "1I0", "1D0", "1O0")
    fetch("0V1", "0a1", "0b1", "0c1", "0d1", "0D1", "0I1", "0O1")
    cot_in.start()

    starts, ends, at = [], [], jnp.int32(0)
    for k in range(SEQS):
        size = lengths[s, 0, k]
        starts.append(at)
        ends.append(at + size)
        at = at + (size + BLOCK - 1) // BLOCK * BLOCK

    def inside(places):
        return [(places >= a) & (places < b) for a, b in zip(starts, ends)]

    def live_tile(k):
        places = lax.broadcasted_iota(jnp.int32, (TILE, 1), 0) + k * TILE
        total = jnp.zeros((TILE, 1), F32)
        for found in inside(places):
            total = total + jnp.where(found, 1.0, 0.0)
        live[columns(k * TILE, TILE), :] = total

    loop(3, live_tile)
    places = lax.broadcasted_iota(jnp.int32, (8, T), 1)
    begin = jnp.zeros((8, T), jnp.int32)
    offset = jnp.zeros((8, T), jnp.int32)
    for found, a in zip(inside(places), starts):
        begin = begin + jnp.where(found, a, 0)
        offset = offset + jnp.where(found, places - a, 0)
    rates = jnp.exp(
        lax.broadcasted_iota(jnp.int32, (8, T), 0).astype(F32) * (-2.0 * math.log(10000.0) / ROT)
    )
    angles = offset.astype(F32) * rates
    cos_ref[...] = jnp.cos(angles)
    sin_ref[...] = jnp.sin(angles)
    for j in range(3):
        for i in range(j + 1):
            keys = lax.broadcasted_iota(jnp.int32, (TILE, TILE), 0) + i * TILE
            queries = lax.broadcasted_iota(jnp.int32, (TILE, TILE), 1) + j * TILE
            fits = (keys >= begin[0:1, j * TILE : (j + 1) * TILE]) & (keys <= queries)
            bias[j * (j + 1) // 2 + i] = jnp.where(fits, 0.0, MASKED)

    def unpack(l):
        ref = w[l][VEC]
        for x in range(4):
            vd[:, 128 * x : 128 * x + 128] = (ref[0, 4 * x] + ref[0, 4 * x + 1]) + (
                ref[0, 4 * x + 2] + ref[0, 4 * x + 3]
            )
            group = (ref[1, x] + ref[1, 4 + x]) + (ref[1, 8 + x] + ref[1, 12 + x])
            for k in range(3):
                vq[3 * x + k : 3 * x + k + 1, :] = group[k : k + 1]
            for z in range(4):
                vf[x : x + 1, 128 * z : 128 * z + 128] = ref[1, 4 * z + x][3:4]

    def normed(l, rows):
        v = hid[l, rows, :].astype(F32)
        centred = v - jnp.mean(v, axis=1, keepdims=True)
        scale = lax.rsqrt(jnp.mean(centred * centred, axis=1, keepdims=True) + EPS)
        return centred * scale, scale

    def norms(l):
        def tile(k):
            rows = columns(k * TILE, TILE)
            u, _ = normed(l, rows)
            n1t[:, rows] = (u * vd[0:1, :] + vd[1:2, :]).astype(BF).T
            n2[rows, :] = (u * vd[2:3, :] + vd[3:4, :]).astype(BF)

        loop(3, tile)

    def project(l, hp):
        value = dg(natural_rows(wq[l].at[hp], slice(0, 384)), n1t[...], 0, 0)
        pair = []
        for which in range(3):
            part = value[128 * which : 128 * which + 128] + to_column(vq[pl.ds(which * 4 + hp, 1), :])
            if which < 2:
                part = turn(part, cos_ref[...], sin_ref[...])
            if which == 0:
                part = part * (LOG2E / 8.0)
            pair.append(part.astype(BF))
            qkvt[columns(hp * 384 + which * 128, 128), :] = pair[which]
        return pair

    def score_block(e, k):
        if e:
            return scores_one.at[k]
        return acc.at[pl.ds(TILE * (k // 2), TILE), pl.ds(TILE * (k % 2), TILE)]

    def attend(l, hp):
        pair = project(l, hp)
        keys = pair[1].T
        blank = jnp.zeros((HEAD, T), BF)
        peaks = ([None] * 3, [None] * 3)
        for e in (0, 1):
            mine = pair[0][e * HEAD : (e + 1) * HEAD]
            mine = jnp.concatenate([mine, blank] if e == 0 else [blank, mine], axis=0)
            for i in range(3):
                for j in range(i, 3):
                    k = j * (j + 1) // 2 + i
                    scores = dg(keys[i * TILE : (i + 1) * TILE], mine[:, j * TILE : (j + 1) * TILE], 1, 0)
                    scores = scores + bias[k]
                    score_block(e, k)[...] = scores
                    peak = jnp.max(scores, axis=0, keepdims=True)
                    peaks[e][j] = peak if i == 0 else jnp.maximum(peaks[e][j], peak)
        for e in (0, 1):
            h = 2 * hp + e
            value = jnp.concatenate([pair[2][e * HEAD : (e + 1) * HEAD], jnp.ones((8, T), BF)], axis=0)
            for j in range(3):
                at_j = slice(j * TILE, (j + 1) * TILE)
                blended = jnp.zeros((HEAD + 8, TILE), F32)
                for i in range(j + 1):
                    raised = jnp.exp2(score_block(e, j * (j + 1) // 2 + i)[...] - peaks[e][j]).astype(BF)
                    probs[i][h, :, (j - i) * TILE : (j - i + 1) * TILE] = raised
                    blended = blended + dg(value[:, i * TILE : (i + 1) * TILE], raised, 1, 0)
                inverse = 1.0 / blended[HEAD : HEAD + 1]
                rinv[pl.ds(h, 1), at_j] = inverse
                bt[columns(hp * 128 + e * HEAD, HEAD), at_j] = (blended[:HEAD] * inverse).astype(BF)

    def widen(l, c):
        cols = columns(c * 512, 512)
        weight = natural_rows(w[l][FIN], cols)
        shift = vf[pl.ds(c, 1), :]

        def tile(k):
            rows = columns(k * TILE, TILE)
            v = dg(n2[rows, :], weight, 1, 0) + shift
            below = 0.5 + 0.5 * lax.erf(v * (1.0 / math.sqrt(2.0)))
            act[rows, cols] = (v * below).astype(BF)
            slope = below + v * (jnp.exp(-0.5 * v * v) * (1.0 / math.sqrt(2.0 * math.pi)))
            slo[rows, cols] = slope.astype(BF)

        for k in range(3):
            tile(k)

    def join(l):
        def part(t):
            cols = columns(t * TILE, TILE)
            weight = jnp.concatenate(
                [
                    piece
                    for x in range(4)
                    for z in range(4)
                    for piece in (w[l][FOUT][0, 4 * x + z, :, cols], w[l][FOUT][1, 4 * z + x, :, cols])
                ],
                axis=0,
            )
            total = dg(act[...], weight, 1, 0)
            total = total + dg(bt[...], natural_rows(w[l][DENSE], cols), 0, 0)
            total = total + hid[l, :, cols].astype(F32) + vd[4:5, cols]
            hid[l + 1, :, cols] = (total * live[...]).astype(BF)

        loop(2, part)

    def local(src, dst, k):
        return pltpu.make_async_copy(src, dst, sems.at[k])

    attention_kept = [
        (qkvt, st_qkv, 2),
        (p0, st_p0, 3),
        (p1, st_p1, 4),
        (p2, st_p2, 5),
        (bt, st_bt, 6),
        (rinv, st_rinv, 7),
    ]
    norms_kept = [(n1t, st_n1t, 12), (n2, st_n2, 13)]
    wide_kept = [(act, st_act, 8), (slo, st_slo, 9)]

    fetch("0V2", "0a2", "0b2", "0c2", "0d2")
    x_in.wait()
    fetch("0V3", "0a3")
    fetch("0D2", "0I2")
    fetch("0V5")
    unpack(0)
    norms(0)
    for a, b, k in norms_kept:
        local(a, b, k).start()
    fetch("0b3", "0O2", "0a5")
    fetch("0c3", "0b5")
    loop(2, lambda hp: attend(0, hp))
    fetch("0d3", "0c5")
    fetch("0D3", "0I3")
    fetch("1V1", "1a1", "1b1", "1c1", "1d1", "0d5")
    loop(2, lambda hp: attend(0, hp + 2))
    for a, b, k in attention_kept:
        local(a, b, k).start()
    fetch("0O3")
    fetch("1I1", "1D1", "1O1")
    fetch("0D4", "0I4", "1V2", "1a2", "1b2")
    fetch("0I5")
    loop(2, lambda c: widen(0, c))
    fetch("0O4")
    fetch("1c2", "1d2", "1V3", "1a3")
    loop(2, lambda c: widen(0, c + 2))
    fetch("1b3", "1c3", "1d3", "1I2", "1D2", "1O2", "0D5", "0O5")
    join(0)
    for a, b, k in wide_kept:
        local(a, b, k).start()

    fetch("1V4", "1a4", "1b4")
    fetch("1V5")
    unpack(1)
    for a, b, k in norms_kept:
        local(a, b, k).wait()
    norms(1)
    fetch("1c4", "1d4", "1a5", "1b5")
    for a, b, k in attention_kept:
        local(a, b, k).wait()
    loop(2, lambda hp: attend(1, hp))
    fetch("1I3", "1D3", "1c5", "1d5")
    loop(2, lambda hp: attend(1, hp + 2))
    fetch("1O3", "1I4", "1D4")
    fetch("1I5")
    for a, b, k in wide_kept:
        local(a, b, k).wait()
    loop(2, lambda c: widen(1, c))
    fetch("1O4")
    loop(2, lambda c: widen(1, c + 2))
    fetch("1D5", "1O5")
    join(1)
    for l in (0, 1):
        for c in range(PARTS):
            gather[l][c].finish()
    act_mine = local(hid.at[1 + s], act_out.at[s], 10)
    act_theirs = remote(hid.at[2 - s], act_out.at[s], ex_send.at[0], ex_recv.at[0], me.sibling())
    act_mine.start()
    act_theirs.start()
    cot_in.wait()

    def start_back(l):
        def tile(k):
            rows = columns(k * TILE, TILE)
            v = grad[1 - l, rows, :].astype(F32) * live[rows, :]
            carried[rows, :] = v.astype(BF)
            here = jnp.sum(v, axis=0, keepdims=True)
            dvec[4:5, :] = here + jnp.where(k == 0, 0.0, dvec[4:5, :])

        dvec[...] = jnp.zeros((8, D), F32)
        loop(3, tile)

    def back_out(c):
        cols = columns(c * 512, 512)
        put_group(g[FOUT], c, dg(act[:, cols], carried[...], 0, 0).astype(BF), 64)

    def back_wide(l, c):
        cols = columns(c * 512, 512)
        weight = group_rows(w[l][FOUT], c)
        total = jnp.zeros((1, 512), F32)
        for k in range(3):
            rows = slice(k * TILE, (k + 1) * TILE)
            v = dg(carried[rows, :], weight, 1, 1) * slo[rows, cols].astype(F32)
            v = v.astype(BF)
            slo[rows, cols] = v
            total = total + jnp.sum(v.astype(F32), axis=0, keepdims=True)
        fvec[pl.ds(c, 1), :] = total

    def back_in(l, c):
        cols = columns(c * 512, 512)
        put_natural(g[FIN], cols, dg(n2[...], slo[:, cols], 0, 0).astype(BF))

    def back_norm_two(l, t):
        low = w[l][FIN][0, pl.ds(8 * t, 8)]
        high = [w[l][FIN][1, pl.ds(4 * z + 2 * t, 2)] for z in range(4)]
        pieces = []
        for x in range(2):
            for z in range(4):
                pieces += [low[4 * x + z], high[z][x]]
        acc[:, columns(t * TILE, TILE)] = dg(slo[...], jnp.concatenate(pieces, axis=0), 1, 1)

    def back_dense(l):
        put_natural(g[DENSE], slice(0, 512), dg(bt[...], carried[...], 1, 0).astype(BF))

    def back_attend(l, hp):
        weight = group_rows(w[l][DENSE], hp)
        below = dg(weight, carried[...], 1, 1)
        queries = qkvt[columns(hp * 384, 128), :]
        keys = qkvt[columns(hp * 384 + 128, 128), :]
        values = qkvt[columns(hp * 384 + 256, 128), :].T
        blended = bt[columns(hp * 128, 128), :].astype(F32)
        blank = jnp.zeros((HEAD, TILE), BF)
        downs = []
        for e in (0, 1):
            h = 2 * hp + e
            down = below[e * HEAD : (e + 1) * HEAD] * rinv[pl.ds(h, 1), :]
            centre = jnp.sum(down * blended[e * HEAD : (e + 1) * HEAD], axis=0, keepdims=True)
            down = down.astype(BF)
            downs.append(down)
            for j in range(3):
                at_j = slice(j * TILE, (j + 1) * TILE)
                mine = down[:, at_j]
                mine = jnp.concatenate([mine, blank] if e == 0 else [blank, mine], axis=0)
                for i in range(j + 1):
                    cols = slice((j - i) * TILE, (j - i + 1) * TILE)
                    slope = dg(values[i * TILE : (i + 1) * TILE], mine, 1, 0) - centre[:, at_j]
                    slope = slope * probs[i][h, :, cols].astype(F32)
                    dscores[i][e, :, cols] = slope.astype(BF)
        done = []
        for e in (0, 1):
            h = 2 * hp + e
            query = queries[e * HEAD : (e + 1) * HEAD]
            key = keys[e * HEAD : (e + 1) * HEAD]
            grad_query, grad_key, grad_value = [], [], []
            for j in range(3):
                total = jnp.zeros((HEAD, TILE), F32)
                for i in range(j + 1):
                    cols = slice((j - i) * TILE, (j - i + 1) * TILE)
                    total = total + dg(key[:, i * TILE : (i + 1) * TILE], dscores[i][e, :, cols], 1, 0)
                grad_query.append(total * 0.125)
            for i in range(3):
                grad_key.append(dg(query[:, i * TILE :], dscores[i][e], 1, 1) * LN2)
                grad_value.append(dg(downs[e][:, i * TILE :], probs[i][h], 1, 1))
            done.append(
                [jnp.concatenate(pieces, axis=1) for pieces in (grad_query, grad_key, grad_value)]
            )
        for which in range(3):
            value = jnp.concatenate([done[0][which], done[1][which]], axis=0)
            if which < 2:
                value = turn(value, cos_ref[...], -sin_ref[...])
            qkvt[columns(hp * 384 + which * 128, 128), :] = value.astype(BF)

    def back_qkv(hp):
        value = dg(n1t[...], qkvt[columns(hp * 384, 384), :], 1, 1)
        put_natural(gq.at[hp], slice(0, 384), value.astype(BF))

    def back_norm_one(l, t):
        weight = jnp.concatenate([group_rows(wq[l].at[hp], t) for hp in range(PAIRS)], axis=1)
        dn1[:, columns(t * 128, 128)] = dg(weight, qkvt[...], 1, 0).astype(BF).T

    def add_sums(u, first, second):
        dvec[0:1, :] += jnp.sum(first * u, axis=0, keepdims=True)
        dvec[1:2, :] += jnp.sum(first, axis=0, keepdims=True)
        dvec[2:3, :] += jnp.sum(second * u, axis=0, keepdims=True)
        dvec[3:4, :] += jnp.sum(second, axis=0, keepdims=True)

    def norm_sums(l):
        def tile(k):
            rows = columns(k * TILE, TILE)
            add_sums(normed(l, rows)[0], dn1[rows, :].astype(F32), acc[rows, :])

        loop(3, tile)

    def end_back(l, with_sums):
        def tile(k):
            rows = columns(k * TILE, TILE)
            u, scale = normed(l, rows)
            first = dn1[rows, :].astype(F32)
            second = acc[rows, :]
            if with_sums:
                add_sums(u, first, second)
            total = first * vd[0:1, :] + second * vd[2:3, :]
            centre = jnp.mean(total, axis=1, keepdims=True)
            along = jnp.mean(total * u, axis=1, keepdims=True)
            total = carried[rows, :].astype(F32) + scale * (total - centre - u * along)
            grad[l, rows, :] = total.astype(BF)

        loop(3, tile)

    def put_biases():
        sums = dg(jnp.ones((8, T), BF), qkvt[...], 1, 1)
        for x in range(4):
            for k in range(3):
                which, hp = divmod(3 * x + k, PAIRS)
                row = 384 * hp + 128 * which
                vq[3 * x + k : 3 * x + k + 1, :] = sums[0:1, row : row + 128]
        for x in range(4):
            rest = jnp.concatenate([vq[3 * x : 3 * x + 3, :], jnp.zeros((5, 128), F32)], axis=0)
            for z in range(4):
                gvec[x, z, 8:16] = rest
                gvec[x, z, 11:12] = fvec[x : x + 1, 128 * z : 128 * z + 128]

    def put_norms():
        for x in range(4):
            for z in range(4):
                gvec[x, z, 0:8] = dvec[:, 128 * x : 128 * x + 128]

    restored = ((qkvt, st_qkv, 2), (p0, st_p0, 3), (p1, st_p1, 4), (p2, st_p2, 5), (bt, st_bt, 6), (rinv, st_rinv, 7))

    start_back(1)
    loop(4, back_out)
    send("1O0")
    loop(4, lambda c: back_wide(1, c))
    send("1O1")
    loop(4, lambda c: back_in(1, c))
    send("1I0")
    loop(2, lambda t: back_norm_two(1, t))
    local(st_act, act, 8).start()
    local(st_slo, slo, 9).start()
    back_dense(1)
    send("1D0", "1I1")
    back_pairs(1, 0)
    send("1D1", "1a1", "1O2")
    back_pairs(1, 2)
    local(st_n1t, n1t, 12).start()
    send("1b1", "1c1", "1I2")
    loop(4, lambda t: back_norm_one(1, t))
    send("1d1", "1D2", "1O3")
    put_biases()
    for a, b, k in restored:
        local(b, a, k).start()
    end_back(1, True)
    put_norms()
    send("1V0", "1a2")
    local(st_n2, n2, 13).start()

    unpack(0)
    start_back(0)
    local(st_act, act, 8).wait()
    local(st_slo, slo, 9).wait()
    send("1b2", "1I3")
    loop(4, back_out)
    send("0O0", "1V1", "1D3", "1c2", "1d2", "1a3")
    loop(4, lambda c: back_wide(0, c))
    send("0O1", "1O4", "1b3")
    local(st_n2, n2, 13).wait()
    loop(4, lambda c: back_in(0, c))
    send("0I0", "1V2", "1c3", "1d3", "1D4")
    loop(2, lambda t: back_norm_two(0, t))
    send("0I1", "1I4", "1a4", "1b4")
    for a, b, k in restored:
        local(b, a, k).wait()
    local(st_n1t, n1t, 12).wait()
    back_dense(0)
    send("0D0")
    back_attend(0, 0)
    back_qkv(0)
    send("0a0", "0D1", "1V3", "1c4", "1d4")
    back_attend(0, 1)
    back_qkv(1)
    send("0b0", "0a1", "0O2")
    back_attend(0, 2)
    back_qkv(2)
    send("0c0", "0b1")
    back_attend(0, 3)
    back_qkv(3)
    send("0d0", "0c1")
    put_biases()
    send("0I2", "0D2", "0a2", "0O3")
    loop(2, lambda t: back_norm_one(0, t))
    send("0d1", "0b2")
    loop(2, lambda t: back_norm_one(0, t + 2))
    norm_sums(0)
    put_norms()
    send("0V0")
    send("0c2", "0d2")
    send("0V1")
    send("0I3")
    end_back(0, False)
    grad_mine = local(grad.at[s], ig_out.at[s], 11)
    grad_theirs = remote(grad.at[1 - s], ig_out.at[s], ex_send.at[1], ex_recv.at[1], me.sibling())
    grad_mine.start()
    grad_theirs.start()
    send("0D3", "0a3", "0b3", "0O4")
    send("0c3", "0d3")
    send("0V2")
    send("0D4", "0a4", "0b4")
    send("0c4", "0d4")
    send("0I4")
    send("0V3")
    for l in (1, 0):
        for c in range(PARTS):
            reduce[l][c].step5()
            reduce[l][c].finish()
    act_mine.wait()
    act_theirs.wait_send()
    remote(hid.at[2 - s], act_out.at[1 - s], ex_send.at[0], ex_recv.at[0], me.sibling()).wait_recv()
    grad_mine.wait()
    grad_theirs.wait_send()
    remote(grad.at[1 - s], ig_out.at[1 - s], ex_send.at[1], ex_recv.at[1], me.sibling()).wait_recv()


def scratch_shapes():
    def parts(lead, kind=None):
        return [pltpu.VMEM((PAIRS, *lead, HALF_ROWS[0], WIDTH[0]), kind or BF)] + [
            pltpu.VMEM((*lead, HALF_ROWS[c], WIDTH[c]), kind or KIND[c]) for c in range(PAIRS, PARTS)
        ]

    shapes = []
    for _ in (0, 1):
        shapes += parts((2, 16))
    for lead in ((2, 16), (16,), (16,), (3, 4), (3, 4), (3,), (3,), (4,), (4,)):
        shapes += parts(lead)[:-1]
    shapes += parts((), F32)[:-1]
    for lead in ((4, 4), (4, 4), (4, 4), (16,), (16,), (4,), (4,)):
        shapes.append(pltpu.VMEM((*lead, 16, 128), F32))
    shapes += [pltpu.VMEM((2, 8, 128), F32), pltpu.VMEM((8, 384), F32)]
    shapes += [
        pltpu.VMEM((3, T, D), BF),
        pltpu.VMEM((2, T, D), BF),
        pltpu.VMEM((D, T), BF),
        pltpu.VMEM((T, D), BF),
        pltpu.VMEM((T, D), F32),
        pltpu.VMEM((T, D), BF),
    ]
    shapes += [pltpu.VMEM(shape, kind) for shape, kind in KEPT[:8]]
    shapes += [
        pltpu.VMEM((2, TILE, 768), BF),
        pltpu.VMEM((2, TILE, 512), BF),
        pltpu.VMEM((2, TILE, 256), BF),
        pltpu.VMEM((6, TILE, TILE), F32),
    ]
    shapes += [
        pltpu.VMEM((8, D), F32),
        pltpu.VMEM((16, 128), F32),
        pltpu.VMEM((8, 512), F32),
        pltpu.VMEM((8, D), F32),
        pltpu.VMEM((8, 512), F32),
        pltpu.VMEM((T, 1), F32),
        pltpu.VMEM((6, TILE, TILE), F32),
        pltpu.VMEM((8, T), F32),
        pltpu.VMEM((8, T), F32),
    ]
    dma = pltpu.SemaphoreType.DMA
    shapes += [dma((2, PARTS, 5))] * 3
    shapes += [dma((PARTS,)), dma((14,)), dma((2,)), dma((2,))]
    return shapes


KEPT = (
    ((3 * D, T), BF),
    ((HEADS, TILE, 768), BF),
    ((HEADS, TILE, 512), BF),
    ((HEADS, TILE, 256), BF),
    ((D, T), BF),
    ((HEADS, T), F32),
    ((T, FF), BF),
    ((T, FF), BF),
    ((D, T), BF),
    ((T, D), BF),
)


def body(
    inputs,
    cotangent,
    lengths,
    norm1_gain,
    norm1_bias,
    qkv_weight,
    qkv_bias,
    dense_weight,
    norm2_gain,
    norm2_bias,
    fc_in_weight,
    fc_in_bias,
    fc_out_weight,
    out_bias,
):
    hbm = pl.BlockSpec(memory_space=pl.ANY)
    vmem = pl.BlockSpec(memory_space=pltpu.VMEM)
    shape = jax.ShapeDtypeStruct
    results = pl.pallas_call(
        kernel,
        out_shape=[shape((2, T, D), BF), shape((2, T, D), BF), shape((PAIRS, 2, 16, 384), F32)]
        + [shape((2, HALF_ROWS[c], WIDTH[c]), F32) for c in range(PAIRS, VEC)]
        + [shape((16, 128), F32)]
        + [shape(s, k) for s, k in KEPT],
        in_specs=[pl.BlockSpec(memory_space=pltpu.SMEM)] + [hbm] * 6 + [vmem] * 7,
        out_specs=[hbm] * 2 + [vmem] * 5 + [hbm] * len(KEPT),
        scratch_shapes=scratch_shapes(),
        compiler_params=pltpu.CompilerParams(
            collective_id=0, has_side_effects=True, vmem_limit_bytes=64 * 1024 * 1024
        ),
        name="layers",
    )(
        lengths,
        inputs,
        cotangent,
        qkv_weight,
        dense_weight,
        fc_in_weight,
        fc_out_weight,
        norm1_gain,
        norm1_bias,
        norm2_gain,
        norm2_bias,
        out_bias,
        qkv_bias,
        fc_in_bias,
    )
    vector, slab = shape((1, 32), F32), shape((1, 2, T, D), BF)
    return pl.pallas_call(
        hand_out,
        out_shape=[slab, slab, vector, vector, shape((1, 32, 1536), F32), shape((1, 96), F32)]
        + [shape((1, 32, 512), F32), vector, vector, shape((1, 32, 2048), F32), shape((1, 128), F32)]
        + [shape((1, 128, 512), F32), vector],
        in_specs=[hbm] * 7,
        out_specs=[hbm] * 2 + [vmem] * 11,
        scratch_shapes=[pltpu.VMEM((4, T, D), BF)]
        + [pltpu.VMEM(r.shape, r.dtype) for r in results[2:7]]
        + [pltpu.SemaphoreType.DMA((9,)), pltpu.SemaphoreType.DMA((4,))],
        compiler_params=pltpu.CompilerParams(vmem_limit_bytes=60 * 1024 * 1024),
        name="hand_out",
    )(*results[:7])


def hand_out(
    act, ig, hq, hd, hi, ho, hv, o_act, o_ig, o_g1, o_b1, o_qkv, o_qkvb, o_d, o_g2, o_b2, o_in, o_inb, o_out, o_last, held, gq, gd, gi, go, gv, arrive, leave
):
    z = lax.axis_index("shard") % 4
    pieces = [(act.at[m], o_act.at[0, m]) for m in (0, 1)] + [(ig.at[m], o_ig.at[0, m]) for m in (0, 1)]
    coming = [pltpu.make_async_copy(src, held.at[k], arrive.at[k]) for k, (src, _) in enumerate(pieces)]
    going = [pltpu.make_async_copy(held.at[k], dst, leave.at[k]) for k, (_, dst) in enumerate(pieces)]
    small = [
        pltpu.make_async_copy(src, dst, arrive.at[4 + k])
        for k, (src, dst) in enumerate(((hq, gq), (hd, gd), (hi, gi), (ho, go), (hv, gv)))
    ]
    for copy in coming + small:
        copy.start()
    for copy, after in zip(coming, going):
        copy.wait()
        after.start()
    for copy in small:
        copy.wait()
    for half in (0, 1):
        rows = slice(16 * half, 16 * half + 16)
        for hp in range(PAIRS):
            for which in range(3):
                column = 512 * which + 128 * hp
                o_qkv[0, rows, column : column + 128] = gq[hp, half, :, 128 * which : 128 * which + 128]
        o_d[0, rows, :] = gd[half]
        o_in[0, rows, :] = gi[half]
        o_out[0, 64 * half : 64 * half + 64, :] = go[half]

    def own(row, width):
        total = jnp.zeros((1, width), F32)
        for k in range(4):
            total = total + jnp.where(z == k, row[:, width * k : width * k + width], 0.0)
        return total

    for row, ref in enumerate((o_g1, o_b1, o_g2, o_b2, o_last)):
        ref[...] = own(gv[row : row + 1, :], 32)
    o_qkvb[...] = own(jnp.concatenate([gv[8 + k : 9 + k, :] for k in range(3)], axis=1), 96)
    o_inb[...] = gv[11:12, :]
    for copy in going:
        copy.wait()


def solution(mesh):
    rows = P(None, ("replica", "shard"), None)
    vector, matrix = P("section", "shard"), P("section", "shard", None)
    slabs = P("section", None, ("replica", "shard"), None)
    return jax.shard_map(
        body,
        mesh=mesh,
        in_specs=(
            rows, rows, rows, vector, vector, matrix, vector, matrix, vector, vector, matrix, vector, matrix, vector,
        ),
        out_specs=(
            slabs, slabs, vector, vector, matrix, vector, matrix, vector, vector, matrix, vector, matrix, vector,
        ),
        check_vma=False,
    )
```
